32 devices in a mesh: row: 16 (over z, y, core), col: 2 (over x).
Axes of the slice: x: 2, y: 2, z: 4, core: 2. Of those that a mesh axis runs over, the one named last changes fastest.
Arguments:
- tokens: bfloat16 [2048, 2048], P('row'), may hold values from -6 to 6
- w_query: bfloat16 [2048, 1280], P('row', 'col'), may hold values from -0.125 to 0.125
- key_value_weight: bfloat16 [2048, 640], P('row'), may hold values from -0.125 to 0.125
- w_out: bfloat16 [1280, 2048], P('col', 'row'), may hold values from -1.25 to 1.25
- w_gate: bfloat16 [2048, 5120], P('row', 'col'), may hold values from -0.125 to 0.125
- w_up: bfloat16 [2048, 5120], P('row', 'col'), may hold values from -0.125 to 0.125
- w_down: bfloat16 [5120, 2048], P('col', 'row'), may hold values from -0.078125 to 0.078125
- attn_gain: float32 [2048], replicated, may hold values from 0.5 to 1.5
- ffn_gain: float32 [2048], replicated, may hold values from 0.5 to 1.5
- query_gain: float32 [64], replicated, may hold values from 0.25 to 1.75
- key_gain: float32 [64], replicated, may hold values from 0.25 to 1.75
- segments: int32 [2048], replicated, may hold values from -1 to 2047, as said below
- positions: int32 [2048], P('row'), may hold values from 0 to 2047, as said below
- out_grad: bfloat16 [2048, 2048], P('row'), may hold values from -6 to 6
Outputs:
- output: bfloat16 [2048, 2048], P('row')
- input_grad: float32 [2048, 2048], P('row')
- grad_query: float32 [2048, 1280], P('row', 'col')
- grad_keyval: float32 [2048, 640], P('row')
- grad_out: float32 [1280, 2048], P('col', 'row')
- grad_gate: float32 [2048, 5120], P('row', 'col')
- grad_up: float32 [2048, 5120], P('row', 'col')
- grad_down: float32 [5120, 2048], P('col', 'row')
- grad_attn_gain: float32 [2048], P('row')
- grad_ffn_gain: float32 [2048], P('row')
- grad_query_gain: float32 [64], P('row')
- grad_key_gain: float32 [64], P('row')
The draws below stay inside these ranges and needn't reach their ends.
Inputs may be any that keep to these rules, and one draw needn't show every extreme that they name: `segments`: the tokens form 2048 // 2048 sequences of 2048 tokens in order, and documents never cross them. Among live tokens the numbers never fall and rise by at most one from token to token; the last document is numbered 2048 - 1. Each sequence ends in padding (-1) of at least one token and fewer than 32, and holds one document of 1152 to 1536 tokens. Within a document positions rise by one from token to token; padding has position 0.
All inputs are finite; a program needn't handle non-finite values.
Results may differ from the reference program's by a relative error of at most 0.017.
Values may be sent and summed in bfloat16 or wider, within the bound.
No kernel may reach another device: no remote copies, remote signals or barrier semaphores. Data moves between devices by JAX's collectives and lax.ppermute only.
A program may use at most 192 MiB of HBM per device.

```python
import math
import jax
import jax.numpy as jnp
from jax import lax

MODEL_WIDTH = 2048
QUERY_HEADS = 20
KEY_VALUE_HEADS = 5
HEAD_SIZE = 64
FF = 5120
TOK_DEV = 128
PACKED_TOKENS = 2048
SEQ = 2048


def layout(key):
    token_index = jnp.arange(PACKED_TOKENS, dtype=jnp.int32)
    local = token_index % SEQ
    seq_number = token_index // SEQ
    seq_count = PACKED_TOKENS // SEQ
    pad_counts = jax.random.randint(jax.random.fold_in(key, 13), (seq_count,), 1, max(TOK_DEV // 4, 2))
    long_lengths = jax.random.randint(jax.random.fold_in(key, 11), (seq_count,), SEQ // 2 + TOK_DEV, 3 * SEQ // 4 + 1)
    long_starts = jax.random.randint(jax.random.fold_in(key, 12), (seq_count,), 0, SEQ - TOK_DEV // 4 - long_lengths + 1)
    level = jax.random.randint(jax.random.fold_in(key, 14), (PACKED_TOKENS // 32,), 2, 9)
    levels = jnp.repeat(level, 32)
    random_marks = jax.random.randint(jax.random.fold_in(key, 15), (PACKED_TOKENS,), 0, jnp.left_shift(jnp.ones_like(levels), levels)) == 0
    pad_row = jnp.take(pad_counts, seq_number)
    long_first = jnp.take(long_starts, seq_number)
    long_length = jnp.take(long_lengths, seq_number).astype(jnp.int32)
    long_last = long_first + long_length - 1
    is_live = local < SEQ - pad_row
    inside_long = (local > long_first) & (local <= long_last)
    starts_at = (random_marks | (local == 0) | (local == long_first) | (local == long_last + 1)) & jnp.logical_not(inside_long) & is_live
    counted = jnp.cumsum(starts_at.astype(jnp.int32)).astype(jnp.int32) - 1
    last_live = jnp.max(counted)
    segment = jnp.where(is_live, counted + (PACKED_TOKENS - 1 - last_live), -1).astype(jnp.int32)
    begins = lax.cummax(jnp.where(starts_at, token_index, 0).astype(jnp.int32), axis=0)
    offset_in = (token_index - begins).astype(jnp.int32)
    in_long = (local >= long_first) & (local <= long_last)
    return (segment, counted, offset_in, is_live, in_long, long_length)


def draw_segments(key, part):
    segment, counted, offset_in, is_live, in_long, long_length = layout(key)
    return segment


def draw_positions(key, part):
    segment, counted, offset_in, is_live, in_long, long_length = layout(key)
    key = jax.random.fold_in(key, 5)
    shifts = jax.random.randint(key, (PACKED_TOKENS,), 0, PACKED_TOKENS - SEQ + 1).astype(jnp.int32)
    other = offset_in + jnp.take(shifts, jnp.maximum(counted, 0))
    longer = offset_in + (PACKED_TOKENS - long_length)
    chosen = jnp.where(in_long, longer, other)
    return jnp.where(is_live, chosen, 0).astype(jnp.int32)


def steps_of(own_key, extent, split, least, largest):
    factor_of = 1.0
    for position, parts in split:
        steps = jax.random.uniform(jax.random.fold_in(jax.random.fold_in(own_key, 6), position), (parts,), jnp.float32, least / len(split), largest / len(split))
        factor_of = factor_of * jnp.repeat(jnp.exp(steps), extent[position] // parts).reshape((-1,) + (1,) * (len(extent) - 1 - position))
    return factor_of


def noise(key, dims, spread, limit, cuts=(), kind=jnp.bfloat16):
    values = jax.random.normal(key, dims, jnp.float32) * spread
    if len(cuts) > 0:
        values = steps_of(key, dims, cuts, -0.22, 0.18) * values
    return jnp.clip(values, min=-limit, max=limit).astype(kind)


def setup_inputs(seed: int = 0) -> dict:
    splits = jax.random.split(jax.random.key(seed), 15)
    return {
        "tokens": noise(splits[0], (PACKED_TOKENS, MODEL_WIDTH), 1.0, 6.0, ((0, 16),)),
        "w_query": noise(splits[1], (MODEL_WIDTH, QUERY_HEADS * HEAD_SIZE), MODEL_WIDTH ** -0.5, 0.125, ((0, 16), (1, 2))),
        "key_value_weight": noise(splits[2], (MODEL_WIDTH, 2 * KEY_VALUE_HEADS * HEAD_SIZE), MODEL_WIDTH ** -0.5, 0.125, ((0, 16),)),
        "w_out": noise(splits[3], (QUERY_HEADS * HEAD_SIZE, MODEL_WIDTH), (QUERY_HEADS * HEAD_SIZE // 64) ** -0.5, 1.25, ((0, 2), (1, 16))),
        "w_gate": noise(splits[4], (MODEL_WIDTH, FF), MODEL_WIDTH ** -0.5, 0.125, ((0, 16), (1, 2))),
        "w_up": noise(splits[5], (MODEL_WIDTH, FF), MODEL_WIDTH ** -0.5, 0.125, ((0, 16), (1, 2))),
        "w_down": noise(splits[6], (FF, MODEL_WIDTH), FF ** -0.5, 0.078125, ((0, 2), (1, 16))),
        "attn_gain": jnp.clip(1.0 + 0.1 * jax.random.normal(splits[7], (MODEL_WIDTH,), jnp.float32), 0.5, 1.5),
        "ffn_gain": jnp.clip(1.0 + 0.1 * jax.random.normal(splits[8], (MODEL_WIDTH,), jnp.float32), 0.5, 1.5),
        "query_gain": jnp.clip(1.0 + 0.15 * jax.random.normal(splits[9], (HEAD_SIZE,), jnp.float32), 0.25, 1.75),
        "key_gain": jnp.clip(1.0 + 0.15 * jax.random.normal(splits[10], (HEAD_SIZE,), jnp.float32), 0.25, 1.75),
        "segments": draw_segments(jax.random.fold_in(splits[14], 71), 0),
        "positions": draw_positions(jax.random.fold_in(splits[14], 71), 0),
        "out_grad": noise(splits[13], (PACKED_TOKENS, MODEL_WIDTH), 1.0, 6.0, ((0, 16),)),
    }


EPSILON = 1e-06
SCALE = 0.125
NEGATIVE = -1e+30
HIGH = lax.Precision.HIGHEST

@jax.custom_vjp
def reduced_precision(v):
    return lax.optimization_barrier(v.astype(jnp.bfloat16)).astype(jnp.float32)

@jax.custom_vjp
def low_back(v):
    return v

def low_keep(v):
    return (reduced_precision(v), None)

def low_pass(kept, grad):
    return (grad,)

def back_keep(v):
    return (v, None)

def back_low(kept, grad):
    return (reduced_precision(grad),)
reduced_precision.defvjp(low_keep, low_pass)
low_back.defvjp(back_keep, back_low)

def tables(positions, head_dim):
    halves = head_dim // 2
    inverse = jnp.exp(jnp.arange(halves, dtype=jnp.float32) * (-2.0 * math.log(10000.0) / head_dim))
    angles = positions.astype(jnp.float32)[:, None] * inverse[None, :]
    return (jnp.cos(angles)[:, None, :], jnp.sin(angles)[:, None, :])

def apply_rotation(vectors, cosine_table, sine_table):
    halves = vectors.shape[-1] // 2
    first_half = vectors[..., :halves]
    second_half = vectors[..., halves:]
    return jnp.concatenate([first_half * cosine_table - second_half * sine_table, second_half * cosine_table + first_half * sine_table], axis=-1)

def root_mean_square_norm(vectors, gains):
    return vectors * lax.rsqrt(lax.optimization_barrier(jnp.mean(vectors * vectors, axis=-1, keepdims=True)) + EPSILON) * gains

def allowed(seg_query, idx_query, seg_key, idx_key):
    same_doc = (seg_query[:, None] == seg_key[None, :]) & (idx_key[None, :] <= idx_query[:, None]) & (seg_key[None, :] >= 0)
    return same_doc | (idx_key[None, :] == idx_query[:, None])

def matmul(left, right):
    return jnp.dot(left, right, precision=HIGH)

def reference(tokens, w_query, key_value_weight, w_out, w_gate, w_up, w_down, attn_gain, ffn_gain, query_gain, key_gain, segments, positions, out_grad):
    query_group_size = QUERY_HEADS // KEY_VALUE_HEADS
    block_rows = 256 if SEQ % 256 == 0 else SEQ
    cosine_table, sine_table = tables(positions, HEAD_SIZE)

    def forward(input_f, wq_f, wkv_f, wo_f, wg_f, wu_f, wd_f, gain_attn, gain_ffn, gain_query, key_norm_gain):
        act = reduced_precision(root_mean_square_norm(input_f, gain_attn))
        q_raw = low_back(matmul(act, wq_f))
        key_value_projected = low_back(matmul(act, wkv_f))
        query = reduced_precision(apply_rotation(root_mean_square_norm(q_raw.reshape(PACKED_TOKENS, QUERY_HEADS, HEAD_SIZE), gain_query), cosine_table, sine_table))
        key_heads = reduced_precision(apply_rotation(root_mean_square_norm(key_value_projected[:, :KEY_VALUE_HEADS * HEAD_SIZE].reshape(PACKED_TOKENS, KEY_VALUE_HEADS, HEAD_SIZE), key_norm_gain), cosine_table, sine_table))
        value_heads = reduced_precision(key_value_projected[:, KEY_VALUE_HEADS * HEAD_SIZE:].reshape(PACKED_TOKENS, KEY_VALUE_HEADS, HEAD_SIZE))
        key_heads = jnp.repeat(key_heads, query_group_size, axis=1)
        value_heads = jnp.repeat(value_heads, query_group_size, axis=1)

        def attend(first_row):
            seq_first = (first_row // SEQ * SEQ).astype(jnp.int32)
            keys_seq = lax.dynamic_slice_in_dim(key_heads, seq_first, SEQ, 0)
            values_seq = lax.dynamic_slice_in_dim(value_heads, seq_first, SEQ, 0)
            query_blk = lax.dynamic_slice_in_dim(query, first_row, block_rows, 0)
            logits = low_back(jnp.einsum('qhd,khd->hqk', query_blk, keys_seq, precision=HIGH) * SCALE)
            seg_query = lax.dynamic_slice_in_dim(segments, first_row, block_rows, 0)
            idx_query = first_row + jnp.arange(block_rows, dtype=jnp.int32)
            seg_key = lax.dynamic_slice_in_dim(segments, seq_first, SEQ, 0)
            idx_key = seq_first + jnp.arange(SEQ, dtype=jnp.int32)
            mask_ok = allowed(seg_query, idx_query, seg_key, idx_key)
            logits = jnp.where(mask_ok[None], logits, NEGATIVE)
            row_max = lax.optimization_barrier(jnp.max(logits, axis=2, keepdims=True))
            expo = jnp.where(mask_ok[None], jnp.exp(logits - row_max), 0.0)
            prob = reduced_precision(expo / lax.optimization_barrier(jnp.sum(expo, axis=2, keepdims=True)))
            return jnp.einsum('hqk,khd->qhd', prob, values_seq, precision=HIGH)
        starts = jnp.arange(PACKED_TOKENS // block_rows, dtype=jnp.int32) * block_rows
        attended = lax.map(jax.checkpoint(attend), starts)
        attended = reduced_precision(low_back(attended.reshape(PACKED_TOKENS, QUERY_HEADS * HEAD_SIZE)))
        residual = input_f + low_back(matmul(attended, wo_f))
        ffn_act = reduced_precision(root_mean_square_norm(residual, gain_ffn))
        gate_pre = low_back(matmul(ffn_act, wg_f))
        up_pre = low_back(matmul(ffn_act, wu_f))
        inner_act = reduced_precision(jax.nn.silu(gate_pre) * up_pre)
        return residual + low_back(matmul(inner_act, wd_f))
    inputs = (tokens.astype(jnp.float32), w_query.astype(jnp.float32), key_value_weight.astype(jnp.float32), w_out.astype(jnp.float32), w_gate.astype(jnp.float32), w_up.astype(jnp.float32), w_down.astype(jnp.float32), attn_gain.astype(jnp.float32), ffn_gain.astype(jnp.float32), query_gain.astype(jnp.float32), key_gain.astype(jnp.float32))
    result, pullback = jax.vjp(forward, *inputs)
    gradients = pullback(out_grad.astype(jnp.float32))
    return (result.astype(jnp.bfloat16), gradients[0], gradients[1], gradients[2], gradients[3], gradients[4], gradients[5], gradients[6], gradients[7], gradients[8], gradients[9], gradients[10])
```

```python
import math

import jax
import jax.numpy as jnp
from jax import lax
from jax.experimental import pallas as pl
from jax.experimental.pallas import tpu as pltpu
from jax.sharding import PartitionSpec as P

EPSILON = 1e-06
SCALE = 0.125
SEQ_MAX = 4096
MEMBERS = 8
LANES = 128
HALF = 64
F32 = jnp.float32
BF16 = jnp.bfloat16
VMEM_LIMIT = 56 * 1024 * 1024


def dot(a, b, dims=((1,), (0,))):
    return lax.dot_general(a, b, (dims, ((), ())), preferred_element_type=F32)


def swap_core(block):
    rows = lax.axis_size("row")
    return lax.ppermute(block, "row", [(i, i ^ 1) for i in range(rows)])


def swap_col(block):
    return lax.ppermute(block, "col", [(0, 1), (1, 0)])


def plane_groups(span):
    rows = lax.axis_size("row")
    return [
        [first + 2 * j + core for j in range(span // 2)]
        for first in range(0, rows, span)
        for core in range(2)
    ]


def cube_groups():
    rows, cols = lax.axis_size("row"), lax.axis_size("col")
    return [
        [(first + 2 * j + core) * cols + c for j in range(MEMBERS // 2) for c in range(cols)]
        for first in range(0, rows, MEMBERS)
        for core in range(2)
    ]


def exchange_plane(blocks, span):
    return lax.all_to_all(
        blocks, "row", split_axis=0, concat_axis=0, tiled=True, axis_index_groups=plane_groups(span)
    )


def exchange_cube(blocks):
    return lax.all_to_all(
        blocks, ("row", "col"), split_axis=0, concat_axis=0, tiled=True, axis_index_groups=cube_groups()
    )


def gather_plane(block, span):
    copies = jnp.broadcast_to(block[None], (span // 2,) + block.shape)
    same = exchange_plane(copies, span)
    return same, swap_core(same)


def gather_cube(block):
    count = MEMBERS // 2 * lax.axis_size("col")
    copies = jnp.broadcast_to(block[None], (count,) + block.shape)
    same = exchange_cube(copies)
    return same, swap_core(same)


def halves(own, other, col):
    low = jnp.where(col == 0, own, other)
    high = jnp.where(col == 0, other, own)
    return jnp.concatenate([low, high], axis=0)


def partner(v):
    lane = lax.broadcasted_iota(jnp.int32, v.shape, 1)
    ahead = pltpu.roll(v, LANES - HALF // 2, 1)
    behind = pltpu.roll(v, HALF // 2, 1)
    return jnp.where(lane % HALF < HALF // 2, ahead, behind)


def head_mean(v):
    lane = lax.broadcasted_iota(jnp.int32, v.shape, 1)
    first = jnp.sum(jnp.where(lane < HALF, v, 0.0), axis=1, keepdims=True)
    second = jnp.sum(jnp.where(lane < HALF, 0.0, v), axis=1, keepdims=True)
    return jnp.where(lane < HALF, first, second) * (1.0 / HALF)


def head_forward(raw, gain, flag, cosine, sine):
    scaler = jnp.where(flag > 0, lax.rsqrt(head_mean(raw * raw) + EPSILON), 1.0)
    normed = raw * scaler * gain
    cosine = jnp.where(flag > 0, cosine, 1.0)
    sine = jnp.where(flag > 0, sine, 0.0)
    return normed * cosine + partner(normed) * sine


def head_backward(grad, raw, gain, flag, cosine, sine):
    on = flag > 0
    scaler = lax.rsqrt(head_mean(raw * raw) + EPSILON)
    back = grad * cosine - partner(grad) * sine
    scaled = back * gain
    inner = head_mean(scaled * raw)
    grad_raw = scaler * scaled - raw * (scaler * scaler * scaler) * inner
    gain_term = jnp.sum(jnp.where(on, back * raw * scaler, 0.0), axis=0, keepdims=True)
    return jnp.where(on, grad_raw, grad), gain_term


def qkv_kernel(act_ref, w_ref, gain_ref, flag_ref, cos_ref, sin_ref, raw_ref, out_ref):
    raw = dot(act_ref[...], w_ref[...])
    raw_ref[...] = raw
    for part in range(raw.shape[1] // LANES):
        at = slice(part * LANES, (part + 1) * LANES)
        done = head_forward(raw[:, at], gain_ref[:, at], flag_ref[:, at], cos_ref[...], sin_ref[...])
        out_ref[:, at] = done.astype(BF16)


def qkv_call(act, w_all, gain, flag, cosine, sine):
    tok, width = act.shape
    cols = w_all.shape[1]
    block = 256
    whole = lambda shape: pl.BlockSpec(shape, lambda i: (0, 0))
    chunk = lambda rows: pl.BlockSpec((rows, block), lambda i: (0, i))
    return pl.pallas_call(
        qkv_kernel,
        grid=(cols // block,),
        in_specs=[whole((tok, width)), chunk(width), chunk(1), chunk(1), whole((tok, LANES)), whole((tok, LANES))],
        out_specs=[chunk(tok), chunk(tok)],
        out_shape=[jax.ShapeDtypeStruct((tok, cols), F32), jax.ShapeDtypeStruct((tok, cols), BF16)],
        compiler_params=pltpu.CompilerParams(vmem_limit_bytes=VMEM_LIMIT),
        cost_estimate=pl.CostEstimate(flops=2 * tok * width * cols, bytes_accessed=2 * width * cols, transcendentals=0),
        name="qkv_heads",
    )(act, w_all, gain, flag, cosine, sine)


GROUPS = ((0, 4), (4, 4), (8, 2))
K_AT = (0, 64, 128)
V_AT = (256, 320, 192)


def stack_heads(wide, tok):
    turned, tall = [], []
    for pair in range(wide.shape[1] // LANES):
        chunk = wide[:, pair * LANES : (pair + 1) * LANES]
        flat = chunk.astype(F32).T.astype(BF16)
        turned += [flat[:HALF], flat[HALF:]]
        tall += [chunk[:, :HALF], chunk[:, HALF:]]
    return jnp.concatenate(turned, axis=1), jnp.concatenate(tall, axis=0)


def key_mask(base_same, base_other, limits_ref, tok):
    key = lax.broadcasted_iota(jnp.int32, (2 * tok, tok), 0)
    key = key + jnp.where(key < tok, base_same, base_other - tok)
    return (key >= limits_ref[0:1, :]) & (key <= limits_ref[1:2, :])


def forward_kernel(bounds_ref, limits_ref, q_ref, same_ref, other_ref, att_ref, turned_ref, inv_ref, q_turned):
    tok = q_ref.shape[0]
    turned, tall = stack_heads(q_ref[...], tok)
    q_turned[...] = turned
    turned_ref[...] = jnp.zeros_like(turned_ref)
    inv_ref[...] = jnp.zeros_like(inv_ref)
    core = bounds_ref[2]

    @pl.loop(bounds_ref[0], bounds_ref[1])
    def step(j):
        kv = jnp.concatenate([same_ref[j], other_ref[j]], axis=0)
        ok = key_mask((2 * j + core) * tok, (2 * j + 1 - core) * tok, limits_ref, tok)
        for g, (first, count) in enumerate(GROUPS):
            at = slice(first * tok, (first + count) * tok)
            keys = kv[:, K_AT[g] : K_AT[g] + HALF]
            vals = kv[:, V_AT[g] : V_AT[g] + HALF]
            logit = dot(keys, q_turned[:, at])
            allowed = jnp.concatenate([ok] * count, axis=1)
            expo = jnp.where(allowed, jnp.exp(logit), 0.0)
            inv_ref[:, at] += jnp.sum(expo, axis=0, keepdims=True)
            turned_ref[:, at] += dot(vals, expo.astype(BF16), ((0,), (0,)))

    inverse = 1.0 / inv_ref[...]
    inv_ref[...] = inverse
    turned_ref[...] = turned_ref[...] * inverse
    for pair in range(att_ref.shape[1] // LANES):
        at = 2 * pair * tok
        both = jnp.concatenate([turned_ref[:, at : at + tok], turned_ref[:, at + tok : at + 2 * tok]], axis=0)
        att_ref[:, pair * LANES : (pair + 1) * LANES] = both.T.astype(BF16)


def vmem(n):
    return [pl.BlockSpec(memory_space=pltpu.VMEM)] * n


SMEM = pl.BlockSpec(memory_space=pltpu.SMEM)


def forward_call(bounds, limits, q, same, other):
    tok, width = q.shape
    wide = width // HALF * tok
    work = same.shape[0] * 2 * tok * wide
    return pl.pallas_call(
        forward_kernel,
        in_specs=[SMEM] + vmem(4),
        out_specs=vmem(3),
        out_shape=[
            jax.ShapeDtypeStruct((tok, width), BF16),
            jax.ShapeDtypeStruct((HALF, wide), F32),
            jax.ShapeDtypeStruct((1, wide), F32),
        ],
        scratch_shapes=[pltpu.VMEM((HALF, wide), BF16)],
        compiler_params=pltpu.CompilerParams(vmem_limit_bytes=VMEM_LIMIT),
        cost_estimate=pl.CostEstimate(flops=4 * HALF * work, bytes_accessed=4 * same.size, transcendentals=work),
        name="attention_forward",
    )(bounds, limits, q, same, other)


def backward_kernel(
    bounds_ref,
    limits_ref,
    q_ref,
    grad_ref,
    turned_ref,
    inv_ref,
    same_ref,
    other_ref,
    raw_ref,
    gain_ref,
    cos_ref,
    sin_ref,
    dq_ref,
    gain_grad_ref,
    same_out,
    other_out,
    q_turned,
    q_tall,
    g_turned,
    g_tall,
    dq_acc,
):
    tok = q_ref.shape[0]
    q_turned[...], q_tall[...] = stack_heads(q_ref[...], tok)
    g_turned[...], g_tall[...] = stack_heads(grad_ref[...], tok)
    dq_acc[...] = jnp.zeros_like(dq_acc)
    same_out[...] = jnp.zeros_like(same_out)
    other_out[...] = jnp.zeros_like(other_out)
    core = bounds_ref[2]
    delta = jnp.sum(g_turned[...].astype(F32) * turned_ref[...], axis=0, keepdims=True)

    @pl.loop(bounds_ref[0], bounds_ref[1])
    def step(j):
        kv = jnp.concatenate([same_ref[j], other_ref[j]], axis=0)
        ok = key_mask((2 * j + core) * tok, (2 * j + 1 - core) * tok, limits_ref, tok)
        for g, (first, count) in enumerate(GROUPS):
            at = slice(first * tok, (first + count) * tok)
            keys = kv[:, K_AT[g] : K_AT[g] + HALF]
            vals = kv[:, V_AT[g] : V_AT[g] + HALF]
            allowed = jnp.concatenate([ok] * count, axis=1)
            prob = jnp.where(allowed, jnp.exp(dot(keys, q_turned[:, at])) * inv_ref[:, at], 0.0)
            d_score = (prob * (dot(vals, g_turned[:, at]) - delta[:, at])).astype(BF16)
            d_keys = dot(d_score, q_tall[at, :]).astype(BF16)
            d_vals = dot(prob.astype(BF16), g_tall[at, :]).astype(BF16)
            dq_acc[:, at] += dot(keys, d_score, ((0,), (0,)))
            same_out[j, :, K_AT[g] : K_AT[g] + HALF] = d_keys[:tok]
            other_out[j, :, K_AT[g] : K_AT[g] + HALF] = d_keys[tok:]
            same_out[j, :, V_AT[g] : V_AT[g] + HALF] = d_vals[:tok]
            other_out[j, :, V_AT[g] : V_AT[g] + HALF] = d_vals[tok:]

    total = jnp.zeros((1, LANES), F32)
    for pair in range(dq_ref.shape[1] // LANES):
        at = 2 * pair * tok
        both = jnp.concatenate([dq_acc[:, at : at + tok], dq_acc[:, at + tok : at + 2 * tok]], axis=0)
        cols = slice(pair * LANES, (pair + 1) * LANES)
        d_raw, term = head_backward(
            both.T * SCALE, raw_ref[:, cols], gain_ref[...], jnp.ones((1, LANES), F32), cos_ref[...], sin_ref[...]
        )
        dq_ref[:, cols] = d_raw.astype(BF16)
        total += term
    gain_grad_ref[...] = total


def backward_call(bounds, limits, q, grad, turned, inv, same, other, raw, gain, cosine, sine):
    tok, width = q.shape
    wide = width // HALF * tok
    work = same.shape[0] * 2 * tok * wide
    return pl.pallas_call(
        backward_kernel,
        in_specs=[SMEM] + vmem(11),
        out_specs=vmem(4),
        out_shape=[
            jax.ShapeDtypeStruct((tok, width), BF16),
            jax.ShapeDtypeStruct((1, LANES), F32),
            jax.ShapeDtypeStruct(same.shape, BF16),
            jax.ShapeDtypeStruct(other.shape, BF16),
        ],
        scratch_shapes=[
            pltpu.VMEM((HALF, wide), BF16),
            pltpu.VMEM((wide, HALF), BF16),
            pltpu.VMEM((HALF, wide), BF16),
            pltpu.VMEM((wide, HALF), BF16),
            pltpu.VMEM((HALF, wide), F32),
        ],
        compiler_params=pltpu.CompilerParams(vmem_limit_bytes=VMEM_LIMIT),
        cost_estimate=pl.CostEstimate(flops=10 * HALF * work, bytes_accessed=8 * same.size, transcendentals=work),
        name="attention_backward",
    )(bounds, limits, q, grad, turned, inv, same, other, raw, gain, cosine, sine)


def kv_back_kernel(parts_ref, raw_ref, gain_ref, flag_ref, cos_ref, sin_ref, out_ref, gain_grad_ref):
    total = jnp.zeros((1, LANES), F32)
    for part in range(out_ref.shape[1] // LANES):
        at = slice(part * LANES, (part + 1) * LANES)
        grad = jnp.sum(parts_ref[:, :, at].astype(F32), axis=0)
        done, term = head_backward(
            grad, raw_ref[:, at], gain_ref[:, at], flag_ref[:, at], cos_ref[...], sin_ref[...]
        )
        out_ref[:, at] = done.astype(BF16)
        total += term
    gain_grad_ref[...] = total


def kv_back_call(parts, raw, gain, flag, cosine, sine):
    tok, width = raw.shape
    return pl.pallas_call(
        kv_back_kernel,
        in_specs=vmem(6),
        out_specs=vmem(2),
        out_shape=[jax.ShapeDtypeStruct((tok, width), BF16), jax.ShapeDtypeStruct((1, LANES), F32)],
        compiler_params=pltpu.CompilerParams(vmem_limit_bytes=VMEM_LIMIT),
        cost_estimate=pl.CostEstimate(flops=30 * tok * width, bytes_accessed=2 * parts.size, transcendentals=0),
        name="key_value_heads_back",
    )(parts, raw, gain, flag, cosine, sine)


def rope_tables(positions, head_dim):
    half = head_dim // 2
    inverse = jnp.exp(jnp.arange(half, dtype=F32) * (-2.0 * math.log(10000.0) / head_dim))
    angles = positions.astype(F32)[:, None] * inverse[None, :]
    cosine, sine = jnp.cos(angles), jnp.sin(angles)
    return jnp.concatenate([cosine] * 4, axis=1), jnp.concatenate([-sine, sine, -sine, sine], axis=1)


def norm_scale(vectors):
    return lax.rsqrt(jnp.mean(vectors * vectors, axis=-1, keepdims=True) + EPSILON)


def norm_back(vectors, scaler, gains, grads_in):
    scaled = grads_in * gains
    inner_mean = jnp.mean(scaled * vectors, axis=-1, keepdims=True)
    return scaler * scaled - vectors * (scaler * scaler * scaler) * inner_mean


def backwards(array, axis, width):
    count = array.shape[axis] // width
    pieces = [lax.slice_in_dim(array, i * width, (i + 1) * width, axis=axis) for i in range(count)]
    return jnp.concatenate(pieces[::-1], axis=axis)


def body(
    tokens,
    w_query,
    key_value_weight,
    w_out,
    w_gate,
    w_up,
    w_down,
    attn_gain,
    ffn_gain,
    query_gain,
    key_gain,
    segments,
    positions,
    out_grad,
):
    tok, width = tokens.shape
    rows = lax.axis_size("row")
    row = lax.axis_index("row")
    col = lax.axis_index("col")
    core = row % 2
    w_rows = w_query.shape[0]
    q_width = w_query.shape[1]
    kv_half = key_value_weight.shape[1] // 2
    ff_cols = w_gate.shape[1]
    ff = ff_cols // MEMBERS
    seq_len = min(SEQ_MAX, tok * rows)
    span = seq_len // tok
    half = tok // 2

    def kv_pick(order):
        k = [key_value_weight[:, h * HALF : (h + 1) * HALF] for h in order]
        v = [key_value_weight[:, kv_half + h * HALF : kv_half + (h + 1) * HALF] for h in order]
        return jnp.concatenate([k[0], k[1], k[2], v[2], v[0], v[1]], axis=1)

    w_one = jnp.where(
        col == 0,
        jnp.concatenate([w_query, kv_pick((0, 1, 2))], axis=1),
        jnp.concatenate([backwards(w_query, 1, LANES), kv_pick((4, 3, 2))], axis=1),
    )
    w_one_all = lax.all_gather(w_one, "row", axis=0, tiled=True)
    w_o = jnp.where(col == 0, w_out, backwards(w_out, 0, LANES))
    w_o_all = lax.all_gather(w_o, "row", axis=1, tiled=True)

    w_ff = jnp.concatenate(
        [
            w_gate.reshape(w_rows, MEMBERS, ff),
            w_up.reshape(w_rows, MEMBERS, ff),
            w_down.T.reshape(w_rows, MEMBERS, ff),
        ],
        axis=2,
    ).transpose(1, 0, 2)
    w_ff_all = lax.all_to_all(
        jnp.concatenate([w_ff] * (rows // MEMBERS), axis=0), "row", split_axis=0, concat_axis=0, tiled=True
    ).reshape(width, 3 * ff)

    input_f = tokens.astype(F32)
    act_scale = norm_scale(input_f)
    act_low = (input_f * act_scale * attn_gain).astype(BF16)
    cosine, sine = rope_tables(positions, HALF)
    q_lanes = jnp.tile(query_gain, 2)[None, :]
    k_lanes = jnp.tile(key_gain, 2)[None, :]
    kv_flag = jnp.concatenate([jnp.ones((1, 3 * HALF), F32), jnp.zeros((1, 3 * HALF), F32)], axis=1)
    kv_gain = jnp.where(kv_flag > 0, jnp.tile(k_lanes, (1, 3)), 1.0)
    flag = jnp.concatenate([jnp.ones((1, q_width), F32), kv_flag], axis=1)
    gain = jnp.concatenate([jnp.tile(q_lanes * SCALE, (1, q_width // LANES)), kv_gain], axis=1)
    raw, heads = qkv_call(act_low, w_one_all, gain, flag, cosine, sine)
    query, kv_low = heads[:, :q_width], heads[:, q_width:]
    same_kv, other_kv = gather_plane(kv_low, span)

    in_span = row % span
    seq_segments = lax.dynamic_slice_in_dim(segments, (row - in_span) * tok, seq_len, 0)
    own_segments = lax.dynamic_slice_in_dim(segments, row * tok, tok, 0)
    own_index = in_span * tok + jnp.arange(tok, dtype=jnp.int32)
    index = jnp.arange(seq_len, dtype=jnp.int32)
    start = jnp.min(jnp.where(seq_segments[None, :] == own_segments[:, None], index[None, :], seq_len), axis=1)
    start = jnp.where(own_segments < 0, own_index, start)
    limits = jnp.stack([start, own_index])
    bounds = jnp.stack([jnp.min(start) // (2 * tok), in_span // 2 + 1, core])
    attn_low, turned, inv = forward_call(bounds, limits, query, same_kv, other_kv)
    same_att, other_att = gather_plane(attn_low, rows)
    attn_part = dot(attn_low, w_o_all).astype(BF16)

    def mine(array, which):
        return lax.dynamic_slice_in_dim(array, which * half, half, 0)

    arrived = swap_col(mine(attn_part, 1 - col))
    hidden = mine(input_f, col) + (mine(attn_part, col).astype(F32) + arrived.astype(F32))

    ffn_scale = norm_scale(hidden)
    ffn_low = (hidden * ffn_scale * ffn_gain).astype(BF16)
    og_low = mine(out_grad, col)
    og_all = jnp.concatenate([a.reshape(-1, width) for a in gather_cube(og_low)], axis=0)
    ffn_all = jnp.concatenate([a.reshape(-1, width) for a in gather_cube(ffn_low)], axis=0)
    group = ffn_all.shape[0]
    gate_up = dot(ffn_all, w_ff_all[:, : 2 * ff])
    gate_pre, up_pre = gate_up[:, :ff], gate_up[:, ff:]
    d_inner = dot(og_all, w_ff_all[:, 2 * ff :])
    sigma = jax.nn.sigmoid(gate_pre)
    silu_gate = gate_pre * sigma
    inner_low = (silu_gate * up_pre).astype(BF16)
    d_gate = d_inner * up_pre * (sigma * (1.0 + gate_pre * (1.0 - sigma)))
    d_up = d_inner * silu_gate
    d_gate_up = jnp.concatenate([d_gate, d_up], axis=1).astype(BF16)

    def reduce_cube(left, right):
        count = group // 2 // half
        away = dot(left[group // 2 :], right, ((1,), (1,))).astype(BF16)
        here = dot(left[: group // 2], right, ((1,), (1,)))
        total = (here + swap_core(away).astype(F32)).astype(BF16)
        parts = exchange_cube(total.reshape(count, half, width))
        return jnp.sum(parts.astype(F32), axis=0)

    ffn_back = reduce_cube(d_gate_up, w_ff_all[:, : 2 * ff])
    grads_ff = jnp.concatenate(
        [dot(ffn_all, d_gate_up, ((0,), (0,))), dot(og_all, inner_low, ((0,), (0,)))], axis=1
    ).astype(BF16)
    grads_ff = lax.all_to_all(
        grads_ff.reshape(rows, w_rows, 3 * ff), "row", split_axis=0, concat_axis=0, tiled=True
    )
    ffn_out = reduce_cube(inner_low, w_ff_all[:, 2 * ff :])
    out_half = (hidden + ffn_out).astype(BF16)
    output = halves(out_half, swap_col(out_half), col)

    d_hidden = og_low.astype(F32) + norm_back(hidden, ffn_scale, ffn_gain, ffn_back)
    d_hidden_half = d_hidden.astype(BF16)
    d_hidden_low = halves(d_hidden_half, swap_col(d_hidden_half), col)

    d_attn = dot(d_hidden_low, w_o_all, ((1,), (1,))).astype(BF16)
    d_q, q_gain_part, same_d, other_d = backward_call(
        bounds, limits, query, d_attn, turned, inv, same_kv, other_kv, raw[:, :q_width], q_lanes, cosine, sine
    )
    same_dq, other_dq = gather_plane(d_q, rows)
    kv_parts = exchange_plane((same_d.astype(F32) + swap_core(other_d).astype(F32)).astype(BF16), span)
    d_kv, k_gain_part = kv_back_call(kv_parts, raw[:, q_width:], kv_gain, kv_flag, cosine, sine)
    same_dkv, other_dkv = gather_plane(d_kv, rows)

    d_one = jnp.concatenate([d_q, d_kv], axis=1)
    act_back = dot(d_one, w_one_all, ((1,), (1,))).astype(BF16)
    act_back = act_back.astype(F32) + swap_col(act_back).astype(F32)
    input_grad = d_hidden_low.astype(F32) + norm_back(input_f, act_scale, attn_gain, act_back)

    columns = jnp.concatenate([act_low.reshape(tok, rows, w_rows), d_hidden_low.reshape(tok, rows, w_rows)], axis=2)
    columns = lax.all_to_all(columns.transpose(1, 0, 2), "row", split_axis=0, concat_axis=0, tiled=True)
    columns = columns.reshape(rows // 2, 2, tok, 2 * w_rows)
    same_cols = lax.dynamic_index_in_dim(columns, core, 1, keepdims=False).reshape(-1, 2 * w_rows)
    other_cols = lax.dynamic_index_in_dim(columns, 1 - core, 1, keepdims=False).reshape(-1, 2 * w_rows)

    def over_tokens(left, right):
        return dot(left[0], right[0].reshape(left[0].shape[0], -1), ((0,), (0,))) + dot(
            left[1], right[1].reshape(left[1].shape[0], -1), ((0,), (0,))
        )

    act_cols = (same_cols[:, :w_rows], other_cols[:, :w_rows])
    hid_cols = (same_cols[:, w_rows:], other_cols[:, w_rows:])
    grad_q = over_tokens(act_cols, (same_dq, other_dq))
    grad_kv = over_tokens(act_cols, (same_dkv, other_dkv))
    grad_o = over_tokens(
        (same_att.reshape(-1, q_width), other_att.reshape(-1, q_width)), hid_cols
    )
    grad_query = jnp.where(col == 0, grad_q, backwards(grad_q, 1, LANES))
    grad_out = jnp.where(col == 0, grad_o, backwards(grad_o, 0, LANES))

    kv_own = grad_kv.astype(BF16)
    kv_away = swap_col(kv_own)
    kv_first = jnp.where(col == 0, kv_own, kv_away).astype(F32)
    kv_last = jnp.where(col == 0, kv_away, kv_own).astype(F32)

    def head_cols(array, at):
        return array[:, at : at + HALF]

    pieces = []
    for at in (K_AT, V_AT):
        pieces += [head_cols(kv_first, at[0]), head_cols(kv_first, at[1])]
        pieces += [head_cols(kv_first, at[2]) + head_cols(kv_last, at[2])]
        pieces += [head_cols(kv_last, at[1]), head_cols(kv_last, at[0])]
    grad_keyval = jnp.concatenate(pieces, axis=1)

    grads_ff = jnp.sum(grads_ff.reshape(rows // MEMBERS, MEMBERS, w_rows, 3 * ff).astype(F32), axis=0)
    grads_ff = grads_ff.transpose(1, 0, 2)
    grad_gate = grads_ff[:, :, :ff].reshape(w_rows, ff_cols)
    grad_up = grads_ff[:, :, ff : 2 * ff].reshape(w_rows, ff_cols)
    grad_down = grads_ff[:, :, 2 * ff :].reshape(w_rows, ff_cols).T

    attn_part_gain = jnp.sum(jnp.concatenate([grad_q, grad_kv], axis=1) * w_one.astype(F32), axis=1)
    ffn_part_gain = jnp.sum(grad_gate * w_gate.astype(F32) + grad_up * w_up.astype(F32), axis=1)
    per_row = HALF // rows
    small = jnp.concatenate(
        [
            (q_gain_part[0, :HALF] + q_gain_part[0, HALF:]).reshape(rows, per_row),
            (k_gain_part[0, :HALF] + k_gain_part[0, HALF:]).reshape(rows, per_row),
        ],
        axis=1,
    )
    small = jnp.sum(lax.all_to_all(small, "row", split_axis=0, concat_axis=0, tiled=True), axis=0)
    gains = jnp.concatenate([attn_part_gain, ffn_part_gain, small])
    gains = gains + swap_col(gains)
    own_gains = lambda whole: lax.dynamic_slice_in_dim(whole, row * w_rows, w_rows, 0)
    grad_attn_gain = gains[:w_rows] / own_gains(attn_gain)
    grad_ffn_gain = gains[w_rows : 2 * w_rows] / own_gains(ffn_gain)
    grad_query_gain = gains[2 * w_rows : 2 * w_rows + per_row]
    grad_key_gain = gains[2 * w_rows + per_row :]
    return (
        output,
        input_grad,
        grad_query,
        grad_keyval,
        grad_out,
        grad_gate,
        grad_up,
        grad_down,
        grad_attn_gain,
        grad_ffn_gain,
        grad_query_gain,
        grad_key_gain,
    )


def solution(mesh):
    placed = (
        P("row", None),
        P("row", "col"),
        P("row", None),
        P("col", "row"),
        P("row", "col"),
        P("row", "col"),
        P("col", "row"),
        P(),
        P(),
        P(),
        P(),
        P(),
        P("row"),
        P("row", None),
    )
    return jax.shard_map(
        body,
        mesh=mesh,
        in_specs=placed,
        out_specs=(
            P("row", None),
            P("row", None),
            P("row", "col"),
            P("row", None),
            P("col", "row"),
            P("row", "col"),
            P("row", "col"),
            P("col", "row"),
            P("row"),
            P("row"),
            P("row"),
            P("row"),
        ),
        check_vma=False,
    )
```

```python
import math

import jax
import jax.numpy as jnp
from jax import lax
from jax.experimental import pallas as pl
from jax.experimental.pallas import tpu as pltpu
from jax.sharding import PartitionSpec as P

EPSILON = 1e-06
SCALE = 0.125
SEQ_MAX = 4096
MEMBERS = 8
LANES = 128
HALF = 64
F32 = jnp.float32
BF16 = jnp.bfloat16
VMEM_LIMIT = 56 * 1024 * 1024


def dot(a, b, dims=((1,), (0,))):
    return lax.dot_general(a, b, (dims, ((), ())), preferred_element_type=F32)


def swap_core(block):
    rows = lax.axis_size("row")
    return lax.ppermute(block, "row", [(i, i ^ 1) for i in range(rows)])


def swap_col(block):
    return lax.ppermute(block, "col", [(0, 1), (1, 0)])


def shift_far(block, steps, span, wrap):
    rows = lax.axis_size("row")
    route = []
    for i in range(rows):
        first, at = i // span * span, i % span + 4 * steps
        if wrap or 0 <= at < span:
            route.append((i, first + at % span))
    return lax.ppermute(block, "row", route)


def swap_near(block):
    rows = lax.axis_size("row")
    return lax.ppermute(block, "row", [(i, i ^ 2) for i in range(rows)])


def swap_cube(block, number):
    rows, cols = lax.axis_size("row"), lax.axis_size("col")
    route = []
    for i in range(rows):
        first, chip, core = i // MEMBERS * MEMBERS, i % MEMBERS // 2, i % 2
        there = first + 2 * (chip ^ (number // cols)) + core
        route += [(i * cols + c, there * cols + (c ^ (number % cols))) for c in range(cols)]
    return lax.ppermute(block, ("row", "col"), route)


def gather_earlier(block, span):
    far = jnp.stack([block] + [shift_far(block, k, span, False) for k in range(1, span // 4)])
    same = jnp.stack([far, swap_near(far)])
    return same, swap_core(same)


def over_core(same, other):
    return (same.astype(F32) + swap_core(other.astype(BF16)).astype(F32)).astype(BF16)


def over_near(total):
    count = total.shape[0] // 2
    return (total[:count].astype(F32) + swap_near(total[count:]).astype(F32)).astype(BF16)


def over_far(total, span, wrap, forward):
    sign = 1 if forward else -1
    return [total[0]] + [shift_far(total[k], sign * k, span, wrap) for k in range(1, span // 4)]


def add_up(parts):
    return sum(p.astype(F32) for p in parts)


def gather_rows(block):
    rows = lax.axis_size("row")
    far = jnp.concatenate([block] + [shift_far(block, -k, rows, True) for k in range(1, rows // 4)], axis=0)
    same = jnp.concatenate([far, swap_near(far)], axis=0)
    return jnp.concatenate([same, swap_core(same)], axis=0)


def distances():
    rows, row = lax.axis_size("row"), lax.axis_index("row")
    order = [((row ^ near) + 4 * k) % rows for near in (0, 2, 1, 3) for k in range(rows // 4)]
    inverse = []
    for r in range(rows):
        step = r ^ row
        place = (step & 1) * 2 + (step >> 1 & 1)
        inverse.append(place * (rows // 4) + (r // 4 - row // 4) % (rows // 4))
    return jnp.stack(order), jnp.stack(inverse)


def reorder_kernel(order_ref, in_ref, out_ref):
    for at in range(in_ref.shape[1] // LANES):
        there = pl.multiple_of(order_ref[at] * LANES, LANES)
        out_ref[:, at * LANES : (at + 1) * LANES] = in_ref[:, pl.ds(there, LANES)]


def reorder_columns(array, order):
    tok, width = array.shape
    if width // order.shape[0] != LANES:
        blocks = array.reshape(tok, order.shape[0], -1)
        return jnp.take(blocks, order, axis=1).reshape(tok, width)
    return pl.pallas_call(
        reorder_kernel,
        in_specs=[pl.BlockSpec(memory_space=pltpu.SMEM), pl.BlockSpec(memory_space=pltpu.VMEM)],
        out_specs=pl.BlockSpec(memory_space=pltpu.VMEM),
        out_shape=jax.ShapeDtypeStruct(array.shape, array.dtype),
        cost_estimate=pl.CostEstimate(flops=0, bytes_accessed=4 * array.size, transcendentals=0),
        name="reorder_columns",
    )(order, array)


def after_all(arrays, *others):
    return lax.optimization_barrier(tuple(arrays) + others)[: len(arrays)]


def after(array, *others):
    return after_all((array,), *others)[0]


def cube_numbers():
    cols = lax.axis_size("col")
    return [(2 * pair + near) * cols + c for c in range(cols) for near in range(2) for pair in range(2)]


def gather_cube(block):
    same = jnp.concatenate([block] + [swap_cube(block, e) for e in cube_numbers()[1:]], axis=0)
    return same, swap_core(same)


def gather_cube_slowly(block):
    cols = lax.axis_size("col")
    block = jnp.concatenate([block, swap_cube(block, 2 * cols)], axis=0)
    block = jnp.concatenate([block, swap_cube(block, cols)], axis=0)
    block = jnp.concatenate([block, swap_cube(block, 1)], axis=0)
    return jnp.concatenate([block, swap_core(block)], axis=0)


def halve_cube(total, number):
    count = total.shape[0] // 2
    return total[:count].astype(F32) + swap_cube(total[count:].astype(BF16), number).astype(F32)


def group_rows():
    rows = lax.axis_size("row")
    return [list(range(first, first + MEMBERS)) for first in range(0, rows, MEMBERS)]


def across_groups():
    rows = lax.axis_size("row")
    return [list(range(member, rows, MEMBERS)) for member in range(MEMBERS)]


def exchange_group(blocks):
    return lax.all_to_all(
        blocks, "row", split_axis=0, concat_axis=0, tiled=True, axis_index_groups=group_rows()
    )


def halves(own, other, col):
    low = jnp.where(col == 0, own, other)
    high = jnp.where(col == 0, other, own)
    return jnp.concatenate([low, high], axis=0)


def partner(v):
    lane = lax.broadcasted_iota(jnp.int32, v.shape, 1)
    ahead = pltpu.roll(v, LANES - HALF // 2, 1)
    behind = pltpu.roll(v, HALF // 2, 1)
    return jnp.where(lane % HALF < HALF // 2, ahead, behind)


def head_mean(v):
    lane = lax.broadcasted_iota(jnp.int32, v.shape, 1)
    first = jnp.sum(jnp.where(lane < HALF, v, 0.0), axis=1, keepdims=True)
    second = jnp.sum(jnp.where(lane < HALF, 0.0, v), axis=1, keepdims=True)
    return jnp.where(lane < HALF, first, second) * (1.0 / HALF)


def head_forward(raw, gain, flag, cosine, sine):
    scaler = jnp.where(flag > 0, lax.rsqrt(head_mean(raw * raw) + EPSILON), 1.0)
    normed = raw * scaler * gain
    cosine = jnp.where(flag > 0, cosine, 1.0)
    sine = jnp.where(flag > 0, sine, 0.0)
    return normed * cosine + partner(normed) * sine


def head_backward(grad, raw, gain, flag, cosine, sine):
    on = flag > 0
    scaler = lax.rsqrt(head_mean(raw * raw) + EPSILON)
    back = grad * cosine - partner(grad) * sine
    scaled = back * gain
    inner = head_mean(scaled * raw)
    grad_raw = scaler * scaled - raw * (scaler * scaler * scaler) * inner
    gain_term = jnp.sum(jnp.where(on, back * raw * scaler, 0.0), axis=0, keepdims=True)
    return jnp.where(on, grad_raw, grad), gain_term


def heads_kernel(act_ref, w_ref, gain_ref, flag_ref, cos_ref, sin_ref, raw_ref, out_ref):
    raw = dot(act_ref[...], w_ref[...])
    raw_ref[...] = raw
    for part in range(raw.shape[1] // LANES):
        at = slice(part * LANES, (part + 1) * LANES)
        done = head_forward(raw[:, at], gain_ref[:, at], flag_ref[:, at], cos_ref[...], sin_ref[...])
        out_ref[:, at] = done.astype(BF16)


def heads_call(act, w_all, gain, flag, cosine, sine):
    tok, width = act.shape
    cols = gain.shape[1]
    block = 256
    whole = lambda shape: pl.BlockSpec(shape, lambda i: (0, 0))
    chunk = lambda rows: pl.BlockSpec((rows, block), lambda i: (0, i))
    return pl.pallas_call(
        heads_kernel,
        grid=(cols // block,),
        in_specs=[whole((tok, width)), chunk(width), chunk(1), chunk(1), whole((tok, LANES)), whole((tok, LANES))],
        out_specs=[chunk(tok), chunk(tok)],
        out_shape=[jax.ShapeDtypeStruct((tok, cols), F32), jax.ShapeDtypeStruct((tok, cols), BF16)],
        compiler_params=pltpu.CompilerParams(vmem_limit_bytes=VMEM_LIMIT),
        cost_estimate=pl.CostEstimate(flops=2 * tok * width * cols, bytes_accessed=2 * width * cols, transcendentals=0),
        name="project_heads",
    )(act, w_all, gain, flag, cosine, sine)


GROUPS = ((0, 4), (4, 4), (8, 2))
K_AT = (0, 64, 128)
V_AT = (256, 320, 192)


def stack_heads(wide, tok):
    turned, tall = [], []
    for pair in range(wide.shape[1] // LANES):
        chunk = wide[:, pair * LANES : (pair + 1) * LANES]
        flat = chunk.astype(F32).T.astype(BF16)
        turned += [flat[:HALF], flat[HALF:]]
        tall += [chunk[:, :HALF], chunk[:, HALF:]]
    return jnp.concatenate(turned, axis=1), jnp.concatenate(tall, axis=0)


def key_block(i, bounds_ref, limits_ref, same_ref, other_ref):
    tok = same_ref.shape[2]
    pair, near = i // 2, i % 2
    row = (bounds_ref[1] ^ (2 * near)) - 4 * pair
    kv = jnp.concatenate([same_ref[near, pair], other_ref[near, pair]], axis=0)
    key = lax.broadcasted_iota(jnp.int32, (2 * tok, tok), 0)
    key = key + jnp.where(key < tok, row * tok, (row ^ 1) * tok - tok)
    return near, pair, kv, (key >= limits_ref[0:1, :]) & (key <= limits_ref[1:2, :])


def forward_kernel(bounds_ref, limits_ref, q_ref, same_ref, other_ref, att_ref, turned_ref, inv_ref, q_turned):
    tok = q_ref.shape[0]
    turned, tall = stack_heads(q_ref[...], tok)
    q_turned[...] = turned
    turned_ref[...] = jnp.zeros_like(turned_ref)
    inv_ref[...] = jnp.zeros_like(inv_ref)

    @pl.loop(0, bounds_ref[0])
    def step(i):
        near, pair, kv, ok = key_block(i, bounds_ref, limits_ref, same_ref, other_ref)
        for g, (first, count) in enumerate(GROUPS):
            at = slice(first * tok, (first + count) * tok)
            keys = kv[:, K_AT[g] : K_AT[g] + HALF]
            vals = kv[:, V_AT[g] : V_AT[g] + HALF]
            logit = dot(keys, q_turned[:, at])
            allowed = jnp.concatenate([ok] * count, axis=1)
            expo = jnp.where(allowed, jnp.exp(logit), 0.0)
            inv_ref[:, at] += jnp.sum(expo, axis=0, keepdims=True)
            turned_ref[:, at] += dot(vals, expo.astype(BF16), ((0,), (0,)))

    inverse = 1.0 / inv_ref[...]
    inv_ref[...] = inverse
    turned_ref[...] = turned_ref[...] * inverse
    for pair in range(att_ref.shape[1] // LANES):
        at = 2 * pair * tok
        both = jnp.concatenate([turned_ref[:, at : at + tok], turned_ref[:, at + tok : at + 2 * tok]], axis=0)
        att_ref[:, pair * LANES : (pair + 1) * LANES] = both.T.astype(BF16)


def vmem(n):
    return [pl.BlockSpec(memory_space=pltpu.VMEM)] * n


SMEM = pl.BlockSpec(memory_space=pltpu.SMEM)


def forward_call(bounds, limits, q, same, other):
    tok, width = q.shape
    wide = width // HALF * tok
    work = same.size // same.shape[3] * 2 * wide
    return pl.pallas_call(
        forward_kernel,
        in_specs=[SMEM] + vmem(4),
        out_specs=vmem(3),
        out_shape=[
            jax.ShapeDtypeStruct((tok, width), BF16),
            jax.ShapeDtypeStruct((HALF, wide), F32),
            jax.ShapeDtypeStruct((1, wide), F32),
        ],
        scratch_shapes=[pltpu.VMEM((HALF, wide), BF16)],
        compiler_params=pltpu.CompilerParams(vmem_limit_bytes=VMEM_LIMIT),
        cost_estimate=pl.CostEstimate(flops=4 * HALF * work, bytes_accessed=4 * same.size, transcendentals=work),
        name="attention_forward",
    )(bounds, limits, q, same, other)


def backward_kernel(
    bounds_ref,
    limits_ref,
    q_ref,
    grad_ref,
    turned_ref,
    inv_ref,
    same_ref,
    other_ref,
    raw_ref,
    gain_ref,
    cos_ref,
    sin_ref,
    dq_ref,
    gain_grad_ref,
    same_out,
    other_out,
    q_turned,
    q_tall,
    g_turned,
    g_tall,
    dq_acc,
):
    tok = q_ref.shape[0]
    q_turned[...], q_tall[...] = stack_heads(q_ref[...], tok)
    g_turned[...], g_tall[...] = stack_heads(grad_ref[...], tok)
    dq_acc[...] = jnp.zeros_like(dq_acc)
    same_out[...] = jnp.zeros_like(same_out)
    other_out[...] = jnp.zeros_like(other_out)
    delta = jnp.sum(g_turned[...].astype(F32) * turned_ref[...], axis=0, keepdims=True)

    @pl.loop(0, bounds_ref[0])
    def step(i):
        near, pair, kv, ok = key_block(i, bounds_ref, limits_ref, same_ref, other_ref)
        for g, (first, count) in enumerate(GROUPS):
            at = slice(first * tok, (first + count) * tok)
            keys = kv[:, K_AT[g] : K_AT[g] + HALF]
            vals = kv[:, V_AT[g] : V_AT[g] + HALF]
            allowed = jnp.concatenate([ok] * count, axis=1)
            prob = jnp.where(allowed, jnp.exp(dot(keys, q_turned[:, at])) * inv_ref[:, at], 0.0)
            d_score = (prob * (dot(vals, g_turned[:, at]) - delta[:, at])).astype(BF16)
            d_keys = dot(d_score, q_tall[at, :]).astype(BF16)
            d_vals = dot(prob.astype(BF16), g_tall[at, :]).astype(BF16)
            dq_acc[:, at] += dot(keys, d_score, ((0,), (0,)))
            same_out[near, pair, :, K_AT[g] : K_AT[g] + HALF] = d_keys[:tok]
            other_out[near, pair, :, K_AT[g] : K_AT[g] + HALF] = d_keys[tok:]
            same_out[near, pair, :, V_AT[g] : V_AT[g] + HALF] = d_vals[:tok]
            other_out[near, pair, :, V_AT[g] : V_AT[g] + HALF] = d_vals[tok:]

    total = jnp.zeros((1, LANES), F32)
    for pair in range(dq_ref.shape[1] // LANES):
        at = 2 * pair * tok
        both = jnp.concatenate([dq_acc[:, at : at + tok], dq_acc[:, at + tok : at + 2 * tok]], axis=0)
        cols = slice(pair * LANES, (pair + 1) * LANES)
        d_raw, term = head_backward(
            both.T * SCALE, raw_ref[:, cols], gain_ref[...], jnp.ones((1, LANES), F32), cos_ref[...], sin_ref[...]
        )
        dq_ref[:, cols] = d_raw.astype(BF16)
        total += term
    gain_grad_ref[...] = total


def backward_call(bounds, limits, q, grad, turned, inv, same, other, raw, gain, cosine, sine):
    tok, width = q.shape
    wide = width // HALF * tok
    work = same.size // same.shape[3] * 2 * wide
    return pl.pallas_call(
        backward_kernel,
        in_specs=[SMEM] + vmem(11),
        out_specs=vmem(4),
        out_shape=[
            jax.ShapeDtypeStruct((tok, width), BF16),
            jax.ShapeDtypeStruct((1, LANES), F32),
            jax.ShapeDtypeStruct(same.shape, BF16),
            jax.ShapeDtypeStruct(other.shape, BF16),
        ],
        scratch_shapes=[
            pltpu.VMEM((HALF, wide), BF16),
            pltpu.VMEM((wide, HALF), BF16),
            pltpu.VMEM((HALF, wide), BF16),
            pltpu.VMEM((wide, HALF), BF16),
            pltpu.VMEM((HALF, wide), F32),
        ],
        compiler_params=pltpu.CompilerParams(vmem_limit_bytes=VMEM_LIMIT),
        cost_estimate=pl.CostEstimate(flops=10 * HALF * work, bytes_accessed=8 * same.size, transcendentals=work),
        name="attention_backward",
    )(bounds, limits, q, grad, turned, inv, same, other, raw, gain, cosine, sine)


def kv_back_kernel(raw_ref, gain_ref, flag_ref, cos_ref, sin_ref, *refs):
    *part_refs, out_ref, gain_grad_ref = refs
    total = jnp.zeros((1, LANES), F32)
    for part in range(out_ref.shape[1] // LANES):
        at = slice(part * LANES, (part + 1) * LANES)
        grad = sum(ref[:, at].astype(F32) for ref in part_refs)
        done, term = head_backward(
            grad, raw_ref[:, at], gain_ref[:, at], flag_ref[:, at], cos_ref[...], sin_ref[...]
        )
        out_ref[:, at] = done.astype(BF16)
        total += term
    gain_grad_ref[...] = total


def kv_back_call(parts, raw, gain, flag, cosine, sine):
    tok, width = raw.shape
    return pl.pallas_call(
        kv_back_kernel,
        in_specs=vmem(5 + len(parts)),
        out_specs=vmem(2),
        out_shape=[jax.ShapeDtypeStruct((tok, width), BF16), jax.ShapeDtypeStruct((1, LANES), F32)],
        compiler_params=pltpu.CompilerParams(vmem_limit_bytes=VMEM_LIMIT),
        cost_estimate=pl.CostEstimate(flops=30 * tok * width, bytes_accessed=2 * tok * width * len(parts), transcendentals=0),
        name="key_value_heads_back",
    )(raw, gain, flag, cosine, sine, *parts)


def rope_tables(positions, head_dim):
    half = head_dim // 2
    inverse = jnp.exp(jnp.arange(half, dtype=F32) * (-2.0 * math.log(10000.0) / head_dim))
    angles = positions.astype(F32)[:, None] * inverse[None, :]
    cosine, sine = jnp.cos(angles), jnp.sin(angles)
    return jnp.concatenate([cosine] * 4, axis=1), jnp.concatenate([-sine, sine, -sine, sine], axis=1)


def norm_scale(vectors):
    return lax.rsqrt(jnp.mean(vectors * vectors, axis=-1, keepdims=True) + EPSILON)


def norm_back(vectors, scaler, gains, grads_in):
    scaled = grads_in * gains
    inner_mean = jnp.mean(scaled * vectors, axis=-1, keepdims=True)
    return scaler * scaled - vectors * (scaler * scaler * scaler) * inner_mean


def backwards(array, axis, width):
    count = array.shape[axis] // width
    pieces = [lax.slice_in_dim(array, i * width, (i + 1) * width, axis=axis) for i in range(count)]
    return jnp.concatenate(pieces[::-1], axis=axis)


def body(
    tokens,
    w_query,
    key_value_weight,
    w_out,
    w_gate,
    w_up,
    w_down,
    attn_gain,
    ffn_gain,
    query_gain,
    key_gain,
    segments,
    positions,
    out_grad,
):
    tok, width = tokens.shape
    rows = lax.axis_size("row")
    row = lax.axis_index("row")
    col = lax.axis_index("col")
    cols = lax.axis_size("col")
    w_rows = w_query.shape[0]
    q_width = w_query.shape[1]
    kv_half = key_value_weight.shape[1] // 2
    ff_cols = w_gate.shape[1]
    ff = ff_cols // MEMBERS
    seq_len = min(SEQ_MAX, tok * rows)
    span = seq_len // tok
    half = tok // 2

    def kv_pick(order):
        k = [key_value_weight[:, h * HALF : (h + 1) * HALF] for h in order]
        v = [key_value_weight[:, kv_half + h * HALF : kv_half + (h + 1) * HALF] for h in order]
        return jnp.concatenate([k[0], k[1], k[2], v[2], v[0], v[1]], axis=1)

    w_kv = jnp.where(col == 0, kv_pick((0, 1, 2)), kv_pick((4, 3, 2)))
    w_q = jnp.where(col == 0, w_query, backwards(w_query, 1, LANES))
    w_o = jnp.where(col == 0, w_out, backwards(w_out, 0, LANES))
    w_all = lax.all_gather(jnp.concatenate([w_q, w_kv, w_o.T], axis=1), "row", axis=0, tiled=True)
    kv_width = w_kv.shape[1]
    head_cols = q_width + kv_width
    w_o_all = w_all[:, head_cols:]
    og_low = lax.dynamic_slice_in_dim(out_grad, col * half, half, 0)
    og_all = gather_cube_slowly(og_low)
    order, inverse_order = distances()
    group = og_all.shape[0]

    w_ff = jnp.concatenate(
        [
            w_gate.reshape(w_rows, MEMBERS, ff),
            w_up.reshape(w_rows, MEMBERS, ff),
            w_down.T.reshape(w_rows, MEMBERS, ff),
        ],
        axis=2,
    ).transpose(1, 0, 2)
    w_ff = jnp.concatenate([after(w_ff, w_all)] * (rows // MEMBERS), axis=0)
    w_ff_all = lax.all_to_all(w_ff, "row", split_axis=0, concat_axis=0, tiled=True).reshape(width, 3 * ff)

    input_f = tokens.astype(F32)
    act_scale = norm_scale(input_f)
    act_low = (input_f * act_scale * attn_gain).astype(BF16)
    cosine, sine = rope_tables(positions, HALF)
    q_lanes = jnp.tile(query_gain, 2)[None, :]
    k_lanes = jnp.tile(key_gain, 2)[None, :]
    kv_flag = jnp.concatenate([jnp.ones((1, 3 * HALF), F32), jnp.zeros((1, 3 * HALF), F32)], axis=1)
    kv_gain = jnp.where(kv_flag > 0, jnp.tile(k_lanes, (1, 3)), 1.0)
    q_flag = jnp.ones((1, q_width), F32)
    q_gain = jnp.tile(q_lanes * SCALE, (1, q_width // LANES))
    act_blocks = reorder_columns(act_low, order)
    gain = jnp.concatenate([q_gain, kv_gain], axis=1)
    flag = jnp.concatenate([q_flag, kv_flag], axis=1)
    act_low, og_all = lax.optimization_barrier((act_low, og_all))
    raw, heads = heads_call(act_low, w_all, gain, flag, cosine, sine)
    query, kv_low = heads[:, :q_width], heads[:, q_width:]
    q_raw, kv_raw = raw[:, :q_width], raw[:, q_width:]
    same_kv, other_kv = gather_earlier(kv_low, span)

    in_span = row % span
    seq_segments = lax.dynamic_slice_in_dim(segments, (row - in_span) * tok, seq_len, 0)
    own_segments = lax.dynamic_slice_in_dim(segments, row * tok, tok, 0)
    own_index = in_span * tok + jnp.arange(tok, dtype=jnp.int32)
    index = jnp.arange(seq_len, dtype=jnp.int32)
    start = jnp.min(jnp.where(seq_segments[None, :] == own_segments[:, None], index[None, :], seq_len), axis=1)
    start = jnp.where(own_segments < 0, own_index, start)
    limits = jnp.stack([start, own_index])
    bounds = jnp.stack([2 * (in_span // 4 + 1 - jnp.min(start) // (4 * tok)), in_span])
    attn_low, turned, inv = forward_call(bounds, limits, query, same_kv, other_kv)
    attn_part = dot(attn_low, w_o_all, ((1,), (1,))).astype(BF16)

    def mine(array, which):
        return lax.dynamic_slice_in_dim(array, which * half, half, 0)

    arrived = swap_col(mine(attn_part, 1 - col))
    hidden = mine(input_f, col) + (mine(attn_part, col).astype(F32) + arrived.astype(F32))

    ffn_scale = norm_scale(hidden)
    ffn_low = (hidden * ffn_scale * ffn_gain).astype(BF16)
    ffn_all = jnp.concatenate(gather_cube(ffn_low), axis=0)
    gate_up = dot(ffn_all, w_ff_all[:, : 2 * ff])
    gate_pre, up_pre = gate_up[:, :ff], gate_up[:, ff:]
    d_inner = dot(og_all, w_ff_all[:, 2 * ff :])
    sigma = jax.nn.sigmoid(gate_pre)
    silu_gate = gate_pre * sigma
    inner_low = (silu_gate * up_pre).astype(BF16)
    d_gate = d_inner * up_pre * (sigma * (1.0 + gate_pre * (1.0 - sigma)))
    d_up = d_inner * silu_gate
    d_gate_up = jnp.concatenate([d_gate, d_up], axis=1).astype(BF16)

    w_gate_up = w_ff_all[:, : 2 * ff]
    away = dot(d_gate_up[group // 2 :], w_gate_up, ((1,), (1,))).astype(BF16)
    here = dot(d_gate_up[: group // 2], w_gate_up, ((1,), (1,)))
    grads_ff = jnp.concatenate(
        [dot(ffn_all, d_gate_up, ((0,), (0,))), dot(og_all, inner_low, ((0,), (0,)))], axis=1
    ).astype(BF16)
    total = (here + swap_core(away).astype(F32)).astype(BF16).reshape(-1, half, width)
    total, grads_ff = lax.optimization_barrier((total, grads_ff))
    grads_ff = lax.psum_scatter(
        grads_ff, "row", scatter_dimension=0, tiled=True, axis_index_groups=across_groups()
    )
    for number in (1, cols, 2 * cols):
        total = halve_cube(total, number)
    ffn_back = total[0]
    d_hidden = og_low.astype(F32) + norm_back(hidden, ffn_scale, ffn_gain, ffn_back)
    d_hidden_half = d_hidden.astype(BF16)
    d_hidden_low = halves(d_hidden_half, swap_col(d_hidden_half), col)

    d_attn = dot(d_hidden_low, w_o_all).astype(BF16)
    d_q, q_gain_part, same_d, other_d = backward_call(
        bounds, limits, query, d_attn, turned, inv, same_kv, other_kv, q_raw, q_lanes, cosine, sine
    )
    d_kv_total = over_core(same_d, other_d).reshape(-1, tok, same_d.shape[3])

    inner_low = after(inner_low, d_hidden_low)
    w_down_all = w_ff_all[:, 2 * ff :]
    away = dot(inner_low[group // 2 :], w_down_all, ((1,), (1,))).astype(BF16)
    here = dot(inner_low[: group // 2], w_down_all, ((1,), (1,)))
    ffn_out = over_core(here, away).reshape(-1, half, width)
    ffn_out = halve_cube(ffn_out, 1)

    grad_oq = jnp.concatenate(
        [dot(d_hidden_low, attn_low, ((0,), (0,))), dot(act_low, d_q, ((0,), (0,)))], axis=1
    ).astype(BF16)
    grad_oq = lax.psum_scatter(grad_oq, "row", scatter_dimension=0, tiled=True).astype(F32)

    def partial_grad(left, right):
        return dot(left, right, ((0,), (0,))).reshape(rows, w_rows, -1)

    d_kv_total = over_near(d_kv_total)
    kv_parts = over_far(d_kv_total, span, False, False)
    d_kv, k_gain_part = kv_back_call(kv_parts, kv_raw, kv_gain, kv_flag, cosine, sine)
    ffn_out = after(ffn_out, d_kv)
    for number in (cols, 2 * cols):
        ffn_out = halve_cube(ffn_out, number)
    out_half = (hidden + ffn_out[0]).astype(BF16)
    output = halves(out_half, swap_col(out_half), col)

    d_one = jnp.concatenate([d_q, d_kv], axis=1)
    act_back = dot(d_one, w_all[:, :head_cols], ((1,), (1,))).astype(BF16)
    act_back = act_back.astype(F32) + swap_col(act_back).astype(F32)
    input_grad = d_hidden_low.astype(F32) + norm_back(input_f, act_scale, attn_gain, act_back)

    grad_o, grad_q = grad_oq[:, :q_width].T, grad_oq[:, q_width:]
    per_row = HALF // rows
    fold = lambda part: (part[0, :HALF] + part[0, HALF:]).reshape(rows, 1, per_row)
    small = jnp.concatenate([fold(q_gain_part), fold(k_gain_part)], axis=2)
    small = jnp.take(small, order, axis=0)
    small = jnp.pad(small, ((0, 0), (0, 15), (0, d_kv.shape[1] - 2 * per_row)))
    kv_partial = jnp.concatenate([partial_grad(act_blocks, d_kv), small], axis=1)
    kv_partial = over_near(over_core(kv_partial[: rows // 2], kv_partial[rows // 2 :]))
    grad_kv = add_up(over_far(kv_partial, rows, True, True))
    grad_kv, small = grad_kv[:w_rows], grad_kv[w_rows, : 2 * per_row]
    grad_query = jnp.where(col == 0, grad_q, backwards(grad_q, 1, LANES))
    grad_out = jnp.where(col == 0, grad_o, backwards(grad_o, 0, LANES))

    kv_own = grad_kv.astype(BF16)
    kv_away = swap_col(kv_own)
    kv_first = jnp.where(col == 0, kv_own, kv_away).astype(F32)
    kv_last = jnp.where(col == 0, kv_away, kv_own).astype(F32)

    def one_head(array, at):
        return array[:, at : at + HALF]

    pieces = []
    for at in (K_AT, V_AT):
        pieces += [one_head(kv_first, at[0]), one_head(kv_first, at[1])]
        pieces += [one_head(kv_first, at[2]) + one_head(kv_last, at[2])]
        pieces += [one_head(kv_last, at[1]), one_head(kv_last, at[0])]
    grad_keyval = jnp.concatenate(pieces, axis=1)

    grads_ff = exchange_group(grads_ff.reshape(MEMBERS, w_rows, 3 * ff))
    grads_ff = grads_ff.astype(F32).transpose(1, 0, 2)
    grad_gate = grads_ff[:, :, :ff].reshape(w_rows, ff_cols)
    grad_up = grads_ff[:, :, ff : 2 * ff].reshape(w_rows, ff_cols)
    grad_down = grads_ff[:, :, 2 * ff :].reshape(w_rows, ff_cols).T

    attn_part_gain = jnp.sum(jnp.concatenate([grad_q * w_q.astype(F32), grad_kv * w_kv.astype(F32)], axis=1), axis=1)
    ffn_part_gain = jnp.sum(grad_gate * w_gate.astype(F32) + grad_up * w_up.astype(F32), axis=1)
    gains = jnp.concatenate([attn_part_gain, ffn_part_gain, small])
    gains = gains + swap_col(gains)
    own_gains = lambda whole: lax.dynamic_slice_in_dim(whole, row * w_rows, w_rows, 0)
    grad_attn_gain = gains[:w_rows] / own_gains(attn_gain)
    grad_ffn_gain = gains[w_rows : 2 * w_rows] / own_gains(ffn_gain)
    grad_query_gain = gains[2 * w_rows : 2 * w_rows + per_row]
    grad_key_gain = gains[2 * w_rows + per_row :]
    return (
        output,
        input_grad,
        grad_query,
        grad_keyval,
        grad_out,
        grad_gate,
        grad_up,
        grad_down,
        grad_attn_gain,
        grad_ffn_gain,
        grad_query_gain,
        grad_key_gain,
    )


def solution(mesh):
    placed = (
        P("row", None),
        P("row", "col"),
        P("row", None),
        P("col", "row"),
        P("row", "col"),
        P("row", "col"),
        P("col", "row"),
        P(),
        P(),
        P(),
        P(),
        P(),
        P("row"),
        P("row", None),
    )
    return jax.shard_map(
        body,
        mesh=mesh,
        in_specs=placed,
        out_specs=(
            P("row", None),
            P("row", None),
            P("row", "col"),
            P("row", None),
            P("col", "row"),
            P("row", "col"),
            P("row", "col"),
            P("col", "row"),
            P("row"),
            P("row"),
            P("row"),
            P("row"),
        ),
        check_vma=False,
    )
```

```python
import math

import jax
import jax.numpy as jnp
from jax import lax
from jax.experimental import pallas as pl
from jax.experimental.pallas import tpu as pltpu
from jax.sharding import PartitionSpec as P

EPSILON = 1e-06
SCALE = 0.125
SEQ_MAX = 4096
MEMBERS = 8
LANES = 128
HALF = 64
F32 = jnp.float32
BF16 = jnp.bfloat16
VMEM_LIMIT = 56 * 1024 * 1024


def dot(a, b, dims=((1,), (0,))):
    return lax.dot_general(a, b, (dims, ((), ())), preferred_element_type=F32)


def swap_core(block):
    rows = lax.axis_size("row")
    return lax.ppermute(block, "row", [(i, i ^ 1) for i in range(rows)])


def swap_col(block):
    return lax.ppermute(block, "col", [(0, 1), (1, 0)])


def shift_far(block, steps, span, wrap):
    rows = lax.axis_size("row")
    route = []
    for i in range(rows):
        first, at = i // span * span, i % span + 4 * steps
        if wrap or 0 <= at < span:
            route.append((i, first + at % span))
    return lax.ppermute(block, "row", route)


def swap_near(block):
    rows = lax.axis_size("row")
    return lax.ppermute(block, "row", [(i, i ^ 2) for i in range(rows)])


def swap_cube(block, number):
    rows, cols = lax.axis_size("row"), lax.axis_size("col")
    route = []
    for i in range(rows):
        first, chip, core = i // MEMBERS * MEMBERS, i % MEMBERS // 2, i % 2
        there = first + 2 * (chip ^ (number // cols)) + core
        route += [(i * cols + c, there * cols + (c ^ (number % cols))) for c in range(cols)]
    return lax.ppermute(block, ("row", "col"), route)


def gather_earlier(block, span):
    far = jnp.stack([block] + [shift_far(block, k, span, False) for k in range(1, span // 4)])
    same = jnp.stack([far, swap_near(far)])
    return same, swap_core(same)


def over_core(same, other):
    return (same.astype(F32) + swap_core(other.astype(BF16)).astype(F32)).astype(BF16)


def over_near(total):
    count = total.shape[0] // 2
    return (total[:count].astype(F32) + swap_near(total[count:]).astype(F32)).astype(BF16)


def over_far(total, span, wrap, forward):
    sign = 1 if forward else -1
    return [total[0]] + [shift_far(total[k], sign * k, span, wrap) for k in range(1, span // 4)]


def add_up(parts):
    return sum(p.astype(F32) for p in parts)


def gather_rows(block):
    rows = lax.axis_size("row")
    far = jnp.concatenate([block] + [shift_far(block, -k, rows, True) for k in range(1, rows // 4)], axis=0)
    same = jnp.concatenate([far, swap_near(far)], axis=0)
    return jnp.concatenate([same, swap_core(same)], axis=0)


def distances(far):
    rows, row = lax.axis_size("row"), lax.axis_index("row")
    order = [
        ((row ^ near) + 4 * k) % rows if far else (row ^ near) % 4 + 4 * k for near in (0, 2, 1, 3) for k in range(rows // 4)
    ]
    return jnp.stack(order)


def reorder_kernel(order_ref, in_ref, out_ref):
    for at in range(in_ref.shape[1] // LANES):
        there = pl.multiple_of(order_ref[at] * LANES, LANES)
        out_ref[:, at * LANES : (at + 1) * LANES] = in_ref[:, pl.ds(there, LANES)]


def reorder_columns(array, order):
    tok, width = array.shape
    if width // order.shape[0] != LANES:
        blocks = array.reshape(tok, order.shape[0], -1)
        return jnp.take(blocks, order, axis=1).reshape(tok, width)
    return pl.pallas_call(
        reorder_kernel,
        in_specs=[pl.BlockSpec(memory_space=pltpu.SMEM), pl.BlockSpec(memory_space=pltpu.VMEM)],
        out_specs=pl.BlockSpec(memory_space=pltpu.VMEM),
        out_shape=jax.ShapeDtypeStruct(array.shape, array.dtype),
        cost_estimate=pl.CostEstimate(flops=0, bytes_accessed=4 * array.size, transcendentals=0),
        name="reorder_columns",
    )(order, array)


def after_all(arrays, *others):
    return lax.optimization_barrier(tuple(arrays) + others)[: len(arrays)]


def after(array, *others):
    return after_all((array,), *others)[0]


def cube_numbers():
    cols = lax.axis_size("col")
    return [(2 * pair + near) * cols + c for c in range(cols) for near in range(2) for pair in range(2)]


def gather_cube(block):
    same = jnp.concatenate([block] + [swap_cube(block, e) for e in cube_numbers()[1:]], axis=0)
    return same, swap_core(same)


def gather_cube_slowly(block):
    cols = lax.axis_size("col")
    block = jnp.concatenate([block, swap_cube(block, 2 * cols)], axis=0)
    block = jnp.concatenate([block, swap_cube(block, cols)], axis=0)
    block = jnp.concatenate([block, swap_cube(block, 1)], axis=0)
    return jnp.concatenate([block, swap_core(block)], axis=0)


def halve(total, axis, number):
    here, away = (lax.index_in_dim(total, i, axis, keepdims=False) for i in range(2))
    return here.astype(F32) + swap_cube(away.astype(BF16), number).astype(F32)


def far_groups():
    rows = lax.axis_size("row")
    return [list(range(near, rows, 4)) for near in range(4)]


def pick(array, place, axis):
    first = lax.index_in_dim(array, 0, axis, keepdims=False)
    second = lax.index_in_dim(array, 1, axis, keepdims=False)
    return jnp.where(place == 0, first, second), jnp.where(place == 0, second, first)


def group_rows():
    rows = lax.axis_size("row")
    return [list(range(first, first + MEMBERS)) for first in range(0, rows, MEMBERS)]


def across_groups():
    rows = lax.axis_size("row")
    return [list(range(member, rows, MEMBERS)) for member in range(MEMBERS)]


def exchange_group(blocks):
    return lax.all_to_all(
        blocks, "row", split_axis=0, concat_axis=0, tiled=True, axis_index_groups=group_rows()
    )


def halves(own, other, col):
    low = jnp.where(col == 0, own, other)
    high = jnp.where(col == 0, other, own)
    return jnp.concatenate([low, high], axis=0)


def partner(v):
    lane = lax.broadcasted_iota(jnp.int32, v.shape, 1)
    ahead = pltpu.roll(v, LANES - HALF // 2, 1)
    behind = pltpu.roll(v, HALF // 2, 1)
    return jnp.where(lane % HALF < HALF // 2, ahead, behind)


def head_mean(v):
    lane = lax.broadcasted_iota(jnp.int32, v.shape, 1)
    first = jnp.sum(jnp.where(lane < HALF, v, 0.0), axis=1, keepdims=True)
    second = jnp.sum(jnp.where(lane < HALF, 0.0, v), axis=1, keepdims=True)
    return jnp.where(lane < HALF, first, second) * (1.0 / HALF)


def head_forward(raw, gain, flag, cosine, sine):
    scaler = jnp.where(flag > 0, lax.rsqrt(head_mean(raw * raw) + EPSILON), 1.0)
    normed = raw * scaler * gain
    cosine = jnp.where(flag > 0, cosine, 1.0)
    sine = jnp.where(flag > 0, sine, 0.0)
    return normed * cosine + partner(normed) * sine


def head_backward(grad, raw, gain, flag, cosine, sine):
    on = flag > 0
    scaler = lax.rsqrt(head_mean(raw * raw) + EPSILON)
    back = grad * cosine - partner(grad) * sine
    scaled = back * gain
    inner = head_mean(scaled * raw)
    grad_raw = scaler * scaled - raw * (scaler * scaler * scaler) * inner
    gain_term = jnp.sum(jnp.where(on, back * raw * scaler, 0.0), axis=0, keepdims=True)
    return jnp.where(on, grad_raw, grad), gain_term


def heads_kernel(act_ref, w_ref, gain_ref, flag_ref, cos_ref, sin_ref, raw_ref, out_ref):
    raw = dot(act_ref[...], w_ref[...])
    raw_ref[...] = raw
    for part in range(raw.shape[1] // LANES):
        at = slice(part * LANES, (part + 1) * LANES)
        done = head_forward(raw[:, at], gain_ref[:, at], flag_ref[:, at], cos_ref[...], sin_ref[...])
        out_ref[:, at] = done.astype(BF16)


def heads_call(act, w_all, gain, flag, cosine, sine):
    tok, width = act.shape
    cols = gain.shape[1]
    block = 256
    whole = lambda shape: pl.BlockSpec(shape, lambda i: (0, 0))
    chunk = lambda rows: pl.BlockSpec((rows, block), lambda i: (0, i))
    return pl.pallas_call(
        heads_kernel,
        grid=(cols // block,),
        in_specs=[whole((tok, width)), chunk(width), chunk(1), chunk(1), whole((tok, LANES)), whole((tok, LANES))],
        out_specs=[chunk(tok), chunk(tok)],
        out_shape=[jax.ShapeDtypeStruct((tok, cols), F32), jax.ShapeDtypeStruct((tok, cols), BF16)],
        compiler_params=pltpu.CompilerParams(vmem_limit_bytes=VMEM_LIMIT),
        cost_estimate=pl.CostEstimate(flops=2 * tok * width * cols, bytes_accessed=2 * width * cols, transcendentals=0),
        name="project_heads",
    )(act, w_all, gain, flag, cosine, sine)


def pack_kernel(col_ref, q_ref, kv_ref, o_ref, out_ref):
    first = col_ref[0] == 0
    pairs = q_ref.shape[1] // LANES
    half = kv_ref.shape[1] // 2
    heads = half // HALF

    def head(number, offset):
        one = kv_ref[:, offset + number * HALF : offset + (number + 1) * HALF]
        two = kv_ref[:, offset + (heads - 1 - number) * HALF : offset + (heads - number) * HALF]
        return jnp.where(first, one, two)

    for pair in range(pairs):
        here = slice(pair * LANES, (pair + 1) * LANES)
        there = slice((pairs - 1 - pair) * LANES, (pairs - pair) * LANES)
        out_ref[:, here] = jnp.where(first, q_ref[:, here], q_ref[:, there])
        turned = jnp.where(first, o_ref[here, :].astype(F32), o_ref[there, :].astype(F32)).T
        at = q_ref.shape[1] + 6 * HALF + pair * LANES
        out_ref[:, at : at + LANES] = turned.astype(BF16)
    at = q_ref.shape[1]
    for one, two in ((head(0, 0), head(1, 0)), (head(2, 0), head(2, half)), (head(0, half), head(1, half))):
        out_ref[:, at : at + LANES] = jnp.concatenate([one, two], axis=1)
        at += LANES


def pack_call(col, w_query, w_kv, w_out):
    lines, width = w_query.shape
    return pl.pallas_call(
        pack_kernel,
        in_specs=[pl.BlockSpec(memory_space=pltpu.SMEM)] + [pl.BlockSpec(memory_space=pltpu.VMEM)] * 3,
        out_specs=pl.BlockSpec(memory_space=pltpu.VMEM),
        out_shape=jax.ShapeDtypeStruct((lines, 2 * width + 6 * HALF), BF16),
        cost_estimate=pl.CostEstimate(flops=0, bytes_accessed=10 * w_query.size, transcendentals=0),
        name="pack_weights",
    )(col.reshape(1), w_query, w_kv, w_out)


GROUPS = ((0, 4), (4, 4), (8, 2))
K_AT = (0, 64, 128)
V_AT = (256, 320, 192)


def stack_heads(wide, tok):
    turned, tall = [], []
    for pair in range(wide.shape[1] // LANES):
        chunk = wide[:, pair * LANES : (pair + 1) * LANES]
        flat = chunk.astype(F32).T.astype(BF16)
        turned += [flat[:HALF], flat[HALF:]]
        tall += [chunk[:, :HALF], chunk[:, HALF:]]
    return jnp.concatenate(turned, axis=1), jnp.concatenate(tall, axis=0)


def key_block(i, bounds_ref, limits_ref, same_ref, other_ref):
    tok = same_ref.shape[2]
    pair, near = i // 2, i % 2
    row = (bounds_ref[1] ^ (2 * near)) - 4 * pair
    kv = jnp.concatenate([same_ref[near, pair], other_ref[near, pair]], axis=0)
    key = lax.broadcasted_iota(jnp.int32, (2 * tok, tok), 0)
    key = key + jnp.where(key < tok, row * tok, (row ^ 1) * tok - tok)
    return near, pair, kv, (key >= limits_ref[0:1, :]) & (key <= limits_ref[1:2, :])


def forward_kernel(bounds_ref, limits_ref, q_ref, same_ref, other_ref, att_ref, turned_ref, inv_ref, q_turned):
    tok = q_ref.shape[0]
    turned, tall = stack_heads(q_ref[...], tok)
    q_turned[...] = turned
    turned_ref[...] = jnp.zeros_like(turned_ref)
    inv_ref[...] = jnp.zeros_like(inv_ref)

    @pl.loop(0, bounds_ref[0])
    def step(i):
        near, pair, kv, ok = key_block(i, bounds_ref, limits_ref, same_ref, other_ref)
        for g, (first, count) in enumerate(GROUPS):
            at = slice(first * tok, (first + count) * tok)
            keys = kv[:, K_AT[g] : K_AT[g] + HALF]
            vals = kv[:, V_AT[g] : V_AT[g] + HALF]
            logit = dot(keys, q_turned[:, at])
            allowed = jnp.concatenate([ok] * count, axis=1)
            expo = jnp.where(allowed, jnp.exp(logit), 0.0)
            inv_ref[:, at] += jnp.sum(expo, axis=0, keepdims=True)
            turned_ref[:, at] += dot(vals, expo.astype(BF16), ((0,), (0,)))

    inverse = 1.0 / inv_ref[...]
    inv_ref[...] = inverse
    turned_ref[...] = turned_ref[...] * inverse
    for pair in range(att_ref.shape[1] // LANES):
        at = 2 * pair * tok
        both = jnp.concatenate([turned_ref[:, at : at + tok], turned_ref[:, at + tok : at + 2 * tok]], axis=0)
        att_ref[:, pair * LANES : (pair + 1) * LANES] = both.T.astype(BF16)


def vmem(n):
    return [pl.BlockSpec(memory_space=pltpu.VMEM)] * n


SMEM = pl.BlockSpec(memory_space=pltpu.SMEM)


def forward_call(bounds, limits, q, same, other):
    tok, width = q.shape
    wide = width // HALF * tok
    work = same.size // same.shape[3] * 2 * wide
    return pl.pallas_call(
        forward_kernel,
        in_specs=[SMEM] + vmem(4),
        out_specs=vmem(3),
        out_shape=[
            jax.ShapeDtypeStruct((tok, width), BF16),
            jax.ShapeDtypeStruct((HALF, wide), F32),
            jax.ShapeDtypeStruct((1, wide), F32),
        ],
        scratch_shapes=[pltpu.VMEM((HALF, wide), BF16)],
        compiler_params=pltpu.CompilerParams(vmem_limit_bytes=VMEM_LIMIT),
        cost_estimate=pl.CostEstimate(flops=4 * HALF * work, bytes_accessed=4 * same.size, transcendentals=work),
        name="attention_forward",
    )(bounds, limits, q, same, other)


def backward_kernel(
    bounds_ref,
    limits_ref,
    q_ref,
    grad_ref,
    turned_ref,
    inv_ref,
    same_ref,
    other_ref,
    raw_ref,
    gain_ref,
    cos_ref,
    sin_ref,
    dq_ref,
    gain_grad_ref,
    same_out,
    other_out,
    q_turned,
    q_tall,
    g_turned,
    g_tall,
    dq_acc,
):
    tok = q_ref.shape[0]
    q_turned[...], q_tall[...] = stack_heads(q_ref[...], tok)
    g_turned[...], g_tall[...] = stack_heads(grad_ref[...], tok)
    dq_acc[...] = jnp.zeros_like(dq_acc)
    same_out[...] = jnp.zeros_like(same_out)
    other_out[...] = jnp.zeros_like(other_out)
    delta = jnp.sum(g_turned[...].astype(F32) * turned_ref[...], axis=0, keepdims=True)

    @pl.loop(0, bounds_ref[0])
    def step(i):
        near, pair, kv, ok = key_block(i, bounds_ref, limits_ref, same_ref, other_ref)
        for g, (first, count) in enumerate(GROUPS):
            at = slice(first * tok, (first + count) * tok)
            keys = kv[:, K_AT[g] : K_AT[g] + HALF]
            vals = kv[:, V_AT[g] : V_AT[g] + HALF]
            allowed = jnp.concatenate([ok] * count, axis=1)
            prob = jnp.where(allowed, jnp.exp(dot(keys, q_turned[:, at])) * inv_ref[:, at], 0.0)
            d_score = (prob * (dot(vals, g_turned[:, at]) - delta[:, at])).astype(BF16)
            d_keys = dot(d_score, q_tall[at, :]).astype(BF16)
            d_vals = dot(prob.astype(BF16), g_tall[at, :]).astype(BF16)
            dq_acc[:, at] += dot(keys, d_score, ((0,), (0,)))
            same_out[near, pair, :, K_AT[g] : K_AT[g] + HALF] = d_keys[:tok]
            other_out[near, pair, :, K_AT[g] : K_AT[g] + HALF] = d_keys[tok:]
            same_out[near, pair, :, V_AT[g] : V_AT[g] + HALF] = d_vals[:tok]
            other_out[near, pair, :, V_AT[g] : V_AT[g] + HALF] = d_vals[tok:]

    total = jnp.zeros((1, LANES), F32)
    for pair in range(dq_ref.shape[1] // LANES):
        at = 2 * pair * tok
        both = jnp.concatenate([dq_acc[:, at : at + tok], dq_acc[:, at + tok : at + 2 * tok]], axis=0)
        cols = slice(pair * LANES, (pair + 1) * LANES)
        d_raw, term = head_backward(
            both.T * SCALE, raw_ref[:, cols], gain_ref[...], jnp.ones((1, LANES), F32), cos_ref[...], sin_ref[...]
        )
        dq_ref[:, cols] = d_raw.astype(BF16)
        total += term
    gain_grad_ref[...] = total


def backward_call(bounds, limits, q, grad, turned, inv, same, other, raw, gain, cosine, sine):
    tok, width = q.shape
    wide = width // HALF * tok
    work = same.size // same.shape[3] * 2 * wide
    return pl.pallas_call(
        backward_kernel,
        in_specs=[SMEM] + vmem(11),
        out_specs=vmem(4),
        out_shape=[
            jax.ShapeDtypeStruct((tok, width), BF16),
            jax.ShapeDtypeStruct((1, LANES), F32),
            jax.ShapeDtypeStruct(same.shape, BF16),
            jax.ShapeDtypeStruct(other.shape, BF16),
        ],
        scratch_shapes=[
            pltpu.VMEM((HALF, wide), BF16),
            pltpu.VMEM((wide, HALF), BF16),
            pltpu.VMEM((HALF, wide), BF16),
            pltpu.VMEM((wide, HALF), BF16),
            pltpu.VMEM((HALF, wide), F32),
        ],
        compiler_params=pltpu.CompilerParams(vmem_limit_bytes=VMEM_LIMIT),
        cost_estimate=pl.CostEstimate(flops=10 * HALF * work, bytes_accessed=8 * same.size, transcendentals=work),
        name="attention_backward",
    )(bounds, limits, q, grad, turned, inv, same, other, raw, gain, cosine, sine)


def kv_back_kernel(raw_ref, gain_ref, flag_ref, cos_ref, sin_ref, *refs):
    *part_refs, out_ref, gain_grad_ref = refs
    total = jnp.zeros((1, LANES), F32)
    for part in range(out_ref.shape[1] // LANES):
        at = slice(part * LANES, (part + 1) * LANES)
        grad = sum(ref[:, at].astype(F32) for ref in part_refs)
        done, term = head_backward(
            grad, raw_ref[:, at], gain_ref[:, at], flag_ref[:, at], cos_ref[...], sin_ref[...]
        )
        out_ref[:, at] = done.astype(BF16)
        total += term
    gain_grad_ref[...] = total


def kv_back_call(parts, raw, gain, flag, cosine, sine):
    tok, width = raw.shape
    return pl.pallas_call(
        kv_back_kernel,
        in_specs=vmem(5 + len(parts)),
        out_specs=vmem(2),
        out_shape=[jax.ShapeDtypeStruct((tok, width), BF16), jax.ShapeDtypeStruct((1, LANES), F32)],
        compiler_params=pltpu.CompilerParams(vmem_limit_bytes=VMEM_LIMIT),
        cost_estimate=pl.CostEstimate(flops=30 * tok * width, bytes_accessed=2 * tok * width * len(parts), transcendentals=0),
        name="key_value_heads_back",
    )(raw, gain, flag, cosine, sine, *parts)


def rope_tables(positions, head_dim):
    half = head_dim // 2
    inverse = jnp.exp(jnp.arange(half, dtype=F32) * (-2.0 * math.log(10000.0) / head_dim))
    angles = positions.astype(F32)[:, None] * inverse[None, :]
    cosine, sine = jnp.cos(angles), jnp.sin(angles)
    return jnp.concatenate([cosine] * 4, axis=1), jnp.concatenate([-sine, sine, -sine, sine], axis=1)


def norm_scale(vectors):
    return lax.rsqrt(jnp.mean(vectors * vectors, axis=-1, keepdims=True) + EPSILON)


def norm_back(vectors, scaler, gains, grads_in):
    scaled = grads_in * gains
    inner_mean = jnp.mean(scaled * vectors, axis=-1, keepdims=True)
    return scaler * scaled - vectors * (scaler * scaler * scaler) * inner_mean


def backwards(array, axis, width):
    count = array.shape[axis] // width
    pieces = [lax.slice_in_dim(array, i * width, (i + 1) * width, axis=axis) for i in range(count)]
    return jnp.concatenate(pieces[::-1], axis=axis)


def body(
    tokens,
    w_query,
    key_value_weight,
    w_out,
    w_gate,
    w_up,
    w_down,
    attn_gain,
    ffn_gain,
    query_gain,
    key_gain,
    segments,
    positions,
    out_grad,
):
    tok, width = tokens.shape
    rows = lax.axis_size("row")
    row = lax.axis_index("row")
    col = lax.axis_index("col")
    cols = lax.axis_size("col")
    w_rows = w_query.shape[0]
    q_width = w_query.shape[1]
    kv_half = key_value_weight.shape[1] // 2
    ff_cols = w_gate.shape[1]
    ff = ff_cols // MEMBERS
    seq_len = min(SEQ_MAX, tok * rows)
    span = seq_len // tok
    half = tok // 2

    w_packed = pack_call(col, w_query, key_value_weight, w_out)
    head_cols = w_packed.shape[1] - q_width
    w_all = lax.all_gather(w_packed, "row", axis=0, tiled=True)
    w_o_all = w_all[:, head_cols:]
    og_low = lax.dynamic_slice_in_dim(out_grad, col * half, half, 0)
    og_all = gather_cube_slowly(og_low)
    order, near_order = distances(True), distances(False)
    group = og_all.shape[0]

    w_ff = jnp.concatenate(
        [
            w_gate.reshape(w_rows, MEMBERS, ff),
            w_up.reshape(w_rows, MEMBERS, ff),
            w_down.T.reshape(w_rows, MEMBERS, ff),
        ],
        axis=2,
    ).transpose(1, 0, 2)
    w_ff = jnp.concatenate([after(w_ff, w_all)] * (rows // MEMBERS), axis=0)
    w_ff_all = lax.all_to_all(w_ff, "row", split_axis=0, concat_axis=0, tiled=True).reshape(width, 3 * ff)

    input_f = tokens.astype(F32)
    act_scale = norm_scale(input_f)
    act_low = (input_f * act_scale * attn_gain).astype(BF16)
    cosine, sine = rope_tables(positions, HALF)
    q_lanes = jnp.tile(query_gain, 2)[None, :]
    k_lanes = jnp.tile(key_gain, 2)[None, :]
    kv_flag = jnp.concatenate([jnp.ones((1, 3 * HALF), F32), jnp.zeros((1, 3 * HALF), F32)], axis=1)
    kv_gain = jnp.where(kv_flag > 0, jnp.tile(k_lanes, (1, 3)), 1.0)
    q_flag = jnp.ones((1, q_width), F32)
    q_gain = jnp.tile(q_lanes * SCALE, (1, q_width // LANES))
    act_blocks = reorder_columns(act_low, order)
    gain = jnp.concatenate([q_gain, kv_gain], axis=1)
    flag = jnp.concatenate([q_flag, kv_flag], axis=1)
    act_low, og_all = lax.optimization_barrier((act_low, og_all))
    raw, heads = heads_call(act_low, w_all, gain, flag, cosine, sine)
    query, kv_low = heads[:, :q_width], heads[:, q_width:]
    q_raw, kv_raw = raw[:, :q_width], raw[:, q_width:]
    same_kv, other_kv = gather_earlier(kv_low, span)

    in_span = row % span
    seq_segments = lax.dynamic_slice_in_dim(segments, (row - in_span) * tok, seq_len, 0)
    own_segments = lax.dynamic_slice_in_dim(segments, row * tok, tok, 0)
    own_index = in_span * tok + jnp.arange(tok, dtype=jnp.int32)
    index = jnp.arange(seq_len, dtype=jnp.int32)
    start = jnp.min(jnp.where(seq_segments[None, :] == own_segments[:, None], index[None, :], seq_len), axis=1)
    start = jnp.where(own_segments < 0, own_index, start)
    limits = jnp.stack([start, own_index])
    bounds = jnp.stack([2 * (in_span // 4 + 1 - jnp.min(start) // (4 * tok)), in_span])
    attn_low, turned, inv = forward_call(bounds, limits, query, same_kv, other_kv)
    attn_part = dot(attn_low, w_o_all, ((1,), (1,))).astype(BF16)

    def mine(array, which):
        return lax.dynamic_slice_in_dim(array, which * half, half, 0)

    arrived = swap_col(mine(attn_part, 1 - col))
    hidden = mine(input_f, col) + (mine(attn_part, col).astype(F32) + arrived.astype(F32))

    ffn_scale = norm_scale(hidden)
    ffn_low = (hidden * ffn_scale * ffn_gain).astype(BF16)
    ffn_all = jnp.concatenate(gather_cube(ffn_low), axis=0)
    gate_up = dot(ffn_all, w_ff_all[:, : 2 * ff])
    gate_pre, up_pre = gate_up[:, :ff], gate_up[:, ff:]
    d_inner = dot(og_all, w_ff_all[:, 2 * ff :])
    sigma = jax.nn.sigmoid(gate_pre)
    silu_gate = gate_pre * sigma
    inner_low = (silu_gate * up_pre).astype(BF16)
    d_gate = d_inner * up_pre * (sigma * (1.0 + gate_pre * (1.0 - sigma)))
    d_up = d_inner * silu_gate
    d_gate_up = jnp.concatenate([d_gate, d_up], axis=1).astype(BF16)

    w_gate_up = w_ff_all[:, : 2 * ff]
    away = dot(d_gate_up[group // 2 :], w_gate_up, ((1,), (1,))).astype(BF16)
    here = dot(d_gate_up[: group // 2], w_gate_up, ((1,), (1,)))
    total = (here + swap_core(away).astype(F32)).astype(BF16).reshape(2, 2, 2, half, width)

    left, right = total[..., : width // 2], total[..., width // 2 :]
    left = halve(left, 0, 1)
    right = halve(right, 1, cols)
    grads_ff = jnp.concatenate(
        [dot(ffn_all, d_gate_up, ((0,), (0,))), dot(og_all, inner_low, ((0,), (0,)))], axis=1
    ).astype(BF16)
    left, right, grads_low = lax.optimization_barrier((left, right, grads_ff))
    grads_ff = lax.psum_scatter(
        grads_low, "row", scatter_dimension=0, tiled=True, axis_index_groups=across_groups()
    )
    left = halve(left, 0, cols)
    right = halve(right, 1, 2 * cols)
    w_down_all = w_ff_all[:, 2 * ff :]
    inner_low = after(inner_low, grads_low)
    away = dot(inner_low[group // 2 :], w_down_all, ((1,), (1,))).astype(BF16)
    here = dot(inner_low[: group // 2], w_down_all, ((1,), (1,)))
    ffn_out = over_core(here, away).reshape(2, 2, 2, half, width)
    left = halve(left, 0, 2 * cols)
    right = halve(right, 0, 1)
    ffn_back = jnp.concatenate([left, right], axis=1)
    d_hidden = og_low.astype(F32) + norm_back(hidden, ffn_scale, ffn_gain, ffn_back)
    d_hidden_half = d_hidden.astype(BF16)
    d_hidden_low = halves(d_hidden_half, swap_col(d_hidden_half), col)

    d_attn = dot(d_hidden_low, w_o_all).astype(BF16)
    d_q, q_gain_part, same_d, other_d = backward_call(
        bounds, limits, query, d_attn, turned, inv, same_kv, other_kv, q_raw, q_lanes, cosine, sine
    )
    d_kv_total = over_core(same_d, other_d).reshape(-1, tok, same_d.shape[3])

    ffn_out = halve(after(ffn_out, d_hidden_low), 0, 1)

    def partial_grad(left, right):
        return dot(left, right, ((0,), (0,))).reshape(rows, w_rows, -1)

    def over_core_only(left, right):
        partial = partial_grad(left, right)
        return over_core(partial[: rows // 2], partial[rows // 2 :])

    grad_o = over_near(over_core_only(reorder_columns(d_hidden_low, near_order), attn_low))
    act_near, d_q_late = after_all((reorder_columns(act_low, near_order), d_q), d_kv_total)
    grad_q = over_core_only(act_near, d_q_late)
    d_kv_total = over_near(d_kv_total)
    grad_q = over_near(after(grad_q, d_kv_total))
    kv_parts = over_far(d_kv_total, span, False, False)
    *kv_parts, ffn_out = lax.optimization_barrier((*kv_parts, ffn_out))
    grad_oq = jnp.concatenate([grad_o, grad_q], axis=2)
    grad_oq = lax.psum_scatter(
        grad_oq, "row", scatter_dimension=0, tiled=True, axis_index_groups=far_groups()
    )[0].astype(F32)
    grad_o, grad_q = grad_oq[:, :q_width].T, grad_oq[:, q_width:]
    d_kv, k_gain_part = kv_back_call(kv_parts, kv_raw, kv_gain, kv_flag, cosine, sine)
    d_one = jnp.concatenate([d_q, d_kv], axis=1)

    per_row = HALF // rows
    fold = lambda part: (part[0, :HALF] + part[0, HALF:]).reshape(rows, 1, per_row)
    small = jnp.concatenate([fold(q_gain_part), fold(k_gain_part)], axis=2)
    small = jnp.take(small, order, axis=0)
    small = jnp.pad(small, ((0, 0), (0, 15), (0, d_kv.shape[1] - 2 * per_row)))
    kv_partial = jnp.concatenate([partial_grad(act_blocks, d_kv), small], axis=1)
    kv_partial = over_core(kv_partial[: rows // 2], kv_partial[rows // 2 :])
    d_one = after(d_one, kv_partial)
    kv_partial = over_near(kv_partial)
    grads_ff = exchange_group(after(grads_ff, kv_partial).reshape(MEMBERS, w_rows, 3 * ff))
    for number in (cols, 2 * cols):
        ffn_out = halve(ffn_out, 0, number)
    out_half = (hidden + ffn_out).astype(BF16)
    output = halves(out_half, swap_col(out_half), col)
    grad_kv = add_up(over_far(kv_partial, rows, True, True))
    grad_kv, grads_ff = lax.optimization_barrier((grad_kv, grads_ff))
    act_back = dot(d_one, w_all[:, :head_cols], ((1,), (1,))).astype(BF16)
    act_back = act_back.astype(F32) + swap_col(act_back).astype(F32)
    input_grad = d_hidden_low.astype(F32) + norm_back(input_f, act_scale, attn_gain, act_back)
    grad_kv, small = grad_kv[:w_rows], grad_kv[w_rows, : 2 * per_row]
    grad_query = jnp.where(col == 0, grad_q, backwards(grad_q, 1, LANES))
    grad_out = jnp.where(col == 0, grad_o, backwards(grad_o, 0, LANES))

    kv_own = grad_kv.astype(BF16)
    kv_away = swap_col(kv_own)
    kv_first = jnp.where(col == 0, kv_own, kv_away).astype(F32)
    kv_last = jnp.where(col == 0, kv_away, kv_own).astype(F32)

    def one_head(array, at):
        return array[:, at : at + HALF]

    pieces = []
    for at in (K_AT, V_AT):
        pieces += [one_head(kv_first, at[0]), one_head(kv_first, at[1])]
        pieces += [one_head(kv_first, at[2]) + one_head(kv_last, at[2])]
        pieces += [one_head(kv_last, at[1]), one_head(kv_last, at[0])]
    grad_keyval = jnp.concatenate(pieces, axis=1)

    grads_ff = grads_ff.astype(F32).transpose(1, 0, 2)
    grad_gate = grads_ff[:, :, :ff].reshape(w_rows, ff_cols)
    grad_up = grads_ff[:, :, ff : 2 * ff].reshape(w_rows, ff_cols)
    grad_down = grads_ff[:, :, 2 * ff :].reshape(w_rows, ff_cols).T

    attn_part_gain = jnp.sum(
        jnp.concatenate([grad_q, grad_kv], axis=1) * w_packed[:, :head_cols].astype(F32), axis=1
    )
    ffn_part_gain = jnp.sum(grad_gate * w_gate.astype(F32) + grad_up * w_up.astype(F32), axis=1)
    gains = jnp.concatenate([attn_part_gain, ffn_part_gain, small])
    gains = gains + swap_col(gains)
    own_gains = lambda whole: lax.dynamic_slice_in_dim(whole, row * w_rows, w_rows, 0)
    grad_attn_gain = gains[:w_rows] / own_gains(attn_gain)
    grad_ffn_gain = gains[w_rows : 2 * w_rows] / own_gains(ffn_gain)
    grad_query_gain = gains[2 * w_rows : 2 * w_rows + per_row]
    grad_key_gain = gains[2 * w_rows + per_row :]
    return (
        output,
        input_grad,
        grad_query,
        grad_keyval,
        grad_out,
        grad_gate,
        grad_up,
        grad_down,
        grad_attn_gain,
        grad_ffn_gain,
        grad_query_gain,
        grad_key_gain,
    )


def solution(mesh):
    placed = (
        P("row", None),
        P("row", "col"),
        P("row", None),
        P("col", "row"),
        P("row", "col"),
        P("row", "col"),
        P("col", "row"),
        P(),
        P(),
        P(),
        P(),
        P(),
        P("row"),
        P("row", None),
    )
    return jax.shard_map(
        body,
        mesh=mesh,
        in_specs=placed,
        out_specs=(
            P("row", None),
            P("row", None),
            P("row", "col"),
            P("row", None),
            P("col", "row"),
            P("row", "col"),
            P("row", "col"),
            P("col", "row"),
            P("row"),
            P("row"),
            P("row"),
            P("row"),
        ),
        check_vma=False,
    )
```

```python
import math

import jax
import jax.numpy as jnp
from jax import lax
from jax.experimental import pallas as pl
from jax.experimental.pallas import tpu as pltpu
from jax.sharding import PartitionSpec as P

EPSILON = 1e-06
SCALE = 0.125
SEQ_MAX = 4096
MEMBERS = 8
LANES = 128
HALF = 64
F32 = jnp.float32
BF16 = jnp.bfloat16
VMEM_LIMIT = 56 * 1024 * 1024


def dot(a, b, dims=((1,), (0,))):
    return lax.dot_general(a, b, (dims, ((), ())), preferred_element_type=F32)


def swap_core(block):
    rows = lax.axis_size("row")
    return lax.ppermute(block, "row", [(i, i ^ 1) for i in range(rows)])


def swap_col(block):
    return lax.ppermute(block, "col", [(0, 1), (1, 0)])


def shift_far(block, steps, span, wrap):
    rows = lax.axis_size("row")
    route = []
    for i in range(rows):
        first, at = i // span * span, i % span + 4 * steps
        if wrap or 0 <= at < span:
            route.append((i, first + at % span))
    return lax.ppermute(block, "row", route)


def swap_near(block):
    rows = lax.axis_size("row")
    return lax.ppermute(block, "row", [(i, i ^ 2) for i in range(rows)])


def swap_cube(block, number):
    rows, cols = lax.axis_size("row"), lax.axis_size("col")
    route = []
    for i in range(rows):
        first, chip, core = i // MEMBERS * MEMBERS, i % MEMBERS // 2, i % 2
        there = first + 2 * (chip ^ (number // cols)) + core
        route += [(i * cols + c, there * cols + (c ^ (number % cols))) for c in range(cols)]
    return lax.ppermute(block, ("row", "col"), route)


def gather_earlier(block, span):
    far = jnp.stack([block] + [shift_far(block, k, span, False) for k in range(1, span // 4)])
    same = jnp.stack([far, swap_near(far)])
    return same, swap_core(same)


def add_low(one, two):
    return (one.astype(F32) + two.astype(F32)).astype(BF16)


def over_core(same, other):
    return (same.astype(F32) + swap_core(other.astype(BF16)).astype(F32)).astype(BF16)


def over_near(total):
    count = total.shape[0] // 2
    return (total[:count].astype(F32) + swap_near(total[count:]).astype(F32)).astype(BF16)


def over_far(total, span, wrap, forward):
    sign = 1 if forward else -1
    return [total[0]] + [shift_far(total[k], sign * k, span, wrap) for k in range(1, span // 4)]


def add_up(parts):
    return sum(p.astype(F32) for p in parts)


def gather_rows(block):
    rows = lax.axis_size("row")
    far = jnp.concatenate([block] + [shift_far(block, -k, rows, True) for k in range(1, rows // 4)], axis=0)
    same = jnp.concatenate([far, swap_near(far)], axis=0)
    return jnp.concatenate([same, swap_core(same)], axis=0)


def distances(far):
    rows, row = lax.axis_size("row"), lax.axis_index("row")
    order = [
        ((row ^ near) + 4 * k) % rows if far else (row ^ near) % 4 + 4 * k for near in (0, 2, 1, 3) for k in range(rows // 4)
    ]
    return jnp.stack(order)


def after_all(arrays, *others):
    return lax.optimization_barrier(tuple(arrays) + others)[: len(arrays)]


def beside(operands, send, inputs, work):
    operands, inputs = lax.optimization_barrier((operands, inputs))
    return lax.optimization_barrier((send(*operands), work(*inputs)))


def after(array, *others):
    return after_all((array,), *others)[0]


def cube_numbers():
    cols = lax.axis_size("col")
    return [(2 * pair + near) * cols + c for c in range(cols) for near in range(2) for pair in range(2)]


def gather_cube(block):
    same = jnp.concatenate([block] + [swap_cube(block, e) for e in cube_numbers()[1:]], axis=0)
    return same, swap_core(same)


def gather_cube_slowly(block):
    cols = lax.axis_size("col")
    block = jnp.concatenate([block, swap_cube(block, 2 * cols)], axis=0)
    block = jnp.concatenate([block, swap_cube(block, cols)], axis=0)
    block = jnp.concatenate([block, swap_cube(block, 1)], axis=0)
    return jnp.concatenate([block, swap_core(block)], axis=0)


def halve(total, axis, number):
    here, away = (lax.index_in_dim(total, i, axis, keepdims=False) for i in range(2))
    return here.astype(F32) + swap_cube(away.astype(BF16), number).astype(F32)


def far_groups():
    rows = lax.axis_size("row")
    return [list(range(near, rows, 4)) for near in range(4)]


def pick(array, place, axis):
    first = lax.index_in_dim(array, 0, axis, keepdims=False)
    second = lax.index_in_dim(array, 1, axis, keepdims=False)
    return jnp.where(place == 0, first, second), jnp.where(place == 0, second, first)


def group_rows():
    rows = lax.axis_size("row")
    return [list(range(first, first + MEMBERS)) for first in range(0, rows, MEMBERS)]


def across_groups():
    rows = lax.axis_size("row")
    return [list(range(member, rows, MEMBERS)) for member in range(MEMBERS)]


def exchange_group(blocks):
    return lax.all_to_all(
        blocks, "row", split_axis=0, concat_axis=0, tiled=True, axis_index_groups=group_rows()
    )


def halves(own, other, col):
    low = jnp.where(col == 0, own, other)
    high = jnp.where(col == 0, other, own)
    return jnp.concatenate([low, high], axis=0)


def partner(v):
    lane = lax.broadcasted_iota(jnp.int32, v.shape, 1)
    ahead = pltpu.roll(v, LANES - HALF // 2, 1)
    behind = pltpu.roll(v, HALF // 2, 1)
    return jnp.where(lane % HALF < HALF // 2, ahead, behind)


def head_mean(v):
    lane = lax.broadcasted_iota(jnp.int32, v.shape, 1)
    first = jnp.sum(jnp.where(lane < HALF, v, 0.0), axis=1, keepdims=True)
    second = jnp.sum(jnp.where(lane < HALF, 0.0, v), axis=1, keepdims=True)
    return jnp.where(lane < HALF, first, second) * (1.0 / HALF)


def head_forward(raw, gain, flag, cosine, sine):
    scaler = jnp.where(flag > 0, lax.rsqrt(head_mean(raw * raw) + EPSILON), 1.0)
    normed = raw * scaler * gain
    cosine = jnp.where(flag > 0, cosine, 1.0)
    sine = jnp.where(flag > 0, sine, 0.0)
    return normed * cosine + partner(normed) * sine


def head_backward(grad, raw, gain, flag, cosine, sine):
    on = flag > 0
    scaler = lax.rsqrt(head_mean(raw * raw) + EPSILON)
    back = grad * cosine - partner(grad) * sine
    scaled = back * gain
    inner = head_mean(scaled * raw)
    grad_raw = scaler * scaled - raw * (scaler * scaler * scaler) * inner
    gain_term = jnp.sum(jnp.where(on, back * raw * scaler, 0.0), axis=0, keepdims=True)
    return jnp.where(on, grad_raw, grad), gain_term


def heads_kernel(act_ref, w_ref, gain_ref, flag_ref, cos_ref, sin_ref, raw_ref, out_ref, kv_ref):
    raw = dot(act_ref[...], w_ref[...])
    raw_ref[...] = raw
    parts = raw.shape[1] // LANES
    query_parts = pl.num_programs(0) * parts - kv_ref.shape[1] // LANES
    for part in range(parts):
        at = slice(part * LANES, (part + 1) * LANES)
        done = head_forward(raw[:, at], gain_ref[:, at], flag_ref[:, at], cos_ref[...], sin_ref[...]).astype(BF16)
        out_ref[:, at] = done
        place = pl.program_id(0) * parts + part - query_parts

        @pl.when(place >= 0)
        def keep():
            kv_ref[:, pl.ds(pl.multiple_of(jnp.maximum(place, 0) * LANES, LANES), LANES)] = done


def heads_call(act, w_all, gain, flag, cosine, sine, kv_width):
    tok, width = act.shape
    cols = gain.shape[1]
    block = 256
    whole = lambda shape: pl.BlockSpec(shape, lambda i: (0, 0))
    chunk = lambda rows: pl.BlockSpec((rows, block), lambda i: (0, i))
    return pl.pallas_call(
        heads_kernel,
        grid=(cols // block,),
        in_specs=[whole((tok, width)), chunk(width), chunk(1), chunk(1), whole((tok, LANES)), whole((tok, LANES))],
        out_specs=[chunk(tok), chunk(tok), whole((tok, kv_width))],
        out_shape=[
            jax.ShapeDtypeStruct((tok, cols), F32),
            jax.ShapeDtypeStruct((tok, cols), BF16),
            jax.ShapeDtypeStruct((tok, kv_width), BF16),
        ],
        compiler_params=pltpu.CompilerParams(vmem_limit_bytes=VMEM_LIMIT),
        cost_estimate=pl.CostEstimate(flops=2 * tok * width * cols, bytes_accessed=2 * width * cols, transcendentals=0),
        name="project_heads",
    )(act, w_all, gain, flag, cosine, sine)


def pack_kernel(col_ref, q_ref, kv_ref, o_ref, out_ref):
    first = col_ref[0] == 0
    pairs = q_ref.shape[1] // LANES
    half = kv_ref.shape[1] // 2
    heads = half // HALF

    def head(number, offset):
        one = kv_ref[:, offset + number * HALF : offset + (number + 1) * HALF]
        two = kv_ref[:, offset + (heads - 1 - number) * HALF : offset + (heads - number) * HALF]
        return jnp.where(first, one, two)

    for pair in range(pairs):
        here = slice(pair * LANES, (pair + 1) * LANES)
        there = slice((pairs - 1 - pair) * LANES, (pairs - pair) * LANES)
        out_ref[:, here] = jnp.where(first, q_ref[:, here], q_ref[:, there])
        turned = jnp.where(first, o_ref[here, :].astype(F32), o_ref[there, :].astype(F32)).T
        at = q_ref.shape[1] + 6 * HALF + pair * LANES
        out_ref[:, at : at + LANES] = turned.astype(BF16)
    at = q_ref.shape[1]
    for one, two in ((head(0, 0), head(1, 0)), (head(2, 0), head(2, half)), (head(0, half), head(1, half))):
        out_ref[:, at : at + LANES] = jnp.concatenate([one, two], axis=1)
        at += LANES


def pack_call(col, w_query, w_kv, w_out):
    lines, width = w_query.shape
    return pl.pallas_call(
        pack_kernel,
        in_specs=[pl.BlockSpec(memory_space=pltpu.SMEM)] + [pl.BlockSpec(memory_space=pltpu.VMEM)] * 3,
        out_specs=pl.BlockSpec(memory_space=pltpu.VMEM),
        out_shape=jax.ShapeDtypeStruct((lines, 2 * width + 6 * HALF), BF16),
        cost_estimate=pl.CostEstimate(flops=0, bytes_accessed=10 * w_query.size, transcendentals=0),
        name="pack_weights",
    )(col.reshape(1), w_query, w_kv, w_out)


BESIDE = pl.CostEstimate(flops=0, bytes_accessed=0, transcendentals=0)


def turn(block):
    return block.astype(F32).T.astype(BF16)


def rows_kernel(order_ref, left_ref, right_ref, *refs):
    *more, own_ref, away_ref = refs
    count = own_ref.shape[0]
    for at in range(2 * count):
        to, place = (own_ref, at) if at < count else (away_ref, at - count)
        row = order_ref[at]
        block = turn(left_ref[:, pl.ds(pl.multiple_of(row * LANES, LANES), LANES)])
        to[place, :LANES] = dot(block, right_ref[...]).astype(BF16)
        if more:
            to[place, LANES:] = more[0][row]


def rows_call(order, left, right, *more):
    count = order.shape[0] // 2
    lines = left.shape[1] // (2 * count)
    if lines != LANES:
        blocks = jnp.take(left.reshape(left.shape[0], 2 * count, lines), order, axis=1)
        product = jnp.einsum("trl,tn->rln", blocks, right, preferred_element_type=F32).astype(BF16)
        if more:
            product = jnp.concatenate([product, jnp.take(more[0], order, axis=0)], axis=1)
        return product[:count], product[count:]
    shape = (count, lines + (more[0].shape[1] if more else 0), right.shape[1])
    return pl.pallas_call(
        rows_kernel,
        in_specs=[pl.BlockSpec(memory_space=pltpu.SMEM)] + [pl.BlockSpec(memory_space=pltpu.VMEM)] * (2 + len(more)),
        out_specs=[pl.BlockSpec(memory_space=pltpu.VMEM)] * 2,
        out_shape=[jax.ShapeDtypeStruct(shape, BF16)] * 2,
        compiler_params=pltpu.CompilerParams(vmem_limit_bytes=VMEM_LIMIT),
        cost_estimate=BESIDE,
        name="weight_rows",
    )(order, left, right, *more)


def ff_grads_kernel(ffn_ref, og_ref, d_ref, inner_ref, out_ref, d_turned, inner_turned):
    @pl.when(pl.program_id(0) == 0)
    def prepare():
        d_turned[...] = turn(d_ref[...])
        inner_turned[...] = turn(inner_ref[...])

    both = d_turned.shape[0]
    gate_up = dot(d_turned[...], ffn_ref[...]).astype(BF16)
    down = dot(inner_turned[...], og_ref[...]).astype(BF16)
    for part in range(out_ref.shape[0]):
        at = slice(part * LANES, (part + 1) * LANES)
        out_ref[part, :both] = gate_up[:, at]
        out_ref[part, both:] = down[:, at]


def ff_grads_call(ffn, og, d_gate_up, inner, rows):
    tokens, width = ffn.shape
    both, ff = d_gate_up.shape[1], inner.shape[1]
    lines = width // rows
    if lines != LANES:
        products = jnp.concatenate([dot(d_gate_up, ffn, ((0,), (0,))), dot(inner, og, ((0,), (0,)))], axis=0)
        return products.astype(BF16).reshape(both + ff, rows, lines).transpose(1, 0, 2)
    parts = 2
    whole = lambda array: pl.BlockSpec(array.shape, lambda i: (0, 0))
    column = pl.BlockSpec((tokens, parts * LANES), lambda i: (0, i))
    return pl.pallas_call(
        ff_grads_kernel,
        grid=(rows // parts,),
        in_specs=[column, column, whole(d_gate_up), whole(inner)],
        out_specs=pl.BlockSpec((parts, both + ff, LANES), lambda i: (i, 0, 0)),
        out_shape=jax.ShapeDtypeStruct((rows, both + ff, LANES), BF16),
        scratch_shapes=[pltpu.VMEM((both, tokens), BF16), pltpu.VMEM((ff, tokens), BF16)],
        compiler_params=pltpu.CompilerParams(vmem_limit_bytes=VMEM_LIMIT),
        cost_estimate=BESIDE,
        name="feed_forward_weight_grads",
    )(ffn, og, d_gate_up, inner)


def ff_format_kernel(in_ref, gate_ref, up_ref, down_ref):
    members, units, lines = in_ref.shape
    ff = units // 3
    for member in range(members):
        at = slice(member * ff, (member + 1) * ff)
        gate_ref[:, at] = in_ref[member, :ff].astype(F32).T
        up_ref[:, at] = in_ref[member, ff : 2 * ff].astype(F32).T
        down_ref[at] = in_ref[member, 2 * ff :].astype(F32)


def ff_format_call(blocks):
    members, units, lines = blocks.shape
    cols = members * units // 3
    return pl.pallas_call(
        ff_format_kernel,
        in_specs=[pl.BlockSpec(memory_space=pltpu.VMEM)],
        out_specs=[pl.BlockSpec(memory_space=pltpu.VMEM)] * 3,
        out_shape=[jax.ShapeDtypeStruct(shape, F32) for shape in ((lines, cols), (lines, cols), (cols, lines))],
        compiler_params=pltpu.CompilerParams(vmem_limit_bytes=VMEM_LIMIT),
        name="feed_forward_grads",
    )(blocks)


GROUPS = ((0, 4), (4, 4), (8, 2))
K_AT = (0, 64, 128)
V_AT = (256, 320, 192)


def stack_heads(wide, tok):
    turned, tall = [], []
    for pair in range(wide.shape[1] // LANES):
        chunk = wide[:, pair * LANES : (pair + 1) * LANES]
        flat = chunk.astype(F32).T.astype(BF16)
        turned += [flat[:HALF], flat[HALF:]]
        tall += [chunk[:, :HALF], chunk[:, HALF:]]
    return jnp.concatenate(turned, axis=1), jnp.concatenate(tall, axis=0)


def key_block(i, bounds_ref, limits_ref, same_ref, other_ref):
    tok = same_ref.shape[2]
    pair, near = i // 2, i % 2
    row = (bounds_ref[1] ^ (2 * near)) - 4 * pair
    kv = jnp.concatenate([same_ref[near, pair], other_ref[near, pair]], axis=0)
    key = lax.broadcasted_iota(jnp.int32, (2 * tok, tok), 0)
    key = key + jnp.where(key < tok, row * tok, (row ^ 1) * tok - tok)
    return near, pair, kv, (key >= limits_ref[0:1, :]) & (key <= limits_ref[1:2, :])


def forward_kernel(bounds_ref, limits_ref, q_ref, same_ref, other_ref, att_ref, turned_ref, inv_ref, q_turned):
    tok = q_ref.shape[0]
    turned, tall = stack_heads(q_ref[:, : att_ref.shape[1]], tok)
    q_turned[...] = turned
    turned_ref[...] = jnp.zeros_like(turned_ref)
    inv_ref[...] = jnp.zeros_like(inv_ref)

    @pl.loop(0, bounds_ref[0])
    def step(i):
        near, pair, kv, ok = key_block(i, bounds_ref, limits_ref, same_ref, other_ref)
        for g, (first, count) in enumerate(GROUPS):
            at = slice(first * tok, (first + count) * tok)
            keys = kv[:, K_AT[g] : K_AT[g] + HALF]
            vals = kv[:, V_AT[g] : V_AT[g] + HALF]
            logit = dot(keys, q_turned[:, at])
            allowed = jnp.concatenate([ok] * count, axis=1)
            expo = jnp.where(allowed, jnp.exp(logit), 0.0)
            inv_ref[:, at] += jnp.sum(expo, axis=0, keepdims=True)
            turned_ref[:, at] += dot(vals, expo.astype(BF16), ((0,), (0,)))

    inverse = 1.0 / inv_ref[...]
    inv_ref[...] = inverse
    turned_ref[...] = turned_ref[...] * inverse
    for pair in range(att_ref.shape[1] // LANES):
        at = 2 * pair * tok
        both = jnp.concatenate([turned_ref[:, at : at + tok], turned_ref[:, at + tok : at + 2 * tok]], axis=0)
        att_ref[:, pair * LANES : (pair + 1) * LANES] = both.T.astype(BF16)


def vmem(n):
    return [pl.BlockSpec(memory_space=pltpu.VMEM)] * n


SMEM = pl.BlockSpec(memory_space=pltpu.SMEM)


def forward_call(bounds, limits, q, same, other, width):
    tok = q.shape[0]
    wide = width // HALF * tok
    work = same.size // same.shape[3] * 2 * wide
    return pl.pallas_call(
        forward_kernel,
        in_specs=[SMEM] + vmem(4),
        out_specs=vmem(3),
        out_shape=[
            jax.ShapeDtypeStruct((tok, width), BF16),
            jax.ShapeDtypeStruct((HALF, wide), F32),
            jax.ShapeDtypeStruct((1, wide), F32),
        ],
        scratch_shapes=[pltpu.VMEM((HALF, wide), BF16)],
        compiler_params=pltpu.CompilerParams(vmem_limit_bytes=VMEM_LIMIT),
        cost_estimate=pl.CostEstimate(flops=4 * HALF * work, bytes_accessed=4 * same.size, transcendentals=work),
        name="attention_forward",
    )(bounds, limits, q, same, other)


def backward_kernel(
    bounds_ref,
    limits_ref,
    q_ref,
    grad_ref,
    turned_ref,
    inv_ref,
    same_ref,
    other_ref,
    raw_ref,
    gain_ref,
    cos_ref,
    sin_ref,
    dq_ref,
    gain_grad_ref,
    same_out,
    other_out,
    q_turned,
    q_tall,
    g_turned,
    g_tall,
    dq_acc,
):
    tok = q_ref.shape[0]
    q_turned[...], q_tall[...] = stack_heads(q_ref[:, : dq_ref.shape[1]], tok)
    g_turned[...], g_tall[...] = stack_heads(grad_ref[...], tok)
    dq_acc[...] = jnp.zeros_like(dq_acc)
    same_out[...] = jnp.zeros_like(same_out)
    other_out[...] = jnp.zeros_like(other_out)
    delta = jnp.sum(g_turned[...].astype(F32) * turned_ref[...], axis=0, keepdims=True)

    @pl.loop(0, bounds_ref[0])
    def step(i):
        near, pair, kv, ok = key_block(i, bounds_ref, limits_ref, same_ref, other_ref)
        for g, (first, count) in enumerate(GROUPS):
            at = slice(first * tok, (first + count) * tok)
            keys = kv[:, K_AT[g] : K_AT[g] + HALF]
            vals = kv[:, V_AT[g] : V_AT[g] + HALF]
            allowed = jnp.concatenate([ok] * count, axis=1)
            prob = jnp.where(allowed, jnp.exp(dot(keys, q_turned[:, at])) * inv_ref[:, at], 0.0)
            d_score = (prob * (dot(vals, g_turned[:, at]) - delta[:, at])).astype(BF16)
            d_keys = dot(d_score, q_tall[at, :]).astype(BF16)
            d_vals = dot(prob.astype(BF16), g_tall[at, :]).astype(BF16)
            dq_acc[:, at] += dot(keys, d_score, ((0,), (0,)))
            same_out[near, pair, :, K_AT[g] : K_AT[g] + HALF] = d_keys[:tok]
            other_out[near, pair, :, K_AT[g] : K_AT[g] + HALF] = d_keys[tok:]
            same_out[near, pair, :, V_AT[g] : V_AT[g] + HALF] = d_vals[:tok]
            other_out[near, pair, :, V_AT[g] : V_AT[g] + HALF] = d_vals[tok:]

    total = jnp.zeros((1, LANES), F32)
    for pair in range(dq_ref.shape[1] // LANES):
        at = 2 * pair * tok
        both = jnp.concatenate([dq_acc[:, at : at + tok], dq_acc[:, at + tok : at + 2 * tok]], axis=0)
        cols = slice(pair * LANES, (pair + 1) * LANES)
        d_raw, term = head_backward(
            both.T * SCALE, raw_ref[:, cols], gain_ref[...], jnp.ones((1, LANES), F32), cos_ref[...], sin_ref[...]
        )
        dq_ref[:, cols] = d_raw.astype(BF16)
        total += term
    gain_grad_ref[...] = total


def backward_call(bounds, limits, q, grad, turned, inv, same, other, raw, gain, cosine, sine):
    tok, width = grad.shape
    wide = width // HALF * tok
    work = same.size // same.shape[3] * 2 * wide
    return pl.pallas_call(
        backward_kernel,
        in_specs=[SMEM] + vmem(11),
        out_specs=vmem(4),
        out_shape=[
            jax.ShapeDtypeStruct((tok, width), BF16),
            jax.ShapeDtypeStruct((1, LANES), F32),
            jax.ShapeDtypeStruct(same.shape, BF16),
            jax.ShapeDtypeStruct(other.shape, BF16),
        ],
        scratch_shapes=[
            pltpu.VMEM((HALF, wide), BF16),
            pltpu.VMEM((wide, HALF), BF16),
            pltpu.VMEM((HALF, wide), BF16),
            pltpu.VMEM((wide, HALF), BF16),
            pltpu.VMEM((HALF, wide), F32),
        ],
        compiler_params=pltpu.CompilerParams(vmem_limit_bytes=VMEM_LIMIT),
        cost_estimate=pl.CostEstimate(flops=10 * HALF * work, bytes_accessed=8 * same.size, transcendentals=work),
        name="attention_backward",
    )(bounds, limits, q, grad, turned, inv, same, other, raw, gain, cosine, sine)


def kv_back_kernel(raw_ref, gain_ref, flag_ref, cos_ref, sin_ref, *refs):
    *part_refs, out_ref, gain_grad_ref = refs
    skip = raw_ref.shape[1] - out_ref.shape[1]
    total = jnp.zeros((1, LANES), F32)
    for part in range(out_ref.shape[1] // LANES):
        at = slice(part * LANES, (part + 1) * LANES)
        grad = sum(ref[:, at].astype(F32) for ref in part_refs)
        done, term = head_backward(
            grad, raw_ref[:, skip + at.start : skip + at.stop], gain_ref[:, at], flag_ref[:, at], cos_ref[...], sin_ref[...]
        )
        out_ref[:, at] = done.astype(BF16)
        total += term
    gain_grad_ref[...] = total


def kv_back_call(parts, raw, gain, flag, cosine, sine):
    tok, width = parts[0].shape
    return pl.pallas_call(
        kv_back_kernel,
        in_specs=vmem(5 + len(parts)),
        out_specs=vmem(2),
        out_shape=[jax.ShapeDtypeStruct((tok, width), BF16), jax.ShapeDtypeStruct((1, LANES), F32)],
        compiler_params=pltpu.CompilerParams(vmem_limit_bytes=VMEM_LIMIT),
        cost_estimate=pl.CostEstimate(flops=30 * tok * width, bytes_accessed=2 * tok * width * len(parts), transcendentals=0),
        name="key_value_heads_back",
    )(raw, gain, flag, cosine, sine, *parts)


def rope_tables(positions, head_dim):
    half = head_dim // 2
    inverse = jnp.exp(jnp.arange(half, dtype=F32) * (-2.0 * math.log(10000.0) / head_dim))
    angles = positions.astype(F32)[:, None] * inverse[None, :]
    cosine, sine = jnp.cos(angles), jnp.sin(angles)
    return jnp.concatenate([cosine] * 4, axis=1), jnp.concatenate([-sine, sine, -sine, sine], axis=1)


def norm_scale(vectors):
    return lax.rsqrt(jnp.mean(vectors * vectors, axis=-1, keepdims=True) + EPSILON)


def norm_back(vectors, scaler, gains, grads_in):
    scaled = grads_in * gains
    inner_mean = jnp.mean(scaled * vectors, axis=-1, keepdims=True)
    return scaler * scaled - vectors * (scaler * scaler * scaler) * inner_mean


def backwards(array, axis, width):
    count = array.shape[axis] // width
    pieces = [lax.slice_in_dim(array, i * width, (i + 1) * width, axis=axis) for i in range(count)]
    return jnp.concatenate(pieces[::-1], axis=axis)


def body(
    tokens,
    w_query,
    key_value_weight,
    w_out,
    w_gate,
    w_up,
    w_down,
    attn_gain,
    ffn_gain,
    query_gain,
    key_gain,
    segments,
    positions,
    out_grad,
):
    tok, width = tokens.shape
    rows = lax.axis_size("row")
    row = lax.axis_index("row")
    col = lax.axis_index("col")
    cols = lax.axis_size("col")
    w_rows = w_query.shape[0]
    q_width = w_query.shape[1]
    kv_half = key_value_weight.shape[1] // 2
    ff_cols = w_gate.shape[1]
    ff = ff_cols // MEMBERS
    seq_len = min(SEQ_MAX, tok * rows)
    span = seq_len // tok
    half = tok // 2

    w_packed = pack_call(col, w_query, key_value_weight, w_out)
    head_cols = w_packed.shape[1] - q_width
    w_all = lax.all_gather(w_packed, "row", axis=0, tiled=True)
    w_o_all = w_all[:, head_cols:]
    og_low = lax.dynamic_slice_in_dim(out_grad, col * half, half, 0)
    og_all = gather_cube_slowly(og_low)
    order, near_order = distances(True), distances(False)
    group = og_all.shape[0]

    w_ff = jnp.concatenate(
        [
            w_gate.reshape(w_rows, MEMBERS, ff),
            w_up.reshape(w_rows, MEMBERS, ff),
            w_down.T.reshape(w_rows, MEMBERS, ff),
        ],
        axis=2,
    ).transpose(1, 0, 2)
    w_ff = jnp.concatenate([after(w_ff, w_all)] * (rows // MEMBERS), axis=0)
    w_ff_all = lax.all_to_all(w_ff, "row", split_axis=0, concat_axis=0, tiled=True).reshape(width, 3 * ff)

    input_f = tokens.astype(F32)
    act_scale = norm_scale(input_f)
    act_low = (input_f * act_scale * attn_gain).astype(BF16)
    cosine, sine = rope_tables(positions, HALF)
    q_lanes = jnp.tile(query_gain, 2)[None, :]
    k_lanes = jnp.tile(key_gain, 2)[None, :]
    kv_flag = jnp.concatenate([jnp.ones((1, 3 * HALF), F32), jnp.zeros((1, 3 * HALF), F32)], axis=1)
    kv_gain = jnp.where(kv_flag > 0, jnp.tile(k_lanes, (1, 3)), 1.0)
    q_flag = jnp.ones((1, q_width), F32)
    q_gain = jnp.tile(q_lanes * SCALE, (1, q_width // LANES))
    gain = jnp.concatenate([q_gain, kv_gain], axis=1)
    flag = jnp.concatenate([q_flag, kv_flag], axis=1)
    act_low, og_all = lax.optimization_barrier((act_low, og_all))
    raw, heads, kv_low = heads_call(act_low, w_all, gain, flag, cosine, sine, head_cols - q_width)
    same_kv, other_kv = gather_earlier(kv_low, span)

    in_span = row % span
    seq_segments = lax.dynamic_slice_in_dim(segments, (row - in_span) * tok, seq_len, 0)
    own_segments = lax.dynamic_slice_in_dim(segments, row * tok, tok, 0)
    own_index = in_span * tok + jnp.arange(tok, dtype=jnp.int32)
    index = jnp.arange(seq_len, dtype=jnp.int32)
    start = jnp.min(jnp.where(seq_segments[None, :] == own_segments[:, None], index[None, :], seq_len), axis=1)
    start = jnp.where(own_segments < 0, own_index, start)
    limits = jnp.stack([start, own_index])
    bounds = jnp.stack([2 * (in_span // 4 + 1 - jnp.min(start) // (4 * tok)), in_span])
    attn_low, turned, inv = forward_call(bounds, limits, heads, same_kv, other_kv, q_width)
    attn_part = dot(attn_low, w_o_all, ((1,), (1,))).astype(BF16)

    def mine(array, which):
        return lax.dynamic_slice_in_dim(array, which * half, half, 0)

    arrived = swap_col(mine(attn_part, 1 - col))
    hidden = mine(input_f, col) + (mine(attn_part, col).astype(F32) + arrived.astype(F32))

    ffn_scale = norm_scale(hidden)
    ffn_low = (hidden * ffn_scale * ffn_gain).astype(BF16)
    ffn_all = jnp.concatenate(gather_cube(ffn_low), axis=0)
    gate_up = dot(ffn_all, w_ff_all[:, : 2 * ff])
    gate_pre, up_pre = gate_up[:, :ff], gate_up[:, ff:]
    d_inner = dot(og_all, w_ff_all[:, 2 * ff :])
    sigma = jax.nn.sigmoid(gate_pre)
    silu_gate = gate_pre * sigma
    inner_low = (silu_gate * up_pre).astype(BF16)
    d_gate = d_inner * up_pre * (sigma * (1.0 + gate_pre * (1.0 - sigma)))
    d_up = d_inner * silu_gate
    d_gate_up = jnp.concatenate([d_gate, d_up], axis=1).astype(BF16)

    w_gate_up = w_ff_all[:, : 2 * ff]
    away = dot(d_gate_up[group // 2 :], w_gate_up, ((1,), (1,))).astype(BF16)
    here = dot(d_gate_up[: group // 2], w_gate_up, ((1,), (1,)))
    total = (here + swap_core(away).astype(F32)).astype(BF16).reshape(2, 2, 2, half, width)

    left, right = total[..., : width // 2], total[..., width // 2 :]
    (left_away, right_away), grads_ff = beside(
        (left[1], right[:, 1]),
        lambda one, two: (swap_cube(one, 1), swap_cube(two, cols)),
        (ffn_all, og_all, d_gate_up, inner_low),
        lambda *arrays: ff_grads_call(*arrays, rows),
    )
    left, right = add_low(left[0], left_away), add_low(right[:, 0], right_away)
    grads_ff = lax.psum_scatter(
        grads_ff, "row", scatter_dimension=0, tiled=True, axis_index_groups=across_groups()
    )

    def down(inner_low):
        w_down_all = w_ff_all[:, 2 * ff :]
        away = dot(inner_low[group // 2 :], w_down_all, ((1,), (1,))).astype(BF16)
        return away, dot(inner_low[: group // 2], w_down_all, ((1,), (1,))).astype(BF16)

    (left_away, right_away), (out_away, out_here) = beside(
        (left[1], right[:, 1]),
        lambda one, two: (swap_cube(one, cols), swap_cube(two, 2 * cols)),
        (inner_low,),
        down,
    )
    left, right = add_low(left[0], left_away), add_low(right[:, 0], right_away)
    ffn_out = over_core(out_here, out_away).reshape(2, 2, 2, half, width)
    left = halve(left, 0, 2 * cols)
    right = halve(right, 0, 1)
    ffn_back = jnp.concatenate([left, right], axis=1)
    ffn_gain_part = jnp.sum(ffn_back * hidden * ffn_scale, axis=0)
    d_hidden = og_low.astype(F32) + norm_back(hidden, ffn_scale, ffn_gain, ffn_back)
    d_hidden_half = d_hidden.astype(BF16)
    d_hidden_low = halves(d_hidden_half, swap_col(d_hidden_half), col)

    d_attn = dot(d_hidden_low, w_o_all).astype(BF16)
    d_q, q_gain_part, same_d, other_d = backward_call(
        bounds, limits, heads, d_attn, turned, inv, same_kv, other_kv, raw, q_lanes, cosine, sine
    )
    d_kv_total = over_core(same_d, other_d).reshape(-1, tok, same_d.shape[3])

    ffn_out = halve(after(ffn_out, d_hidden_low), 0, 1)

    count = d_kv_total.shape[0] // 2
    (kv_away,), (grad_o, grad_q) = beside(
        (d_kv_total[count:],),
        lambda block: (swap_near(block),),
        (d_hidden_low, act_low, d_q),
        lambda hid, act, grad: (
            over_core(*rows_call(near_order, hid, attn_low)),
            over_core(*rows_call(near_order, act, grad)),
        ),
    )
    d_kv_total = add_low(d_kv_total[:count], kv_away)
    grad_o = over_near(grad_o)
    grad_q = over_near(after(grad_q, d_kv_total))
    kv_parts = over_far(d_kv_total, span, False, False)
    *kv_parts, ffn_out = lax.optimization_barrier((*kv_parts, ffn_out))
    grad_oq = jnp.concatenate([grad_o, grad_q], axis=2)
    grad_oq = lax.psum_scatter(
        grad_oq, "row", scatter_dimension=0, tiled=True, axis_index_groups=far_groups()
    )[0].astype(F32)
    grad_o, grad_q = grad_oq[:, :q_width].T, grad_oq[:, q_width:]
    d_kv, k_gain_part = kv_back_call(kv_parts, raw, kv_gain, kv_flag, cosine, sine)
    d_one = jnp.concatenate([d_q, d_kv], axis=1)

    per_row = HALF // rows
    fold = lambda part: (part[0, :HALF] + part[0, HALF:]).reshape(rows, 1, per_row)
    line = lambda values: jnp.pad(values, ((0, 0), (0, 0), (0, d_kv.shape[1] - values.shape[2])))
    small = [
        line(jnp.concatenate([fold(q_gain_part), fold(k_gain_part)], axis=2)),
        line(ffn_gain_part.reshape(rows, 1, w_rows)),
        jnp.zeros((rows, 14, d_kv.shape[1]), F32),
    ]
    small = jnp.concatenate(small, axis=1).astype(BF16)
    kv_partial = over_core(*rows_call(order, act_low, d_kv, small))
    d_one = after(d_one, kv_partial)
    kv_partial = over_near(kv_partial)
    grads_ff = exchange_group(after(grads_ff, kv_partial))
    for number in (cols, 2 * cols):
        ffn_out = halve(ffn_out, 0, number)
    out_half = (hidden + ffn_out).astype(BF16)
    output = halves(out_half, swap_col(out_half), col)
    grad_kv = add_up(over_far(kv_partial, rows, True, True))
    grad_kv, grads_ff = lax.optimization_barrier((grad_kv, grads_ff))
    act_back = dot(d_one, w_all[:, :head_cols], ((1,), (1,))).astype(BF16)
    act_back = act_back.astype(F32) + swap_col(act_back).astype(F32)
    input_grad = d_hidden_low.astype(F32) + norm_back(input_f, act_scale, attn_gain, act_back)
    grad_kv, small = grad_kv[:w_rows], grad_kv[w_rows : w_rows + 2]
    grad_query = jnp.where(col == 0, grad_q, backwards(grad_q, 1, LANES))
    grad_out = jnp.where(col == 0, grad_o, backwards(grad_o, 0, LANES))

    kv_own = grad_kv.astype(BF16)
    kv_away = swap_col(kv_own)
    kv_first = jnp.where(col == 0, kv_own, kv_away).astype(F32)
    kv_last = jnp.where(col == 0, kv_away, kv_own).astype(F32)

    def one_head(array, at):
        return array[:, at : at + HALF]

    pieces = []
    for at in (K_AT, V_AT):
        pieces += [one_head(kv_first, at[0]), one_head(kv_first, at[1])]
        pieces += [one_head(kv_first, at[2]) + one_head(kv_last, at[2])]
        pieces += [one_head(kv_last, at[1]), one_head(kv_last, at[0])]
    grad_keyval = jnp.concatenate(pieces, axis=1)

    grad_gate, grad_up, grad_down = ff_format_call(grads_ff)

    attn_part_gain = jnp.sum(
        jnp.concatenate([grad_q, grad_kv], axis=1) * w_packed[:, :head_cols].astype(F32), axis=1
    )
    gains = jnp.concatenate([attn_part_gain, small[1, :w_rows], small[0, : 2 * per_row]])
    gains = gains + swap_col(gains)
    own_gains = lambda whole: lax.dynamic_slice_in_dim(whole, row * w_rows, w_rows, 0)
    grad_attn_gain = gains[:w_rows] / own_gains(attn_gain)
    grad_ffn_gain = gains[w_rows : 2 * w_rows]
    grad_query_gain = gains[2 * w_rows : 2 * w_rows + per_row]
    grad_key_gain = gains[2 * w_rows + per_row :]
    return (
        output,
        input_grad,
        grad_query,
        grad_keyval,
        grad_out,
        grad_gate,
        grad_up,
        grad_down,
        grad_attn_gain,
        grad_ffn_gain,
        grad_query_gain,
        grad_key_gain,
    )


def solution(mesh):
    placed = (
        P("row", None),
        P("row", "col"),
        P("row", None),
        P("col", "row"),
        P("row", "col"),
        P("row", "col"),
        P("col", "row"),
        P(),
        P(),
        P(),
        P(),
        P(),
        P("row"),
        P("row", None),
    )
    return jax.shard_map(
        body,
        mesh=mesh,
        in_specs=placed,
        out_specs=(
            P("row", None),
            P("row", None),
            P("row", "col"),
            P("row", None),
            P("col", "row"),
            P("row", "col"),
            P("row", "col"),
            P("col", "row"),
            P("row"),
            P("row"),
            P("row"),
            P("row"),
        ),
        check_vma=False,
    )
```

```python
import math

import jax
import jax.numpy as jnp
from jax import lax
from jax.experimental import pallas as pl
from jax.experimental.pallas import tpu as pltpu
from jax.sharding import PartitionSpec as P

EPSILON = 1e-06
SCALE = 0.125
SEQ_MAX = 4096
MEMBERS = 8
LANES = 128
HALF = 64
F32 = jnp.float32
BF16 = jnp.bfloat16
VMEM_LIMIT = 56 * 1024 * 1024


def dot(a, b, dims=((1,), (0,))):
    return lax.dot_general(a, b, (dims, ((), ())), preferred_element_type=F32)


def swap_core(block):
    rows = lax.axis_size("row")
    return lax.ppermute(block, "row", [(i, i ^ 1) for i in range(rows)])


def swap_col(block):
    return lax.ppermute(block, "col", [(0, 1), (1, 0)])


def shift_far(block, steps, span, wrap):
    rows = lax.axis_size("row")
    route = []
    for i in range(rows):
        first, at = i // span * span, i % span + 4 * steps
        if wrap or 0 <= at < span:
            route.append((i, first + at % span))
    return lax.ppermute(block, "row", route)


def swap_near(block):
    rows = lax.axis_size("row")
    return lax.ppermute(block, "row", [(i, i ^ 2) for i in range(rows)])


def swap_cube(block, number):
    rows, cols = lax.axis_size("row"), lax.axis_size("col")
    route = []
    for i in range(rows):
        first, chip, core = i // MEMBERS * MEMBERS, i % MEMBERS // 2, i % 2
        there = first + 2 * (chip ^ (number // cols)) + core
        route += [(i * cols + c, there * cols + (c ^ (number % cols))) for c in range(cols)]
    return lax.ppermute(block, ("row", "col"), route)


def gather_earlier(block, span, weights):
    far = jnp.stack([block] + [shift_far(block, k, span, False) for k in range(1, span // 4)])
    same, weights = lax.optimization_barrier((jnp.stack([far, swap_near(far)]), weights))
    return same, swap_core(same), weights


def add_low(one, two):
    return (one.astype(F32) + two.astype(F32)).astype(BF16)


def over_core(same, other):
    return (same.astype(F32) + swap_core(other.astype(BF16)).astype(F32)).astype(BF16)


def over_near(total):
    count = total.shape[0] // 2
    return (total[:count].astype(F32) + swap_near(total[count:]).astype(F32)).astype(BF16)


def over_far(total, span, wrap, forward):
    sign = 1 if forward else -1
    return [total[0]] + [shift_far(total[k], sign * k, span, wrap) for k in range(1, span // 4)]


def add_up(parts):
    return sum(p.astype(F32) for p in parts)


def gather_rows(block):
    rows = lax.axis_size("row")
    far = jnp.concatenate([block] + [shift_far(block, -k, rows, True) for k in range(1, rows // 4)], axis=0)
    same = jnp.concatenate([far, swap_near(far)], axis=0)
    return jnp.concatenate([same, swap_core(same)], axis=0)


def distances(far):
    rows, row = lax.axis_size("row"), lax.axis_index("row")
    order = [
        ((row ^ near) + 4 * k) % rows if far else (row ^ near) % 4 + 4 * k for near in (0, 2, 1, 3) for k in range(rows // 4)
    ]
    return jnp.stack(order)


def after_all(arrays, *others):
    return lax.optimization_barrier(tuple(arrays) + others)[: len(arrays)]


def beside(operands, send, inputs, work):
    operands, inputs = lax.optimization_barrier((operands, inputs))
    return lax.optimization_barrier((send(*operands), work(*inputs)))


def after(array, *others):
    return after_all((array,), *others)[0]


def gather_cube(block, weights):
    cols = lax.axis_size("col")
    both = jnp.stack([block, swap_cube(block, 1)])
    *pieces, weights = lax.optimization_barrier((*(swap_cube(both, number * cols) for number in (2, 1, 3)), weights))
    pieces = [both] + pieces
    same = jnp.concatenate([piece[c] for c in range(2) for piece in pieces], axis=0)
    return same, swap_core(same), weights


def gather_cube_slowly(block):
    cols = lax.axis_size("col")
    block = jnp.concatenate([block, swap_cube(block, 2 * cols)], axis=0)
    block = jnp.concatenate([block, swap_cube(block, cols)], axis=0)
    block = jnp.concatenate([block, swap_cube(block, 1)], axis=0)
    return jnp.concatenate([block, swap_core(block)], axis=0)


def halve(total, axis, number):
    here, away = (lax.index_in_dim(total, i, axis, keepdims=False) for i in range(2))
    return here.astype(F32) + swap_cube(away.astype(BF16), number).astype(F32)


def far_groups():
    rows = lax.axis_size("row")
    return [list(range(near, rows, 4)) for near in range(4)]


def pick(array, place, axis):
    first = lax.index_in_dim(array, 0, axis, keepdims=False)
    second = lax.index_in_dim(array, 1, axis, keepdims=False)
    return jnp.where(place == 0, first, second), jnp.where(place == 0, second, first)


def group_rows():
    rows = lax.axis_size("row")
    return [list(range(first, first + MEMBERS)) for first in range(0, rows, MEMBERS)]


def across_groups():
    rows = lax.axis_size("row")
    return [list(range(member, rows, MEMBERS)) for member in range(MEMBERS)]


def exchange_group(blocks):
    return lax.all_to_all(
        blocks, "row", split_axis=0, concat_axis=0, tiled=True, axis_index_groups=group_rows()
    )


def halves(own, other, col):
    low = jnp.where(col == 0, own, other)
    high = jnp.where(col == 0, other, own)
    return jnp.concatenate([low, high], axis=0)


def partner(v):
    lane = lax.broadcasted_iota(jnp.int32, v.shape, 1)
    ahead = pltpu.roll(v, LANES - HALF // 2, 1)
    behind = pltpu.roll(v, HALF // 2, 1)
    return jnp.where(lane % HALF < HALF // 2, ahead, behind)


def head_mean(v):
    lane = lax.broadcasted_iota(jnp.int32, v.shape, 1)
    first = jnp.sum(jnp.where(lane < HALF, v, 0.0), axis=1, keepdims=True)
    second = jnp.sum(jnp.where(lane < HALF, 0.0, v), axis=1, keepdims=True)
    return jnp.where(lane < HALF, first, second) * (1.0 / HALF)


def head_forward(raw, gain, flag, cosine, sine):
    scaler = jnp.where(flag > 0, lax.rsqrt(head_mean(raw * raw) + EPSILON), 1.0)
    normed = raw * scaler * gain
    cosine = jnp.where(flag > 0, cosine, 1.0)
    sine = jnp.where(flag > 0, sine, 0.0)
    return normed * cosine + partner(normed) * sine


def head_backward(grad, raw, gain, flag, cosine, sine):
    on = flag > 0
    scaler = lax.rsqrt(head_mean(raw * raw) + EPSILON)
    back = grad * cosine - partner(grad) * sine
    scaled = back * gain
    inner = head_mean(scaled * raw)
    grad_raw = scaler * scaled - raw * (scaler * scaler * scaler) * inner
    gain_term = jnp.sum(jnp.where(on, back * raw * scaler, 0.0), axis=0, keepdims=True)
    return jnp.where(on, grad_raw, grad), gain_term


def heads_kernel(act_ref, w_ref, gain_ref, flag_ref, cos_ref, sin_ref, raw_ref, out_ref, kv_ref):
    raw = dot(act_ref[...], w_ref[...])
    raw_ref[...] = raw
    parts = raw.shape[1] // LANES
    query_parts = pl.num_programs(0) * parts - kv_ref.shape[1] // LANES
    for part in range(parts):
        at = slice(part * LANES, (part + 1) * LANES)
        done = head_forward(raw[:, at], gain_ref[:, at], flag_ref[:, at], cos_ref[...], sin_ref[...]).astype(BF16)
        out_ref[:, at] = done
        place = pl.program_id(0) * parts + part - query_parts

        @pl.when(place >= 0)
        def keep():
            kv_ref[:, pl.ds(pl.multiple_of(jnp.maximum(place, 0) * LANES, LANES), LANES)] = done


def heads_call(act, w_all, gain, flag, cosine, sine, kv_width):
    tok, width = act.shape
    cols = gain.shape[1]
    block = 256
    whole = lambda shape: pl.BlockSpec(shape, lambda i: (0, 0))
    chunk = lambda rows: pl.BlockSpec((rows, block), lambda i: (0, i))
    return pl.pallas_call(
        heads_kernel,
        grid=(cols // block,),
        in_specs=[whole((tok, width)), chunk(width), chunk(1), chunk(1), whole((tok, LANES)), whole((tok, LANES))],
        out_specs=[chunk(tok), chunk(tok), whole((tok, kv_width))],
        out_shape=[
            jax.ShapeDtypeStruct((tok, cols), F32),
            jax.ShapeDtypeStruct((tok, cols), BF16),
            jax.ShapeDtypeStruct((tok, kv_width), BF16),
        ],
        compiler_params=pltpu.CompilerParams(vmem_limit_bytes=VMEM_LIMIT),
        cost_estimate=pl.CostEstimate(flops=2 * tok * width * cols, bytes_accessed=2 * width * cols, transcendentals=0),
        name="project_heads",
    )(act, w_all, gain, flag, cosine, sine)


def pack_kernel(col_ref, q_ref, kv_ref, o_ref, out_ref):
    first = col_ref[0] == 0
    pairs = q_ref.shape[1] // LANES
    half = kv_ref.shape[1] // 2
    heads = half // HALF

    def head(number, offset):
        one = kv_ref[:, offset + number * HALF : offset + (number + 1) * HALF]
        two = kv_ref[:, offset + (heads - 1 - number) * HALF : offset + (heads - number) * HALF]
        return jnp.where(first, one, two)

    for pair in range(pairs):
        here = slice(pair * LANES, (pair + 1) * LANES)
        there = slice((pairs - 1 - pair) * LANES, (pairs - pair) * LANES)
        out_ref[:, here] = jnp.where(first, q_ref[:, here], q_ref[:, there])
        turned = jnp.where(first, o_ref[here, :].astype(F32), o_ref[there, :].astype(F32)).T
        at = q_ref.shape[1] + 6 * HALF + pair * LANES
        out_ref[:, at : at + LANES] = turned.astype(BF16)
    at = q_ref.shape[1]
    for one, two in ((head(0, 0), head(1, 0)), (head(2, 0), head(2, half)), (head(0, half), head(1, half))):
        out_ref[:, at : at + LANES] = jnp.concatenate([one, two], axis=1)
        at += LANES


def pack_call(col, w_query, w_kv, w_out):
    lines, width = w_query.shape
    return pl.pallas_call(
        pack_kernel,
        in_specs=[pl.BlockSpec(memory_space=pltpu.SMEM)] + [pl.BlockSpec(memory_space=pltpu.VMEM)] * 3,
        out_specs=pl.BlockSpec(memory_space=pltpu.VMEM),
        out_shape=jax.ShapeDtypeStruct((lines, 2 * width + 6 * HALF), BF16),
        cost_estimate=pl.CostEstimate(flops=0, bytes_accessed=10 * w_query.size, transcendentals=0),
        name="pack_weights",
    )(col.reshape(1), w_query, w_kv, w_out)


BESIDE = pl.CostEstimate(flops=0, bytes_accessed=0, transcendentals=0)


def turn(block):
    return block.astype(F32).T.astype(BF16)


def rows_kernel(order_ref, left_ref, right_ref, *refs):
    *more, own_ref, away_ref = refs
    count = own_ref.shape[0]
    for at in range(2 * count):
        to, place = (own_ref, at) if at < count else (away_ref, at - count)
        row = order_ref[at]
        block = turn(left_ref[:, pl.ds(pl.multiple_of(row * LANES, LANES), LANES)])
        to[place, :LANES] = dot(block, right_ref[...]).astype(BF16)
        if more:
            to[place, LANES:] = more[0][row]


def rows_call(order, left, right, *more):
    count = order.shape[0] // 2
    lines = left.shape[1] // (2 * count)
    if lines != LANES:
        blocks = jnp.take(left.reshape(left.shape[0], 2 * count, lines), order, axis=1)
        product = jnp.einsum("trl,tn->rln", blocks, right, preferred_element_type=F32).astype(BF16)
        if more:
            product = jnp.concatenate([product, jnp.take(more[0], order, axis=0)], axis=1)
        return product[:count], product[count:]
    shape = (count, lines + (more[0].shape[1] if more else 0), right.shape[1])
    return pl.pallas_call(
        rows_kernel,
        in_specs=[pl.BlockSpec(memory_space=pltpu.SMEM)] + [pl.BlockSpec(memory_space=pltpu.VMEM)] * (2 + len(more)),
        out_specs=[pl.BlockSpec(memory_space=pltpu.VMEM)] * 2,
        out_shape=[jax.ShapeDtypeStruct(shape, BF16)] * 2,
        compiler_params=pltpu.CompilerParams(vmem_limit_bytes=VMEM_LIMIT),
        cost_estimate=BESIDE,
        name="weight_rows",
    )(order, left, right, *more)


def ff_grads_kernel(ffn_ref, og_ref, d_ref, inner_ref, out_ref, d_turned, inner_turned):
    @pl.when(pl.program_id(0) == 0)
    def prepare():
        d_turned[...] = turn(d_ref[...])
        inner_turned[...] = turn(inner_ref[...])

    both = d_turned.shape[0]
    gate_up = dot(d_turned[...], ffn_ref[...]).astype(BF16)
    down = dot(inner_turned[...], og_ref[...]).astype(BF16)
    for part in range(out_ref.shape[0]):
        at = slice(part * LANES, (part + 1) * LANES)
        out_ref[part, :both] = gate_up[:, at]
        out_ref[part, both:] = down[:, at]


def ff_grads_call(ffn, og, d_gate_up, inner, rows):
    tokens, width = ffn.shape
    both, ff = d_gate_up.shape[1], inner.shape[1]
    lines = width // rows
    if lines != LANES:
        products = jnp.concatenate([dot(d_gate_up, ffn, ((0,), (0,))), dot(inner, og, ((0,), (0,)))], axis=0)
        return products.astype(BF16).reshape(both + ff, rows, lines).transpose(1, 0, 2)
    parts = 2
    whole = lambda array: pl.BlockSpec(array.shape, lambda i: (0, 0))
    column = pl.BlockSpec((tokens, parts * LANES), lambda i: (0, i))
    return pl.pallas_call(
        ff_grads_kernel,
        grid=(rows // parts,),
        in_specs=[column, column, whole(d_gate_up), whole(inner)],
        out_specs=pl.BlockSpec((parts, both + ff, LANES), lambda i: (i, 0, 0)),
        out_shape=jax.ShapeDtypeStruct((rows, both + ff, LANES), BF16),
        scratch_shapes=[pltpu.VMEM((both, tokens), BF16), pltpu.VMEM((ff, tokens), BF16)],
        compiler_params=pltpu.CompilerParams(vmem_limit_bytes=VMEM_LIMIT),
        cost_estimate=BESIDE,
        name="feed_forward_weight_grads",
    )(ffn, og, d_gate_up, inner)


def ff_format_kernel(in_ref, gate_ref, up_ref, down_ref):
    members, units, lines = in_ref.shape
    ff = units // 3
    for member in range(members):
        at = slice(member * ff, (member + 1) * ff)
        gate_ref[:, at] = in_ref[member, :ff].astype(F32).T
        up_ref[:, at] = in_ref[member, ff : 2 * ff].astype(F32).T
        down_ref[at] = in_ref[member, 2 * ff :].astype(F32)


def ff_format_call(blocks):
    members, units, lines = blocks.shape
    cols = members * units // 3
    return pl.pallas_call(
        ff_format_kernel,
        in_specs=[pl.BlockSpec(memory_space=pltpu.VMEM)],
        out_specs=[pl.BlockSpec(memory_space=pltpu.VMEM)] * 3,
        out_shape=[jax.ShapeDtypeStruct(shape, F32) for shape in ((lines, cols), (lines, cols), (cols, lines))],
        compiler_params=pltpu.CompilerParams(vmem_limit_bytes=VMEM_LIMIT),
        name="feed_forward_grads",
    )(blocks)


GROUPS = ((0, 4), (4, 4), (8, 2))
K_AT = (0, 64, 128)
V_AT = (256, 320, 192)


def stack_heads(wide, tok):
    turned, tall = [], []
    for pair in range(wide.shape[1] // LANES):
        chunk = wide[:, pair * LANES : (pair + 1) * LANES]
        flat = chunk.astype(F32).T.astype(BF16)
        turned += [flat[:HALF], flat[HALF:]]
        tall += [chunk[:, :HALF], chunk[:, HALF:]]
    return jnp.concatenate(turned, axis=1), jnp.concatenate(tall, axis=0)


def key_block(i, bounds_ref, limits_ref, same_ref, other_ref):
    tok = same_ref.shape[2]
    pair, near = i // 2, i % 2
    row = (bounds_ref[1] ^ (2 * near)) - 4 * pair
    kv = jnp.concatenate([same_ref[near, pair], other_ref[near, pair]], axis=0)
    key = lax.broadcasted_iota(jnp.int32, (2 * tok, tok), 0)
    key = key + jnp.where(key < tok, row * tok, (row ^ 1) * tok - tok)
    return near, pair, kv, (key >= limits_ref[0:1, :]) & (key <= limits_ref[1:2, :])


def forward_kernel(bounds_ref, limits_ref, q_ref, same_ref, other_ref, att_ref, turned_ref, inv_ref, q_turned):
    tok = q_ref.shape[0]
    turned, tall = stack_heads(q_ref[:, : att_ref.shape[1]], tok)
    q_turned[...] = turned
    turned_ref[...] = jnp.zeros_like(turned_ref)
    inv_ref[...] = jnp.zeros_like(inv_ref)

    @pl.loop(0, bounds_ref[0])
    def step(i):
        near, pair, kv, ok = key_block(i, bounds_ref, limits_ref, same_ref, other_ref)
        for g, (first, count) in enumerate(GROUPS):
            at = slice(first * tok, (first + count) * tok)
            keys = kv[:, K_AT[g] : K_AT[g] + HALF]
            vals = kv[:, V_AT[g] : V_AT[g] + HALF]
            logit = dot(keys, q_turned[:, at])
            allowed = jnp.concatenate([ok] * count, axis=1)
            expo = jnp.where(allowed, jnp.exp(logit), 0.0)
            inv_ref[:, at] += jnp.sum(expo, axis=0, keepdims=True)
            turned_ref[:, at] += dot(vals, expo.astype(BF16), ((0,), (0,)))

    inverse = 1.0 / inv_ref[...]
    inv_ref[...] = inverse
    turned_ref[...] = turned_ref[...] * inverse
    for pair in range(att_ref.shape[1] // LANES):
        at = 2 * pair * tok
        both = jnp.concatenate([turned_ref[:, at : at + tok], turned_ref[:, at + tok : at + 2 * tok]], axis=0)
        att_ref[:, pair * LANES : (pair + 1) * LANES] = both.T.astype(BF16)


def vmem(n):
    return [pl.BlockSpec(memory_space=pltpu.VMEM)] * n


SMEM = pl.BlockSpec(memory_space=pltpu.SMEM)


def forward_call(bounds, limits, q, same, other, width):
    tok = q.shape[0]
    wide = width // HALF * tok
    work = same.size // same.shape[3] * 2 * wide
    return pl.pallas_call(
        forward_kernel,
        in_specs=[SMEM] + vmem(4),
        out_specs=vmem(3),
        out_shape=[
            jax.ShapeDtypeStruct((tok, width), BF16),
            jax.ShapeDtypeStruct((HALF, wide), F32),
            jax.ShapeDtypeStruct((1, wide), F32),
        ],
        scratch_shapes=[pltpu.VMEM((HALF, wide), BF16)],
        compiler_params=pltpu.CompilerParams(vmem_limit_bytes=VMEM_LIMIT),
        cost_estimate=pl.CostEstimate(flops=4 * HALF * work, bytes_accessed=4 * same.size, transcendentals=work),
        name="attention_forward",
    )(bounds, limits, q, same, other)


def backward_kernel(
    bounds_ref,
    limits_ref,
    q_ref,
    grad_ref,
    turned_ref,
    inv_ref,
    same_ref,
    other_ref,
    raw_ref,
    gain_ref,
    cos_ref,
    sin_ref,
    dq_ref,
    gain_grad_ref,
    same_out,
    other_out,
    q_turned,
    q_tall,
    g_turned,
    g_tall,
    dq_acc,
):
    tok = q_ref.shape[0]
    q_turned[...], q_tall[...] = stack_heads(q_ref[:, : dq_ref.shape[1]], tok)
    g_turned[...], g_tall[...] = stack_heads(grad_ref[...], tok)
    dq_acc[...] = jnp.zeros_like(dq_acc)
    same_out[...] = jnp.zeros_like(same_out)
    other_out[...] = jnp.zeros_like(other_out)
    delta = jnp.sum(g_turned[...].astype(F32) * turned_ref[...], axis=0, keepdims=True)

    @pl.loop(0, bounds_ref[0])
    def step(i):
        near, pair, kv, ok = key_block(i, bounds_ref, limits_ref, same_ref, other_ref)
        for g, (first, count) in enumerate(GROUPS):
            at = slice(first * tok, (first + count) * tok)
            keys = kv[:, K_AT[g] : K_AT[g] + HALF]
            vals = kv[:, V_AT[g] : V_AT[g] + HALF]
            allowed = jnp.concatenate([ok] * count, axis=1)
            prob = jnp.where(allowed, jnp.exp(dot(keys, q_turned[:, at])) * inv_ref[:, at], 0.0)
            d_score = (prob * (dot(vals, g_turned[:, at]) - delta[:, at])).astype(BF16)
            d_keys = dot(d_score, q_tall[at, :]).astype(BF16)
            d_vals = dot(prob.astype(BF16), g_tall[at, :]).astype(BF16)
            dq_acc[:, at] += dot(keys, d_score, ((0,), (0,)))
            same_out[near, pair, :, K_AT[g] : K_AT[g] + HALF] = d_keys[:tok]
            other_out[near, pair, :, K_AT[g] : K_AT[g] + HALF] = d_keys[tok:]
            same_out[near, pair, :, V_AT[g] : V_AT[g] + HALF] = d_vals[:tok]
            other_out[near, pair, :, V_AT[g] : V_AT[g] + HALF] = d_vals[tok:]

    total = jnp.zeros((1, LANES), F32)
    for pair in range(dq_ref.shape[1] // LANES):
        at = 2 * pair * tok
        both = jnp.concatenate([dq_acc[:, at : at + tok], dq_acc[:, at + tok : at + 2 * tok]], axis=0)
        cols = slice(pair * LANES, (pair + 1) * LANES)
        d_raw, term = head_backward(
            both.T * SCALE, raw_ref[:, cols], gain_ref[...], jnp.ones((1, LANES), F32), cos_ref[...], sin_ref[...]
        )
        dq_ref[:, cols] = d_raw.astype(BF16)
        total += term
    gain_grad_ref[...] = total


def backward_call(bounds, limits, q, grad, turned, inv, same, other, raw, gain, cosine, sine):
    tok, width = grad.shape
    wide = width // HALF * tok
    work = same.size // same.shape[3] * 2 * wide
    return pl.pallas_call(
        backward_kernel,
        in_specs=[SMEM] + vmem(11),
        out_specs=vmem(4),
        out_shape=[
            jax.ShapeDtypeStruct((tok, width), BF16),
            jax.ShapeDtypeStruct((1, LANES), F32),
            jax.ShapeDtypeStruct(same.shape, BF16),
            jax.ShapeDtypeStruct(other.shape, BF16),
        ],
        scratch_shapes=[
            pltpu.VMEM((HALF, wide), BF16),
            pltpu.VMEM((wide, HALF), BF16),
            pltpu.VMEM((HALF, wide), BF16),
            pltpu.VMEM((wide, HALF), BF16),
            pltpu.VMEM((HALF, wide), F32),
        ],
        compiler_params=pltpu.CompilerParams(vmem_limit_bytes=VMEM_LIMIT),
        cost_estimate=BESIDE,
        name="attention_backward",
    )(bounds, limits, q, grad, turned, inv, same, other, raw, gain, cosine, sine)


def kv_back_kernel(raw_ref, gain_ref, flag_ref, cos_ref, sin_ref, *refs):
    *part_refs, out_ref, gain_grad_ref = refs
    skip = raw_ref.shape[1] - out_ref.shape[1]
    total = jnp.zeros((1, LANES), F32)
    for part in range(out_ref.shape[1] // LANES):
        at = slice(part * LANES, (part + 1) * LANES)
        grad = sum(ref[:, at].astype(F32) for ref in part_refs)
        done, term = head_backward(
            grad, raw_ref[:, skip + at.start : skip + at.stop], gain_ref[:, at], flag_ref[:, at], cos_ref[...], sin_ref[...]
        )
        out_ref[:, at] = done.astype(BF16)
        total += term
    gain_grad_ref[...] = total


def kv_back_call(parts, raw, gain, flag, cosine, sine):
    tok, width = parts[0].shape
    return pl.pallas_call(
        kv_back_kernel,
        in_specs=vmem(5 + len(parts)),
        out_specs=vmem(2),
        out_shape=[jax.ShapeDtypeStruct((tok, width), BF16), jax.ShapeDtypeStruct((1, LANES), F32)],
        compiler_params=pltpu.CompilerParams(vmem_limit_bytes=VMEM_LIMIT),
        cost_estimate=BESIDE,
        name="key_value_heads_back",
    )(raw, gain, flag, cosine, sine, *parts)


def rope_tables(positions, head_dim):
    half = head_dim // 2
    inverse = jnp.exp(jnp.arange(half, dtype=F32) * (-2.0 * math.log(10000.0) / head_dim))
    angles = positions.astype(F32)[:, None] * inverse[None, :]
    cosine, sine = jnp.cos(angles), jnp.sin(angles)
    return jnp.concatenate([cosine] * 4, axis=1), jnp.concatenate([-sine, sine, -sine, sine], axis=1)


def norm_scale(vectors):
    return lax.rsqrt(jnp.mean(vectors * vectors, axis=-1, keepdims=True) + EPSILON)


def norm_back(vectors, scaler, gains, grads_in):
    scaled = grads_in * gains
    inner_mean = jnp.mean(scaled * vectors, axis=-1, keepdims=True)
    return scaler * scaled - vectors * (scaler * scaler * scaler) * inner_mean


def backwards(array, axis, width):
    count = array.shape[axis] // width
    pieces = [lax.slice_in_dim(array, i * width, (i + 1) * width, axis=axis) for i in range(count)]
    return jnp.concatenate(pieces[::-1], axis=axis)


def body(
    tokens,
    w_query,
    key_value_weight,
    w_out,
    w_gate,
    w_up,
    w_down,
    attn_gain,
    ffn_gain,
    query_gain,
    key_gain,
    segments,
    positions,
    out_grad,
):
    tok, width = tokens.shape
    rows = lax.axis_size("row")
    row = lax.axis_index("row")
    col = lax.axis_index("col")
    cols = lax.axis_size("col")
    w_rows = w_query.shape[0]
    q_width = w_query.shape[1]
    kv_half = key_value_weight.shape[1] // 2
    ff_cols = w_gate.shape[1]
    ff = ff_cols // MEMBERS
    seq_len = min(SEQ_MAX, tok * rows)
    span = seq_len // tok
    half = tok // 2

    w_packed = pack_call(col, w_query, key_value_weight, w_out)
    head_cols = w_packed.shape[1] - q_width
    w_all = lax.all_gather(w_packed, "row", axis=0, tiled=True)
    w_o_all = w_all[:, head_cols:]
    og_low = lax.dynamic_slice_in_dim(out_grad, col * half, half, 0)
    og_all = gather_cube_slowly(og_low)
    order, near_order = distances(True), distances(False)
    group = og_all.shape[0]

    w_ff = jnp.concatenate(
        [
            w_gate.reshape(w_rows, MEMBERS, ff),
            w_up.reshape(w_rows, MEMBERS, ff),
            w_down.T.reshape(w_rows, MEMBERS, ff),
        ],
        axis=2,
    ).transpose(1, 0, 2)
    w_ff = jnp.concatenate([w_ff] * (rows // MEMBERS), axis=0)

    input_f = tokens.astype(F32)
    act_scale = norm_scale(input_f)
    act_low = (input_f * act_scale * attn_gain).astype(BF16)
    cosine, sine = rope_tables(positions, HALF)
    q_lanes = jnp.tile(query_gain, 2)[None, :]
    k_lanes = jnp.tile(key_gain, 2)[None, :]
    kv_flag = jnp.concatenate([jnp.ones((1, 3 * HALF), F32), jnp.zeros((1, 3 * HALF), F32)], axis=1)
    kv_gain = jnp.where(kv_flag > 0, jnp.tile(k_lanes, (1, 3)), 1.0)
    q_flag = jnp.ones((1, q_width), F32)
    q_gain = jnp.tile(q_lanes * SCALE, (1, q_width // LANES))
    gain = jnp.concatenate([q_gain, kv_gain], axis=1)
    flag = jnp.concatenate([q_flag, kv_flag], axis=1)
    act_low, og_all = lax.optimization_barrier((act_low, og_all))
    raw, heads, kv_low = heads_call(act_low, w_all, gain, flag, cosine, sine, head_cols - q_width)
    same_kv, other_kv, w_ff = gather_earlier(kv_low, span, w_ff)
    w_ff_all = lax.all_to_all(w_ff, "row", split_axis=0, concat_axis=0, tiled=True).reshape(width, 3 * ff)

    in_span = row % span
    seq_segments = lax.dynamic_slice_in_dim(segments, (row - in_span) * tok, seq_len, 0)
    own_segments = lax.dynamic_slice_in_dim(segments, row * tok, tok, 0)
    own_index = in_span * tok + jnp.arange(tok, dtype=jnp.int32)
    index = jnp.arange(seq_len, dtype=jnp.int32)
    start = jnp.min(jnp.where(seq_segments[None, :] == own_segments[:, None], index[None, :], seq_len), axis=1)
    start = jnp.where(own_segments < 0, own_index, start)
    limits = jnp.stack([start, own_index])
    bounds = jnp.stack([2 * (in_span // 4 + 1 - jnp.min(start) // (4 * tok)), in_span])
    attn_low, turned, inv = forward_call(bounds, limits, heads, same_kv, other_kv, q_width)
    attn_part = dot(attn_low, w_o_all, ((1,), (1,))).astype(BF16)

    def mine(array, which):
        return lax.dynamic_slice_in_dim(array, which * half, half, 0)

    arrived = swap_col(mine(attn_part, 1 - col))
    hidden = mine(input_f, col) + (mine(attn_part, col).astype(F32) + arrived.astype(F32))

    ffn_scale = norm_scale(hidden)
    ffn_low = (hidden * ffn_scale * ffn_gain).astype(BF16)
    ffn_same, ffn_other, w_ff_all = gather_cube(ffn_low, w_ff_all)
    ffn_all = jnp.concatenate([ffn_same, ffn_other], axis=0)
    gate_up = dot(ffn_all, w_ff_all[:, : 2 * ff])
    gate_pre, up_pre = gate_up[:, :ff], gate_up[:, ff:]
    d_inner = dot(og_all, w_ff_all[:, 2 * ff :])
    sigma = jax.nn.sigmoid(gate_pre)
    silu_gate = gate_pre * sigma
    inner_low = (silu_gate * up_pre).astype(BF16)
    d_gate = d_inner * up_pre * (sigma * (1.0 + gate_pre * (1.0 - sigma)))
    d_up = d_inner * silu_gate
    d_gate_up = jnp.concatenate([d_gate, d_up], axis=1).astype(BF16)

    w_gate_up = w_ff_all[:, : 2 * ff]
    away = dot(d_gate_up[group // 2 :], w_gate_up, ((1,), (1,))).astype(BF16)
    here = dot(d_gate_up[: group // 2], w_gate_up, ((1,), (1,)))
    total = (here + swap_core(away).astype(F32)).astype(BF16).reshape(2, 2, 2, half, width)

    left, right = total[..., : width // 2], total[..., width // 2 :]
    (left_away, right_away), grads_ff = beside(
        (left[1], right[:, 1]),
        lambda one, two: (swap_cube(one, 1), swap_cube(two, cols)),
        (ffn_all, og_all, d_gate_up, inner_low),
        lambda *arrays: ff_grads_call(*arrays, rows),
    )
    left, right = add_low(left[0], left_away), add_low(right[:, 0], right_away)
    grads_ff = lax.psum_scatter(
        grads_ff, "row", scatter_dimension=0, tiled=True, axis_index_groups=across_groups()
    )

    def down(inner_low):
        w_down_all = w_ff_all[:, 2 * ff :]
        away = dot(inner_low[group // 2 :], w_down_all, ((1,), (1,))).astype(BF16)
        return away, dot(inner_low[: group // 2], w_down_all, ((1,), (1,))).astype(BF16)

    (left_away, right_away), (out_away, out_here) = beside(
        (left[1], right[:, 1]),
        lambda one, two: (swap_cube(one, cols), swap_cube(two, 2 * cols)),
        (inner_low,),
        down,
    )
    left, right = add_low(left[0], left_away), add_low(right[:, 0], right_away)
    ffn_out = over_core(out_here, out_away).reshape(2, 2, 2, half, width)
    left = halve(left, 0, 2 * cols)
    right = halve(right, 0, 1)
    ffn_back = jnp.concatenate([left, right], axis=1)
    ffn_gain_part = jnp.sum(ffn_back * hidden * ffn_scale, axis=0)
    d_hidden = og_low.astype(F32) + norm_back(hidden, ffn_scale, ffn_gain, ffn_back)
    d_hidden_half = d_hidden.astype(BF16)
    d_hidden_low = halves(d_hidden_half, swap_col(d_hidden_half), col)

    d_attn = dot(d_hidden_low, w_o_all).astype(BF16)
    d_q, q_gain_part, same_d, other_d = backward_call(
        bounds, limits, heads, d_attn, turned, inv, same_kv, other_kv, raw, q_lanes, cosine, sine
    )
    d_kv_total = over_core(same_d, other_d).reshape(-1, tok, same_d.shape[3])

    ffn_out = halve(after(ffn_out, d_hidden_low), 0, 1)

    count = d_kv_total.shape[0] // 2
    (kv_away,), (grad_o, grad_q) = beside(
        (d_kv_total[count:],),
        lambda block: (swap_near(block),),
        (d_hidden_low, act_low, d_q),
        lambda hid, act, grad: (
            over_core(*rows_call(near_order, hid, attn_low)),
            over_core(*rows_call(near_order, act, grad)),
        ),
    )
    d_kv_total = add_low(d_kv_total[:count], kv_away)
    grad_o = over_near(grad_o)
    grad_q = over_near(after(grad_q, d_kv_total))
    kv_parts = over_far(d_kv_total, span, False, False)
    *kv_parts, ffn_out = lax.optimization_barrier((*kv_parts, ffn_out))
    grad_oq = jnp.concatenate([grad_o, grad_q], axis=2)
    grad_oq = lax.psum_scatter(
        grad_oq, "row", scatter_dimension=0, tiled=True, axis_index_groups=far_groups()
    )[0].astype(F32)
    grad_o, grad_q = grad_oq[:, :q_width].T, grad_oq[:, q_width:]
    d_kv, k_gain_part = kv_back_call(kv_parts, raw, kv_gain, kv_flag, cosine, sine)
    d_one = jnp.concatenate([d_q, d_kv], axis=1)

    per_row = HALF // rows
    fold = lambda part: (part[0, :HALF] + part[0, HALF:]).reshape(rows, 1, per_row)
    line = lambda values: jnp.pad(values, ((0, 0), (0, 0), (0, d_kv.shape[1] - values.shape[2])))
    small = [
        line(jnp.concatenate([fold(q_gain_part), fold(k_gain_part)], axis=2)),
        line(ffn_gain_part.reshape(rows, 1, w_rows)),
        jnp.zeros((rows, 14, d_kv.shape[1]), F32),
    ]
    small = jnp.concatenate(small, axis=1).astype(BF16)
    kv_partial = over_core(*rows_call(order, act_low, d_kv, small))
    d_one = after(d_one, kv_partial)
    kv_partial = over_near(kv_partial)
    grads_ff = exchange_group(after(grads_ff, kv_partial))
    ffn_out = halve(after(ffn_out, kv_partial), 0, cols)
    grad_kv, grads_ff, ffn_out = lax.optimization_barrier(
        (over_far(kv_partial, rows, True, True), grads_ff, halve(ffn_out, 0, 2 * cols))
    )
    out_half = (hidden + ffn_out).astype(BF16)
    output = halves(out_half, swap_col(out_half), col)
    grad_kv = add_up(grad_kv)
    act_back = dot(d_one, w_all[:, :head_cols], ((1,), (1,))).astype(BF16)
    act_back = act_back.astype(F32) + swap_col(act_back).astype(F32)
    input_grad = d_hidden_low.astype(F32) + norm_back(input_f, act_scale, attn_gain, act_back)
    grad_kv, small = grad_kv[:w_rows], grad_kv[w_rows : w_rows + 2]
    grad_query = jnp.where(col == 0, grad_q, backwards(grad_q, 1, LANES))
    grad_out = jnp.where(col == 0, grad_o, backwards(grad_o, 0, LANES))

    kv_own = grad_kv.astype(BF16)
    kv_away = swap_col(kv_own)
    kv_first = jnp.where(col == 0, kv_own, kv_away).astype(F32)
    kv_last = jnp.where(col == 0, kv_away, kv_own).astype(F32)

    def one_head(array, at):
        return array[:, at : at + HALF]

    pieces = []
    for at in (K_AT, V_AT):
        pieces += [one_head(kv_first, at[0]), one_head(kv_first, at[1])]
        pieces += [one_head(kv_first, at[2]) + one_head(kv_last, at[2])]
        pieces += [one_head(kv_last, at[1]), one_head(kv_last, at[0])]
    grad_keyval = jnp.concatenate(pieces, axis=1)

    grad_gate, grad_up, grad_down = ff_format_call(grads_ff)

    attn_part_gain = jnp.sum(
        jnp.concatenate([grad_q, grad_kv], axis=1) * w_packed[:, :head_cols].astype(F32), axis=1
    )
    gains = jnp.concatenate([attn_part_gain, small[1, :w_rows], small[0, : 2 * per_row]])
    gains = gains + swap_col(gains)
    own_gains = lambda whole: lax.dynamic_slice_in_dim(whole, row * w_rows, w_rows, 0)
    grad_attn_gain = gains[:w_rows] / own_gains(attn_gain)
    grad_ffn_gain = gains[w_rows : 2 * w_rows]
    grad_query_gain = gains[2 * w_rows : 2 * w_rows + per_row]
    grad_key_gain = gains[2 * w_rows + per_row :]
    return (
        output,
        input_grad,
        grad_query,
        grad_keyval,
        grad_out,
        grad_gate,
        grad_up,
        grad_down,
        grad_attn_gain,
        grad_ffn_gain,
        grad_query_gain,
        grad_key_gain,
    )


def solution(mesh):
    placed = (
        P("row", None),
        P("row", "col"),
        P("row", None),
        P("col", "row"),
        P("row", "col"),
        P("row", "col"),
        P("col", "row"),
        P(),
        P(),
        P(),
        P(),
        P(),
        P("row"),
        P("row", None),
    )
    return jax.shard_map(
        body,
        mesh=mesh,
        in_specs=placed,
        out_specs=(
            P("row", None),
            P("row", None),
            P("row", "col"),
            P("row", None),
            P("col", "row"),
            P("row", "col"),
            P("row", "col"),
            P("col", "row"),
            P("row"),
            P("row"),
            P("row"),
            P("row"),
        ),
        check_vma=False,
    )
```

```python
import math

import jax
import jax.numpy as jnp
from jax import lax
from jax.experimental import pallas as pl
from jax.experimental.pallas import tpu as pltpu
from jax.sharding import PartitionSpec as P

EPSILON = 1e-06
SCALE = 0.125
SEQ_MAX = 4096
MEMBERS = 8
LANES = 128
HALF = 64
F32 = jnp.float32
BF16 = jnp.bfloat16
VMEM_LIMIT = 56 * 1024 * 1024


def dot(a, b, dims=((1,), (0,))):
    return lax.dot_general(a, b, (dims, ((), ())), preferred_element_type=F32)


def swap_core(block):
    rows = lax.axis_size("row")
    return lax.ppermute(block, "row", [(i, i ^ 1) for i in range(rows)])


def swap_col(block):
    return lax.ppermute(block, "col", [(0, 1), (1, 0)])


def shift_far(block, steps, span, wrap):
    rows = lax.axis_size("row")
    route = []
    for i in range(rows):
        first, at = i // span * span, i % span + 4 * steps
        if wrap or 0 <= at < span:
            route.append((i, first + at % span))
    return lax.ppermute(block, "row", route)


def swap_near(block):
    rows = lax.axis_size("row")
    return lax.ppermute(block, "row", [(i, i ^ 2) for i in range(rows)])


def swap_cube(block, number):
    rows, cols = lax.axis_size("row"), lax.axis_size("col")
    route = []
    for i in range(rows):
        first, chip, core = i // MEMBERS * MEMBERS, i % MEMBERS // 2, i % 2
        there = first + 2 * (chip ^ (number // cols)) + core
        route += [(i * cols + c, there * cols + (c ^ (number % cols))) for c in range(cols)]
    return lax.ppermute(block, ("row", "col"), route)


def gather_earlier(block, span, weights):
    far = jnp.stack([block] + [shift_far(block, k, span, False) for k in range(1, span // 4)])
    far, weights = lax.optimization_barrier((far, weights))
    same = jnp.stack([far, swap_near(far)])
    return same, swap_core(same), weights


def add_low(one, two):
    return (one.astype(F32) + two.astype(F32)).astype(BF16)


def over_core(same, other):
    return (same.astype(F32) + swap_core(other.astype(BF16)).astype(F32)).astype(BF16)


def over_near(total):
    count = total.shape[0] // 2
    return (total[:count].astype(F32) + swap_near(total[count:]).astype(F32)).astype(BF16)


def over_far(total, span, wrap, forward):
    sign = 1 if forward else -1
    return [total[0]] + [shift_far(total[k], sign * k, span, wrap) for k in range(1, span // 4)]


def add_up(parts):
    return sum(p.astype(F32) for p in parts)


def gather_rows(block):
    rows = lax.axis_size("row")
    far = jnp.concatenate([block] + [shift_far(block, -k, rows, True) for k in range(1, rows // 4)], axis=0)
    same = jnp.concatenate([far, swap_near(far)], axis=0)
    return jnp.concatenate([same, swap_core(same)], axis=0)


def distances(far):
    rows, row = lax.axis_size("row"), lax.axis_index("row")
    order = [
        ((row ^ near) + 4 * k) % rows if far else (row ^ near) % 4 + 4 * k for near in (0, 2, 1, 3) for k in range(rows // 4)
    ]
    return jnp.stack(order)


def after_all(arrays, *others):
    return lax.optimization_barrier(tuple(arrays) + others)[: len(arrays)]


def beside(operands, send, inputs, work):
    operands, inputs = lax.optimization_barrier((operands, inputs))
    return lax.optimization_barrier((send(*operands), work(*inputs)))


def after(array, *others):
    return after_all((array,), *others)[0]


def gather_cube(block, weights):
    cols = lax.axis_size("col")
    both = jnp.stack([block, swap_cube(block, 1)])
    *pieces, weights = lax.optimization_barrier((*(swap_cube(both, number * cols) for number in (2, 1, 3)), weights))
    pieces = [both] + pieces
    same = jnp.concatenate([piece[c] for c in range(2) for piece in pieces], axis=0)
    return same, swap_core(same), weights


def gather_cube_slowly(block):
    cols = lax.axis_size("col")
    block = jnp.concatenate([block, swap_cube(block, 2 * cols)], axis=0)
    block = jnp.concatenate([block, swap_cube(block, cols)], axis=0)
    block = jnp.concatenate([block, swap_cube(block, 1)], axis=0)
    return jnp.concatenate([block, swap_core(block)], axis=0)


def halve(total, axis, number):
    here, away = (lax.index_in_dim(total, i, axis, keepdims=False) for i in range(2))
    return here.astype(F32) + swap_cube(away.astype(BF16), number).astype(F32)


def far_groups():
    rows = lax.axis_size("row")
    return [list(range(near, rows, 4)) for near in range(4)]


def pick(array, place, axis):
    first = lax.index_in_dim(array, 0, axis, keepdims=False)
    second = lax.index_in_dim(array, 1, axis, keepdims=False)
    return jnp.where(place == 0, first, second), jnp.where(place == 0, second, first)


def group_rows():
    rows = lax.axis_size("row")
    return [list(range(first, first + MEMBERS)) for first in range(0, rows, MEMBERS)]


def across_groups():
    rows = lax.axis_size("row")
    return [list(range(member, rows, MEMBERS)) for member in range(MEMBERS)]


def exchange_group(blocks):
    return lax.all_to_all(
        blocks, "row", split_axis=0, concat_axis=0, tiled=True, axis_index_groups=group_rows()
    )


def halves(own, other, col):
    low = jnp.where(col == 0, own, other)
    high = jnp.where(col == 0, other, own)
    return jnp.concatenate([low, high], axis=0)


def partner(v):
    lane = lax.broadcasted_iota(jnp.int32, v.shape, 1)
    ahead = pltpu.roll(v, LANES - HALF // 2, 1)
    behind = pltpu.roll(v, HALF // 2, 1)
    return jnp.where(lane % HALF < HALF // 2, ahead, behind)


def head_mean(v):
    lane = lax.broadcasted_iota(jnp.int32, v.shape, 1)
    first = jnp.sum(jnp.where(lane < HALF, v, 0.0), axis=1, keepdims=True)
    second = jnp.sum(jnp.where(lane < HALF, 0.0, v), axis=1, keepdims=True)
    return jnp.where(lane < HALF, first, second) * (1.0 / HALF)


def head_forward(raw, gain, flag, cosine, sine):
    scaler = jnp.where(flag > 0, lax.rsqrt(head_mean(raw * raw) + EPSILON), 1.0)
    normed = raw * scaler * gain
    cosine = jnp.where(flag > 0, cosine, 1.0)
    sine = jnp.where(flag > 0, sine, 0.0)
    return normed * cosine + partner(normed) * sine


def head_backward(grad, raw, gain, flag, cosine, sine):
    on = flag > 0
    scaler = lax.rsqrt(head_mean(raw * raw) + EPSILON)
    back = grad * cosine - partner(grad) * sine
    scaled = back * gain
    inner = head_mean(scaled * raw)
    grad_raw = scaler * scaled - raw * (scaler * scaler * scaler) * inner
    gain_term = jnp.sum(jnp.where(on, back * raw * scaler, 0.0), axis=0, keepdims=True)
    return jnp.where(on, grad_raw, grad), gain_term


def heads_kernel(act_ref, w_ref, gain_ref, flag_ref, cos_ref, sin_ref, raw_ref, out_ref, kv_ref):
    raw = dot(act_ref[...], w_ref[...])
    raw_ref[...] = raw
    parts = raw.shape[1] // LANES
    query_parts = pl.num_programs(0) * parts - kv_ref.shape[1] // LANES
    for part in range(parts):
        at = slice(part * LANES, (part + 1) * LANES)
        done = head_forward(raw[:, at], gain_ref[:, at], flag_ref[:, at], cos_ref[...], sin_ref[...]).astype(BF16)
        out_ref[:, at] = done
        place = pl.program_id(0) * parts + part - query_parts

        @pl.when(place >= 0)
        def keep():
            kv_ref[:, pl.ds(pl.multiple_of(jnp.maximum(place, 0) * LANES, LANES), LANES)] = done


def heads_call(act, w_all, gain, flag, cosine, sine, kv_width):
    tok, width = act.shape
    cols = gain.shape[1]
    block = 256
    whole = lambda shape: pl.BlockSpec(shape, lambda i: (0, 0))
    chunk = lambda rows: pl.BlockSpec((rows, block), lambda i: (0, i))
    return pl.pallas_call(
        heads_kernel,
        grid=(cols // block,),
        in_specs=[whole((tok, width)), chunk(width), chunk(1), chunk(1), whole((tok, LANES)), whole((tok, LANES))],
        out_specs=[chunk(tok), chunk(tok), whole((tok, kv_width))],
        out_shape=[
            jax.ShapeDtypeStruct((tok, cols), F32),
            jax.ShapeDtypeStruct((tok, cols), BF16),
            jax.ShapeDtypeStruct((tok, kv_width), BF16),
        ],
        compiler_params=pltpu.CompilerParams(vmem_limit_bytes=VMEM_LIMIT),
        cost_estimate=pl.CostEstimate(flops=2 * tok * width * cols, bytes_accessed=2 * width * cols, transcendentals=0),
        name="project_heads",
    )(act, w_all, gain, flag, cosine, sine)


def pack_kernel(col_ref, q_ref, kv_ref, o_ref, out_ref):
    first = col_ref[0] == 0
    pairs = q_ref.shape[1] // LANES
    half = kv_ref.shape[1] // 2
    heads = half // HALF

    def head(number, offset):
        one = kv_ref[:, offset + number * HALF : offset + (number + 1) * HALF]
        two = kv_ref[:, offset + (heads - 1 - number) * HALF : offset + (heads - number) * HALF]
        return jnp.where(first, one, two)

    for pair in range(pairs):
        here = slice(pair * LANES, (pair + 1) * LANES)
        there = slice((pairs - 1 - pair) * LANES, (pairs - pair) * LANES)
        out_ref[:, here] = jnp.where(first, q_ref[:, here], q_ref[:, there])
        turned = jnp.where(first, o_ref[here, :].astype(F32), o_ref[there, :].astype(F32)).T
        at = q_ref.shape[1] + 6 * HALF + pair * LANES
        out_ref[:, at : at + LANES] = turned.astype(BF16)
    at = q_ref.shape[1]
    for one, two in ((head(0, 0), head(1, 0)), (head(2, 0), head(2, half)), (head(0, half), head(1, half))):
        out_ref[:, at : at + LANES] = jnp.concatenate([one, two], axis=1)
        at += LANES


def pack_call(col, w_query, w_kv, w_out):
    lines, width = w_query.shape
    return pl.pallas_call(
        pack_kernel,
        in_specs=[pl.BlockSpec(memory_space=pltpu.SMEM)] + [pl.BlockSpec(memory_space=pltpu.VMEM)] * 3,
        out_specs=pl.BlockSpec(memory_space=pltpu.VMEM),
        out_shape=jax.ShapeDtypeStruct((lines, 2 * width + 6 * HALF), BF16),
        cost_estimate=pl.CostEstimate(flops=0, bytes_accessed=10 * w_query.size, transcendentals=0),
        name="pack_weights",
    )(col.reshape(1), w_query, w_kv, w_out)


BESIDE = pl.CostEstimate(flops=0, bytes_accessed=0, transcendentals=0)


def turn(block):
    return block.astype(F32).T.astype(BF16)


def rows_kernel(order_ref, left_ref, right_ref, *refs):
    *more, own_ref, away_ref = refs
    count = own_ref.shape[0]
    for at in range(2 * count):
        to, place = (own_ref, at) if at < count else (away_ref, at - count)
        row = order_ref[at]
        block = turn(left_ref[:, pl.ds(pl.multiple_of(row * LANES, LANES), LANES)])
        to[place, :LANES] = dot(block, right_ref[...]).astype(BF16)
        if more:
            to[place, LANES:] = more[0][row]


def rows_call(order, left, right, *more):
    count = order.shape[0] // 2
    lines = left.shape[1] // (2 * count)
    if lines != LANES:
        blocks = jnp.take(left.reshape(left.shape[0], 2 * count, lines), order, axis=1)
        product = jnp.einsum("trl,tn->rln", blocks, right, preferred_element_type=F32).astype(BF16)
        if more:
            product = jnp.concatenate([product, jnp.take(more[0], order, axis=0)], axis=1)
        return product[:count], product[count:]
    shape = (count, lines + (more[0].shape[1] if more else 0), right.shape[1])
    return pl.pallas_call(
        rows_kernel,
        in_specs=[pl.BlockSpec(memory_space=pltpu.SMEM)] + [pl.BlockSpec(memory_space=pltpu.VMEM)] * (2 + len(more)),
        out_specs=[pl.BlockSpec(memory_space=pltpu.VMEM)] * 2,
        out_shape=[jax.ShapeDtypeStruct(shape, BF16)] * 2,
        compiler_params=pltpu.CompilerParams(vmem_limit_bytes=VMEM_LIMIT),
        cost_estimate=BESIDE,
        name="weight_rows",
    )(order, left, right, *more)


def ff_grads_kernel(ffn_ref, og_ref, d_ref, inner_ref, out_ref, d_turned, inner_turned):
    @pl.when(pl.program_id(0) == 0)
    def prepare():
        d_turned[...] = turn(d_ref[...])
        inner_turned[...] = turn(inner_ref[...])

    both = d_turned.shape[0]
    gate_up = dot(d_turned[...], ffn_ref[...]).astype(BF16)
    down = dot(inner_turned[...], og_ref[...]).astype(BF16)
    for part in range(out_ref.shape[0]):
        at = slice(part * LANES, (part + 1) * LANES)
        out_ref[part, :both] = gate_up[:, at]
        out_ref[part, both:] = down[:, at]


def ff_grads_call(ffn, og, d_gate_up, inner, rows):
    tokens, width = ffn.shape
    both, ff = d_gate_up.shape[1], inner.shape[1]
    lines = width // rows
    if lines != LANES:
        products = jnp.concatenate([dot(d_gate_up, ffn, ((0,), (0,))), dot(inner, og, ((0,), (0,)))], axis=0)
        return products.astype(BF16).reshape(both + ff, rows, lines).transpose(1, 0, 2)
    parts = 2
    whole = lambda array: pl.BlockSpec(array.shape, lambda i: (0, 0))
    column = pl.BlockSpec((tokens, parts * LANES), lambda i: (0, i))
    return pl.pallas_call(
        ff_grads_kernel,
        grid=(rows // parts,),
        in_specs=[column, column, whole(d_gate_up), whole(inner)],
        out_specs=pl.BlockSpec((parts, both + ff, LANES), lambda i: (i, 0, 0)),
        out_shape=jax.ShapeDtypeStruct((rows, both + ff, LANES), BF16),
        scratch_shapes=[pltpu.VMEM((both, tokens), BF16), pltpu.VMEM((ff, tokens), BF16)],
        compiler_params=pltpu.CompilerParams(vmem_limit_bytes=VMEM_LIMIT),
        cost_estimate=BESIDE,
        name="feed_forward_weight_grads",
    )(ffn, og, d_gate_up, inner)


def ff_format_kernel(in_ref, gate_ref, up_ref, down_ref):
    members, units, lines = in_ref.shape
    ff = units // 3
    for member in range(members):
        at = slice(member * ff, (member + 1) * ff)
        gate_ref[:, at] = in_ref[member, :ff].astype(F32).T
        up_ref[:, at] = in_ref[member, ff : 2 * ff].astype(F32).T
        down_ref[at] = in_ref[member, 2 * ff :].astype(F32)


def ff_format_call(blocks):
    members, units, lines = blocks.shape
    cols = members * units // 3
    return pl.pallas_call(
        ff_format_kernel,
        in_specs=[pl.BlockSpec(memory_space=pltpu.VMEM)],
        out_specs=[pl.BlockSpec(memory_space=pltpu.VMEM)] * 3,
        out_shape=[jax.ShapeDtypeStruct(shape, F32) for shape in ((lines, cols), (lines, cols), (cols, lines))],
        compiler_params=pltpu.CompilerParams(vmem_limit_bytes=VMEM_LIMIT),
        name="feed_forward_grads",
    )(blocks)


GROUPS = ((0, 4), (4, 4), (8, 2))
K_AT = (0, 64, 128)
V_AT = (256, 320, 192)


def stack_heads(wide, tok):
    turned, tall = [], []
    for pair in range(wide.shape[1] // LANES):
        chunk = wide[:, pair * LANES : (pair + 1) * LANES]
        flat = chunk.astype(F32).T.astype(BF16)
        turned += [flat[:HALF], flat[HALF:]]
        tall += [chunk[:, :HALF], chunk[:, HALF:]]
    return jnp.concatenate(turned, axis=1), jnp.concatenate(tall, axis=0)


def key_block(i, bounds_ref, limits_ref, same_ref, other_ref):
    tok = same_ref.shape[2]
    pair, near = i // 2, i % 2
    row = (bounds_ref[1] ^ (2 * near)) - 4 * pair
    kv = jnp.concatenate([same_ref[near, pair], other_ref[near, pair]], axis=0)
    key = lax.broadcasted_iota(jnp.int32, (2 * tok, tok), 0)
    key = key + jnp.where(key < tok, row * tok, (row ^ 1) * tok - tok)
    return near, pair, kv, (key >= limits_ref[0:1, :]) & (key <= limits_ref[1:2, :])


def forward_kernel(bounds_ref, limits_ref, q_ref, same_ref, other_ref, att_ref, turned_ref, inv_ref, q_turned):
    tok = q_ref.shape[0]
    turned, tall = stack_heads(q_ref[:, : att_ref.shape[1]], tok)
    q_turned[...] = turned
    turned_ref[...] = jnp.zeros_like(turned_ref)
    inv_ref[...] = jnp.zeros_like(inv_ref)

    @pl.loop(0, bounds_ref[0])
    def step(i):
        near, pair, kv, ok = key_block(i, bounds_ref, limits_ref, same_ref, other_ref)
        for g, (first, count) in enumerate(GROUPS):
            at = slice(first * tok, (first + count) * tok)
            keys = kv[:, K_AT[g] : K_AT[g] + HALF]
            vals = kv[:, V_AT[g] : V_AT[g] + HALF]
            logit = dot(keys, q_turned[:, at])
            allowed = jnp.concatenate([ok] * count, axis=1)
            expo = jnp.where(allowed, jnp.exp(logit), 0.0)
            inv_ref[:, at] += jnp.sum(expo, axis=0, keepdims=True)
            turned_ref[:, at] += dot(vals, expo.astype(BF16), ((0,), (0,)))

    inverse = 1.0 / inv_ref[...]
    inv_ref[...] = inverse
    turned_ref[...] = turned_ref[...] * inverse
    for pair in range(att_ref.shape[1] // LANES):
        at = 2 * pair * tok
        both = jnp.concatenate([turned_ref[:, at : at + tok], turned_ref[:, at + tok : at + 2 * tok]], axis=0)
        att_ref[:, pair * LANES : (pair + 1) * LANES] = both.T.astype(BF16)


def vmem(n):
    return [pl.BlockSpec(memory_space=pltpu.VMEM)] * n


SMEM = pl.BlockSpec(memory_space=pltpu.SMEM)


def forward_call(bounds, limits, q, same, other, width):
    tok = q.shape[0]
    wide = width // HALF * tok
    work = same.size // same.shape[3] * 2 * wide
    return pl.pallas_call(
        forward_kernel,
        in_specs=[SMEM] + vmem(4),
        out_specs=vmem(3),
        out_shape=[
            jax.ShapeDtypeStruct((tok, width), BF16),
            jax.ShapeDtypeStruct((HALF, wide), F32),
            jax.ShapeDtypeStruct((1, wide), F32),
        ],
        scratch_shapes=[pltpu.VMEM((HALF, wide), BF16)],
        compiler_params=pltpu.CompilerParams(vmem_limit_bytes=VMEM_LIMIT),
        cost_estimate=pl.CostEstimate(flops=4 * HALF * work, bytes_accessed=4 * same.size, transcendentals=work),
        name="attention_forward",
    )(bounds, limits, q, same, other)


def backward_kernel(
    bounds_ref,
    limits_ref,
    q_ref,
    grad_ref,
    turned_ref,
    inv_ref,
    same_ref,
    other_ref,
    raw_ref,
    gain_ref,
    cos_ref,
    sin_ref,
    dq_ref,
    gain_grad_ref,
    same_out,
    other_out,
    q_turned,
    q_tall,
    g_turned,
    g_tall,
    dq_acc,
):
    tok = q_ref.shape[0]
    q_turned[...], q_tall[...] = stack_heads(q_ref[:, : dq_ref.shape[1]], tok)
    g_turned[...], g_tall[...] = stack_heads(grad_ref[...], tok)
    dq_acc[...] = jnp.zeros_like(dq_acc)
    same_out[...] = jnp.zeros_like(same_out)
    other_out[...] = jnp.zeros_like(other_out)
    delta = jnp.sum(g_turned[...].astype(F32) * turned_ref[...], axis=0, keepdims=True)

    @pl.loop(0, bounds_ref[0])
    def step(i):
        near, pair, kv, ok = key_block(i, bounds_ref, limits_ref, same_ref, other_ref)
        for g, (first, count) in enumerate(GROUPS):
            at = slice(first * tok, (first + count) * tok)
            keys = kv[:, K_AT[g] : K_AT[g] + HALF]
            vals = kv[:, V_AT[g] : V_AT[g] + HALF]
            allowed = jnp.concatenate([ok] * count, axis=1)
            prob = jnp.where(allowed, jnp.exp(dot(keys, q_turned[:, at])) * inv_ref[:, at], 0.0)
            d_score = (prob * (dot(vals, g_turned[:, at]) - delta[:, at])).astype(BF16)
            d_keys = dot(d_score, q_tall[at, :]).astype(BF16)
            d_vals = dot(prob.astype(BF16), g_tall[at, :]).astype(BF16)
            dq_acc[:, at] += dot(keys, d_score, ((0,), (0,)))
            same_out[near, pair, :, K_AT[g] : K_AT[g] + HALF] = d_keys[:tok]
            other_out[near, pair, :, K_AT[g] : K_AT[g] + HALF] = d_keys[tok:]
            same_out[near, pair, :, V_AT[g] : V_AT[g] + HALF] = d_vals[:tok]
            other_out[near, pair, :, V_AT[g] : V_AT[g] + HALF] = d_vals[tok:]

    total = jnp.zeros((1, LANES), F32)
    for pair in range(dq_ref.shape[1] // LANES):
        at = 2 * pair * tok
        both = jnp.concatenate([dq_acc[:, at : at + tok], dq_acc[:, at + tok : at + 2 * tok]], axis=0)
        cols = slice(pair * LANES, (pair + 1) * LANES)
        d_raw, term = head_backward(
            both.T * SCALE, raw_ref[:, cols], gain_ref[...], jnp.ones((1, LANES), F32), cos_ref[...], sin_ref[...]
        )
        dq_ref[:, cols] = d_raw.astype(BF16)
        total += term
    gain_grad_ref[...] = total


def backward_call(bounds, limits, q, grad, turned, inv, same, other, raw, gain, cosine, sine):
    tok, width = grad.shape
    wide = width // HALF * tok
    work = same.size // same.shape[3] * 2 * wide
    return pl.pallas_call(
        backward_kernel,
        in_specs=[SMEM] + vmem(11),
        out_specs=vmem(4),
        out_shape=[
            jax.ShapeDtypeStruct((tok, width), BF16),
            jax.ShapeDtypeStruct((1, LANES), F32),
            jax.ShapeDtypeStruct(same.shape, BF16),
            jax.ShapeDtypeStruct(other.shape, BF16),
        ],
        scratch_shapes=[
            pltpu.VMEM((HALF, wide), BF16),
            pltpu.VMEM((wide, HALF), BF16),
            pltpu.VMEM((HALF, wide), BF16),
            pltpu.VMEM((wide, HALF), BF16),
            pltpu.VMEM((HALF, wide), F32),
        ],
        compiler_params=pltpu.CompilerParams(vmem_limit_bytes=VMEM_LIMIT),
        cost_estimate=BESIDE,
        name="attention_backward",
    )(bounds, limits, q, grad, turned, inv, same, other, raw, gain, cosine, sine)


def kv_back_kernel(raw_ref, gain_ref, flag_ref, cos_ref, sin_ref, *refs):
    *part_refs, out_ref, gain_grad_ref = refs
    skip = raw_ref.shape[1] - out_ref.shape[1]
    total = jnp.zeros((1, LANES), F32)
    for part in range(out_ref.shape[1] // LANES):
        at = slice(part * LANES, (part + 1) * LANES)
        grad = sum(ref[:, at].astype(F32) for ref in part_refs)
        done, term = head_backward(
            grad, raw_ref[:, skip + at.start : skip + at.stop], gain_ref[:, at], flag_ref[:, at], cos_ref[...], sin_ref[...]
        )
        out_ref[:, at] = done.astype(BF16)
        total += term
    gain_grad_ref[...] = total


def kv_back_call(parts, raw, gain, flag, cosine, sine):
    tok, width = parts[0].shape
    return pl.pallas_call(
        kv_back_kernel,
        in_specs=vmem(5 + len(parts)),
        out_specs=vmem(2),
        out_shape=[jax.ShapeDtypeStruct((tok, width), BF16), jax.ShapeDtypeStruct((1, LANES), F32)],
        compiler_params=pltpu.CompilerParams(vmem_limit_bytes=VMEM_LIMIT),
        cost_estimate=BESIDE,
        name="key_value_heads_back",
    )(raw, gain, flag, cosine, sine, *parts)


def rope_tables(positions, head_dim):
    half = head_dim // 2
    inverse = jnp.exp(jnp.arange(half, dtype=F32) * (-2.0 * math.log(10000.0) / head_dim))
    angles = positions.astype(F32)[:, None] * inverse[None, :]
    cosine, sine = jnp.cos(angles), jnp.sin(angles)
    return jnp.concatenate([cosine] * 4, axis=1), jnp.concatenate([-sine, sine, -sine, sine], axis=1)


def norm_scale(vectors):
    return lax.rsqrt(jnp.mean(vectors * vectors, axis=-1, keepdims=True) + EPSILON)


def norm_back(vectors, scaler, gains, grads_in):
    scaled = grads_in * gains
    inner_mean = jnp.mean(scaled * vectors, axis=-1, keepdims=True)
    return scaler * scaled - vectors * (scaler * scaler * scaler) * inner_mean


def backwards(array, axis, width):
    count = array.shape[axis] // width
    pieces = [lax.slice_in_dim(array, i * width, (i + 1) * width, axis=axis) for i in range(count)]
    return jnp.concatenate(pieces[::-1], axis=axis)


def body(
    tokens,
    w_query,
    key_value_weight,
    w_out,
    w_gate,
    w_up,
    w_down,
    attn_gain,
    ffn_gain,
    query_gain,
    key_gain,
    segments,
    positions,
    out_grad,
):
    tok, width = tokens.shape
    rows = lax.axis_size("row")
    row = lax.axis_index("row")
    col = lax.axis_index("col")
    cols = lax.axis_size("col")
    w_rows = w_query.shape[0]
    q_width = w_query.shape[1]
    kv_half = key_value_weight.shape[1] // 2
    ff_cols = w_gate.shape[1]
    ff = ff_cols // MEMBERS
    seq_len = min(SEQ_MAX, tok * rows)
    span = seq_len // tok
    half = tok // 2

    w_packed = pack_call(col, w_query, key_value_weight, w_out)
    head_cols = w_packed.shape[1] - q_width
    w_all = lax.all_gather(w_packed, "row", axis=0, tiled=True)
    w_o_all = w_all[:, head_cols:]
    og_low = lax.dynamic_slice_in_dim(out_grad, col * half, half, 0)
    og_all = gather_cube_slowly(og_low)
    order, near_order = distances(True), distances(False)
    group = og_all.shape[0]

    w_ff = jnp.concatenate(
        [
            w_gate.reshape(w_rows, MEMBERS, ff),
            w_up.reshape(w_rows, MEMBERS, ff),
            w_down.T.reshape(w_rows, MEMBERS, ff),
        ],
        axis=2,
    ).transpose(1, 0, 2)
    w_ff = jnp.concatenate([w_ff] * (rows // MEMBERS), axis=0)

    input_f = tokens.astype(F32)
    act_scale = norm_scale(input_f)
    act_low = (input_f * act_scale * attn_gain).astype(BF16)
    cosine, sine = rope_tables(positions, HALF)
    q_lanes = jnp.tile(query_gain, 2)[None, :]
    k_lanes = jnp.tile(key_gain, 2)[None, :]
    kv_flag = jnp.concatenate([jnp.ones((1, 3 * HALF), F32), jnp.zeros((1, 3 * HALF), F32)], axis=1)
    kv_gain = jnp.where(kv_flag > 0, jnp.tile(k_lanes, (1, 3)), 1.0)
    q_flag = jnp.ones((1, q_width), F32)
    q_gain = jnp.tile(q_lanes * SCALE, (1, q_width // LANES))
    gain = jnp.concatenate([q_gain, kv_gain], axis=1)
    flag = jnp.concatenate([q_flag, kv_flag], axis=1)
    act_low, og_all = lax.optimization_barrier((act_low, og_all))
    raw, heads, kv_low = heads_call(act_low, w_all, gain, flag, cosine, sine, head_cols - q_width)
    same_kv, other_kv, w_ff = gather_earlier(kv_low, span, w_ff)
    w_ff_all = lax.all_to_all(w_ff, "row", split_axis=0, concat_axis=0, tiled=True).reshape(width, 3 * ff)

    in_span = row % span
    seq_segments = lax.dynamic_slice_in_dim(segments, (row - in_span) * tok, seq_len, 0)
    own_segments = lax.dynamic_slice_in_dim(segments, row * tok, tok, 0)
    own_index = in_span * tok + jnp.arange(tok, dtype=jnp.int32)
    index = jnp.arange(seq_len, dtype=jnp.int32)
    start = jnp.min(jnp.where(seq_segments[None, :] == own_segments[:, None], index[None, :], seq_len), axis=1)
    start = jnp.where(own_segments < 0, own_index, start)
    limits = jnp.stack([start, own_index])
    bounds = jnp.stack([2 * (in_span // 4 + 1 - jnp.min(start) // (4 * tok)), in_span])
    attn_low, turned, inv = forward_call(bounds, limits, heads, same_kv, other_kv, q_width)
    attn_part = dot(attn_low, w_o_all, ((1,), (1,))).astype(BF16)

    def mine(array, which):
        return lax.dynamic_slice_in_dim(array, which * half, half, 0)

    arrived = swap_col(mine(attn_part, 1 - col))
    hidden = mine(input_f, col) + (mine(attn_part, col).astype(F32) + arrived.astype(F32))

    ffn_scale = norm_scale(hidden)
    ffn_low = (hidden * ffn_scale * ffn_gain).astype(BF16)
    ffn_same, ffn_other, w_ff_all = gather_cube(ffn_low, w_ff_all)
    ffn_all = jnp.concatenate([ffn_same, ffn_other], axis=0)
    gate_up = dot(ffn_all, w_ff_all[:, : 2 * ff])
    gate_pre, up_pre = gate_up[:, :ff], gate_up[:, ff:]
    d_inner = dot(og_all, w_ff_all[:, 2 * ff :])
    sigma = jax.nn.sigmoid(gate_pre)
    silu_gate = gate_pre * sigma
    inner_low = (silu_gate * up_pre).astype(BF16)
    d_gate = d_inner * up_pre * (sigma * (1.0 + gate_pre * (1.0 - sigma)))
    d_up = d_inner * silu_gate
    d_gate_up = jnp.concatenate([d_gate, d_up], axis=1).astype(BF16)

    w_gate_up = w_ff_all[:, : 2 * ff]
    away = dot(d_gate_up[group // 2 :], w_gate_up, ((1,), (1,))).astype(BF16)
    here = dot(d_gate_up[: group // 2], w_gate_up, ((1,), (1,)))
    total = (here + swap_core(away).astype(F32)).astype(BF16).reshape(2, 2, 2, half, width)

    left, right = total[..., : width // 2], total[..., width // 2 :]
    (left_away, right_away), grads_ff = beside(
        (left[1], right[:, 1]),
        lambda one, two: (swap_cube(one, 1), swap_cube(two, cols)),
        (ffn_all, og_all, d_gate_up, inner_low),
        lambda *arrays: ff_grads_call(*arrays, rows),
    )
    left, right = add_low(left[0], left_away), add_low(right[:, 0], right_away)
    grads_ff = lax.psum_scatter(
        grads_ff, "row", scatter_dimension=0, tiled=True, axis_index_groups=across_groups()
    )

    def down(inner_low):
        w_down_all = w_ff_all[:, 2 * ff :]
        away = dot(inner_low[group // 2 :], w_down_all, ((1,), (1,))).astype(BF16)
        return away, dot(inner_low[: group // 2], w_down_all, ((1,), (1,))).astype(BF16)

    (left_away, right_away), (out_away, out_here) = beside(
        (left[1], right[:, 1]),
        lambda one, two: (swap_cube(one, cols), swap_cube(two, 2 * cols)),
        (inner_low,),
        down,
    )
    left, right = add_low(left[0], left_away), add_low(right[:, 0], right_away)
    ffn_out = over_core(out_here, out_away).reshape(2, 2, 2, half, width)
    left = halve(left, 0, 2 * cols)
    right = halve(right, 0, 1)
    ffn_back = jnp.concatenate([left, right], axis=1)
    ffn_gain_part = jnp.sum(ffn_back * hidden * ffn_scale, axis=0)
    d_hidden = og_low.astype(F32) + norm_back(hidden, ffn_scale, ffn_gain, ffn_back)
    d_hidden_half = d_hidden.astype(BF16)
    d_hidden_low = halves(d_hidden_half, swap_col(d_hidden_half), col)

    d_attn = dot(d_hidden_low, w_o_all).astype(BF16)
    d_q, q_gain_part, same_d, other_d = backward_call(
        bounds, limits, heads, d_attn, turned, inv, same_kv, other_kv, raw, q_lanes, cosine, sine
    )
    d_kv_total = over_core(same_d, other_d).reshape(-1, tok, same_d.shape[3])

    ffn_out = halve(after(ffn_out, d_hidden_low), 0, 1)

    count = d_kv_total.shape[0] // 2
    (kv_away,), (grad_o, grad_q) = beside(
        (d_kv_total[count:],),
        lambda block: (swap_near(block),),
        (d_hidden_low, act_low, d_q),
        lambda hid, act, grad: (
            over_core(*rows_call(near_order, hid, attn_low)),
            over_core(*rows_call(near_order, act, grad)),
        ),
    )
    d_kv_total = add_low(d_kv_total[:count], kv_away)
    grad_o = over_near(grad_o)
    grad_q = over_near(after(grad_q, d_kv_total))
    kv_parts = over_far(d_kv_total, span, False, False)
    *kv_parts, ffn_out = lax.optimization_barrier((*kv_parts, ffn_out))
    grad_oq = jnp.concatenate([grad_o, grad_q], axis=2)
    grad_oq = lax.psum_scatter(
        grad_oq, "row", scatter_dimension=0, tiled=True, axis_index_groups=far_groups()
    )[0].astype(F32)
    grad_o, grad_q = grad_oq[:, :q_width].T, grad_oq[:, q_width:]
    d_kv, k_gain_part = kv_back_call(kv_parts, raw, kv_gain, kv_flag, cosine, sine)
    d_one = jnp.concatenate([d_q, d_kv], axis=1)

    per_row = HALF // rows
    fold = lambda part: (part[0, :HALF] + part[0, HALF:]).reshape(rows, 1, per_row)
    line = lambda values: jnp.pad(values, ((0, 0), (0, 0), (0, d_kv.shape[1] - values.shape[2])))
    small = [
        line(jnp.concatenate([fold(q_gain_part), fold(k_gain_part)], axis=2)),
        line(ffn_gain_part.reshape(rows, 1, w_rows)),
        jnp.zeros((rows, 14, d_kv.shape[1]), F32),
    ]
    small = jnp.concatenate(small, axis=1).astype(BF16)
    kv_partial = over_core(*rows_call(order, act_low, d_kv, small))
    d_one = after(d_one, kv_partial)
    kv_partial = over_near(kv_partial)
    grads_ff = exchange_group(after(grads_ff, kv_partial))
    ffn_out = halve(after(ffn_out, kv_partial), 0, cols)
    grad_kv, grads_ff, ffn_out = lax.optimization_barrier(
        (over_far(kv_partial, rows, True, True), grads_ff, halve(ffn_out, 0, 2 * cols))
    )
    out_half = (hidden + ffn_out).astype(BF16)
    output = halves(out_half, swap_col(out_half), col)
    grad_kv = add_up(grad_kv)
    act_back = dot(d_one, w_all[:, :head_cols], ((1,), (1,))).astype(BF16)
    act_back = act_back.astype(F32) + swap_col(act_back).astype(F32)
    input_grad = d_hidden_low.astype(F32) + norm_back(input_f, act_scale, attn_gain, act_back)
    grad_kv, small = grad_kv[:w_rows], grad_kv[w_rows : w_rows + 2]
    grad_query = jnp.where(col == 0, grad_q, backwards(grad_q, 1, LANES))
    grad_out = jnp.where(col == 0, grad_o, backwards(grad_o, 0, LANES))

    kv_own = grad_kv.astype(BF16)
    kv_away = swap_col(kv_own)
    kv_first = jnp.where(col == 0, kv_own, kv_away).astype(F32)
    kv_last = jnp.where(col == 0, kv_away, kv_own).astype(F32)

    def one_head(array, at):
        return array[:, at : at + HALF]

    pieces = []
    for at in (K_AT, V_AT):
        pieces += [one_head(kv_first, at[0]), one_head(kv_first, at[1])]
        pieces += [one_head(kv_first, at[2]) + one_head(kv_last, at[2])]
        pieces += [one_head(kv_last, at[1]), one_head(kv_last, at[0])]
    grad_keyval = jnp.concatenate(pieces, axis=1)

    grad_gate, grad_up, grad_down = ff_format_call(grads_ff)

    attn_part_gain = jnp.sum(
        jnp.concatenate([grad_q, grad_kv], axis=1) * w_packed[:, :head_cols].astype(F32), axis=1
    )
    gains = jnp.concatenate([attn_part_gain, small[1, :w_rows], small[0, : 2 * per_row]])
    gains = gains + swap_col(gains)
    own_gains = lambda whole: lax.dynamic_slice_in_dim(whole, row * w_rows, w_rows, 0)
    grad_attn_gain = gains[:w_rows] / own_gains(attn_gain)
    grad_ffn_gain = gains[w_rows : 2 * w_rows]
    grad_query_gain = gains[2 * w_rows : 2 * w_rows + per_row]
    grad_key_gain = gains[2 * w_rows + per_row :]
    return (
        output,
        input_grad,
        grad_query,
        grad_keyval,
        grad_out,
        grad_gate,
        grad_up,
        grad_down,
        grad_attn_gain,
        grad_ffn_gain,
        grad_query_gain,
        grad_key_gain,
    )


def solution(mesh):
    placed = (
        P("row", None),
        P("row", "col"),
        P("row", None),
        P("col", "row"),
        P("row", "col"),
        P("row", "col"),
        P("col", "row"),
        P(),
        P(),
        P(),
        P(),
        P(),
        P("row"),
        P("row", None),
    )
    return jax.shard_map(
        body,
        mesh=mesh,
        in_specs=placed,
        out_specs=(
            P("row", None),
            P("row", None),
            P("row", "col"),
            P("row", None),
            P("col", "row"),
            P("row", "col"),
            P("row", "col"),
            P("col", "row"),
            P("row"),
            P("row"),
            P("row"),
            P("row"),
        ),
        check_vma=False,
    )
```

```python
import math

import jax
import jax.numpy as jnp
from jax import lax
from jax.experimental import pallas as pl
from jax.experimental.pallas import tpu as pltpu
from jax.sharding import PartitionSpec as P

EPSILON = 1e-06
SCALE = 0.125
SEQ_MAX = 4096
MEMBERS = 8
LANES = 128
HALF = 64
F32 = jnp.float32
BF16 = jnp.bfloat16
VMEM_LIMIT = 56 * 1024 * 1024


def dot(a, b, dims=((1,), (0,))):
    return lax.dot_general(a, b, (dims, ((), ())), preferred_element_type=F32)


def swap_core(block):
    rows = lax.axis_size("row")
    return lax.ppermute(block, "row", [(i, i ^ 1) for i in range(rows)])


def swap_col(block):
    return lax.ppermute(block, "col", [(0, 1), (1, 0)])


def shift_far(block, steps, span, wrap):
    rows = lax.axis_size("row")
    route = []
    for i in range(rows):
        first, at = i // span * span, i % span + 4 * steps
        if wrap or 0 <= at < span:
            route.append((i, first + at % span))
    return lax.ppermute(block, "row", route)


def swap_near(block):
    rows = lax.axis_size("row")
    return lax.ppermute(block, "row", [(i, i ^ 2) for i in range(rows)])


def swap_cube(block, number):
    rows, cols = lax.axis_size("row"), lax.axis_size("col")
    route = []
    for i in range(rows):
        first, chip, core = i // MEMBERS * MEMBERS, i % MEMBERS // 2, i % 2
        there = first + 2 * (chip ^ (number // cols)) + core
        route += [(i * cols + c, there * cols + (c ^ (number % cols))) for c in range(cols)]
    return lax.ppermute(block, ("row", "col"), route)


def gather_earlier(block, span, weights):
    far = jnp.stack([block] + [shift_far(block, k, span, False) for k in range(1, span // 4)])
    far, weights = lax.optimization_barrier((far, weights))
    same = jnp.stack([far, swap_near(far)])
    return same, swap_core(same), weights


def add_low(one, two):
    return (one.astype(F32) + two.astype(F32)).astype(BF16)


def over_core(same, other):
    return (same.astype(F32) + swap_core(other.astype(BF16)).astype(F32)).astype(BF16)


def over_near(total):
    count = total.shape[0] // 2
    return (total[:count].astype(F32) + swap_near(total[count:]).astype(F32)).astype(BF16)


def over_far(total, span, wrap, forward):
    sign = 1 if forward else -1
    return [total[0]] + [shift_far(total[k], sign * k, span, wrap) for k in range(1, span // 4)]


def add_up(parts):
    return sum(p.astype(F32) for p in parts)


def gather_rows(block):
    rows = lax.axis_size("row")
    far = jnp.concatenate([block] + [shift_far(block, -k, rows, True) for k in range(1, rows // 4)], axis=0)
    same = jnp.concatenate([far, swap_near(far)], axis=0)
    return jnp.concatenate([same, swap_core(same)], axis=0)


def distances(far):
    rows, row = lax.axis_size("row"), lax.axis_index("row")
    order = [
        ((row ^ near) + 4 * k) % rows if far else (row ^ near) % 4 + 4 * k for near in (0, 2, 1, 3) for k in range(rows // 4)
    ]
    return jnp.stack(order)


def after_all(arrays, *others):
    return lax.optimization_barrier(tuple(arrays) + others)[: len(arrays)]


def beside(operands, send, inputs, work):
    operands, inputs = lax.optimization_barrier((operands, inputs))
    return lax.optimization_barrier((send(*operands), work(*inputs)))


def after(array, *others):
    return after_all((array,), *others)[0]


def gather_cube(block, weights):
    cols = lax.axis_size("col")
    both = jnp.stack([block, swap_cube(block, 1)])
    *pieces, weights = lax.optimization_barrier((*(swap_cube(both, number * cols) for number in (2, 1, 3)), weights))
    pieces = [both] + pieces
    same = jnp.concatenate([piece[c] for c in range(2) for piece in pieces], axis=0)
    return same, swap_core(same), weights


def gather_cube_slowly(block):
    cols = lax.axis_size("col")
    block = jnp.concatenate([block, swap_cube(block, 2 * cols)], axis=0)
    block = jnp.concatenate([block, swap_cube(block, cols)], axis=0)
    block = jnp.concatenate([block, swap_cube(block, 1)], axis=0)
    return jnp.concatenate([block, swap_core(block)], axis=0)


def halve(total, axis, number):
    here, away = (lax.index_in_dim(total, i, axis, keepdims=False) for i in range(2))
    return here.astype(F32) + swap_cube(away.astype(BF16), number).astype(F32)


def far_groups():
    rows = lax.axis_size("row")
    return [list(range(near, rows, 4)) for near in range(4)]


def pick(array, place, axis):
    first = lax.index_in_dim(array, 0, axis, keepdims=False)
    second = lax.index_in_dim(array, 1, axis, keepdims=False)
    return jnp.where(place == 0, first, second), jnp.where(place == 0, second, first)


def group_rows():
    rows = lax.axis_size("row")
    return [list(range(first, first + MEMBERS)) for first in range(0, rows, MEMBERS)]


def across_groups():
    rows = lax.axis_size("row")
    return [list(range(member, rows, MEMBERS)) for member in range(MEMBERS)]


def exchange_group(blocks):
    return lax.all_to_all(
        blocks, "row", split_axis=0, concat_axis=0, tiled=True, axis_index_groups=group_rows()
    )


def halves(own, other, col):
    low = jnp.where(col == 0, own, other)
    high = jnp.where(col == 0, other, own)
    return jnp.concatenate([low, high], axis=0)


def partner(v):
    lane = lax.broadcasted_iota(jnp.int32, v.shape, 1)
    ahead = pltpu.roll(v, LANES - HALF // 2, 1)
    behind = pltpu.roll(v, HALF // 2, 1)
    return jnp.where(lane % HALF < HALF // 2, ahead, behind)


def head_mean(v):
    lane = lax.broadcasted_iota(jnp.int32, v.shape, 1)
    first = jnp.sum(jnp.where(lane < HALF, v, 0.0), axis=1, keepdims=True)
    second = jnp.sum(jnp.where(lane < HALF, 0.0, v), axis=1, keepdims=True)
    return jnp.where(lane < HALF, first, second) * (1.0 / HALF)


def head_forward(raw, gain, flag, cosine, sine):
    scaler = jnp.where(flag > 0, lax.rsqrt(head_mean(raw * raw) + EPSILON), 1.0)
    normed = raw * scaler * gain
    cosine = jnp.where(flag > 0, cosine, 1.0)
    sine = jnp.where(flag > 0, sine, 0.0)
    return normed * cosine + partner(normed) * sine


def head_backward(grad, raw, gain, flag, cosine, sine):
    on = flag > 0
    scaler = lax.rsqrt(head_mean(raw * raw) + EPSILON)
    back = grad * cosine - partner(grad) * sine
    scaled = back * gain
    inner = head_mean(scaled * raw)
    grad_raw = scaler * scaled - raw * (scaler * scaler * scaler) * inner
    gain_term = jnp.sum(jnp.where(on, back * raw * scaler, 0.0), axis=0, keepdims=True)
    return jnp.where(on, grad_raw, grad), gain_term


def heads_kernel(act_ref, w_ref, gain_ref, flag_ref, cos_ref, sin_ref, raw_ref, out_ref, kv_ref):
    raw = dot(act_ref[...], w_ref[...])
    raw_ref[...] = raw
    parts = raw.shape[1] // LANES
    query_parts = pl.num_programs(0) * parts - kv_ref.shape[1] // LANES
    for part in range(parts):
        at = slice(part * LANES, (part + 1) * LANES)
        done = head_forward(raw[:, at], gain_ref[:, at], flag_ref[:, at], cos_ref[...], sin_ref[...]).astype(BF16)
        out_ref[:, at] = done
        place = pl.program_id(0) * parts + part - query_parts

        @pl.when(place >= 0)
        def keep():
            kv_ref[:, pl.ds(pl.multiple_of(jnp.maximum(place, 0) * LANES, LANES), LANES)] = done


def heads_call(act, w_all, gain, flag, cosine, sine, kv_width):
    tok, width = act.shape
    cols = gain.shape[1]
    block = 256
    whole = lambda shape: pl.BlockSpec(shape, lambda i: (0, 0))
    chunk = lambda rows: pl.BlockSpec((rows, block), lambda i: (0, i))
    return pl.pallas_call(
        heads_kernel,
        grid=(cols // block,),
        in_specs=[whole((tok, width)), chunk(width), chunk(1), chunk(1), whole((tok, LANES)), whole((tok, LANES))],
        out_specs=[chunk(tok), chunk(tok), whole((tok, kv_width))],
        out_shape=[
            jax.ShapeDtypeStruct((tok, cols), F32),
            jax.ShapeDtypeStruct((tok, cols), BF16),
            jax.ShapeDtypeStruct((tok, kv_width), BF16),
        ],
        compiler_params=pltpu.CompilerParams(vmem_limit_bytes=VMEM_LIMIT),
        cost_estimate=pl.CostEstimate(flops=2 * tok * width * cols, bytes_accessed=2 * width * cols, transcendentals=0),
        name="project_heads",
    )(act, w_all, gain, flag, cosine, sine)


def pack_kernel(col_ref, q_ref, kv_ref, o_ref, out_ref):
    first = col_ref[0] == 0
    pairs = q_ref.shape[1] // LANES
    half = kv_ref.shape[1] // 2
    heads = half // HALF

    def head(number, offset):
        one = kv_ref[:, offset + number * HALF : offset + (number + 1) * HALF]
        two = kv_ref[:, offset + (heads - 1 - number) * HALF : offset + (heads - number) * HALF]
        return jnp.where(first, one, two)

    for pair in range(pairs):
        here = slice(pair * LANES, (pair + 1) * LANES)
        there = slice((pairs - 1 - pair) * LANES, (pairs - pair) * LANES)
        out_ref[:, here] = jnp.where(first, q_ref[:, here], q_ref[:, there])
        turned = jnp.where(first, o_ref[here, :].astype(F32), o_ref[there, :].astype(F32)).T
        at = q_ref.shape[1] + 6 * HALF + pair * LANES
        out_ref[:, at : at + LANES] = turned.astype(BF16)
    at = q_ref.shape[1]
    for one, two in ((head(0, 0), head(1, 0)), (head(2, 0), head(2, half)), (head(0, half), head(1, half))):
        out_ref[:, at : at + LANES] = jnp.concatenate([one, two], axis=1)
        at += LANES


def pack_call(col, w_query, w_kv, w_out):
    lines, width = w_query.shape
    return pl.pallas_call(
        pack_kernel,
        in_specs=[pl.BlockSpec(memory_space=pltpu.SMEM)] + [pl.BlockSpec(memory_space=pltpu.VMEM)] * 3,
        out_specs=pl.BlockSpec(memory_space=pltpu.VMEM),
        out_shape=jax.ShapeDtypeStruct((lines, 2 * width + 6 * HALF), BF16),
        cost_estimate=pl.CostEstimate(flops=0, bytes_accessed=10 * w_query.size, transcendentals=0),
        name="pack_weights",
    )(col.reshape(1), w_query, w_kv, w_out)


BESIDE = pl.CostEstimate(flops=0, bytes_accessed=0, transcendentals=0)


def turn(block):
    return block.astype(F32).T.astype(BF16)


def rows_kernel(order_ref, left_ref, right_ref, *refs):
    *more, own_ref, away_ref = refs
    count = own_ref.shape[0]
    for at in range(2 * count):
        to, place = (own_ref, at) if at < count else (away_ref, at - count)
        row = order_ref[at]
        block = turn(left_ref[:, pl.ds(pl.multiple_of(row * LANES, LANES), LANES)])
        to[place, :LANES] = dot(block, right_ref[...]).astype(BF16)
        if more:
            to[place, LANES:] = more[0][row]


def rows_call(order, left, right, *more):
    count = order.shape[0] // 2
    lines = left.shape[1] // (2 * count)
    if lines != LANES:
        blocks = jnp.take(left.reshape(left.shape[0], 2 * count, lines), order, axis=1)
        product = jnp.einsum("trl,tn->rln", blocks, right, preferred_element_type=F32).astype(BF16)
        if more:
            product = jnp.concatenate([product, jnp.take(more[0], order, axis=0)], axis=1)
        return product[:count], product[count:]
    shape = (count, lines + (more[0].shape[1] if more else 0), right.shape[1])
    return pl.pallas_call(
        rows_kernel,
        in_specs=[pl.BlockSpec(memory_space=pltpu.SMEM)] + [pl.BlockSpec(memory_space=pltpu.VMEM)] * (2 + len(more)),
        out_specs=[pl.BlockSpec(memory_space=pltpu.VMEM)] * 2,
        out_shape=[jax.ShapeDtypeStruct(shape, BF16)] * 2,
        compiler_params=pltpu.CompilerParams(vmem_limit_bytes=VMEM_LIMIT),
        cost_estimate=BESIDE,
        name="weight_rows",
    )(order, left, right, *more)


def ff_grads_kernel(ffn_ref, og_ref, d_ref, inner_ref, out_ref, d_turned, inner_turned):
    @pl.when(pl.program_id(0) == 0)
    def prepare():
        d_turned[...] = turn(d_ref[...])
        inner_turned[...] = turn(inner_ref[...])

    both = d_turned.shape[0]
    gate_up = dot(d_turned[...], ffn_ref[...]).astype(BF16)
    down = dot(inner_turned[...], og_ref[...]).astype(BF16)
    for part in range(out_ref.shape[0]):
        at = slice(part * LANES, (part + 1) * LANES)
        out_ref[part, :both] = gate_up[:, at]
        out_ref[part, both:] = down[:, at]


def ff_grads_call(ffn, og, d_gate_up, inner, rows):
    tokens, width = ffn.shape
    both, ff = d_gate_up.shape[1], inner.shape[1]
    lines = width // rows
    if lines != LANES:
        products = jnp.concatenate([dot(d_gate_up, ffn, ((0,), (0,))), dot(inner, og, ((0,), (0,)))], axis=0)
        return products.astype(BF16).reshape(both + ff, rows, lines).transpose(1, 0, 2)
    parts = 2
    whole = lambda array: pl.BlockSpec(array.shape, lambda i: (0, 0))
    column = pl.BlockSpec((tokens, parts * LANES), lambda i: (0, i))
    return pl.pallas_call(
        ff_grads_kernel,
        grid=(rows // parts,),
        in_specs=[column, column, whole(d_gate_up), whole(inner)],
        out_specs=pl.BlockSpec((parts, both + ff, LANES), lambda i: (i, 0, 0)),
        out_shape=jax.ShapeDtypeStruct((rows, both + ff, LANES), BF16),
        scratch_shapes=[pltpu.VMEM((both, tokens), BF16), pltpu.VMEM((ff, tokens), BF16)],
        compiler_params=pltpu.CompilerParams(vmem_limit_bytes=VMEM_LIMIT),
        cost_estimate=BESIDE,
        name="feed_forward_weight_grads",
    )(ffn, og, d_gate_up, inner)


def ff_format_kernel(in_ref, gate_ref, up_ref, down_ref):
    members, units, lines = in_ref.shape
    ff = units // 3
    for member in range(members):
        at = slice(member * ff, (member + 1) * ff)
        gate_ref[:, at] = in_ref[member, :ff].astype(F32).T
        up_ref[:, at] = in_ref[member, ff : 2 * ff].astype(F32).T
        down_ref[at] = in_ref[member, 2 * ff :].astype(F32)


def ff_format_call(blocks):
    members, units, lines = blocks.shape
    cols = members * units // 3
    return pl.pallas_call(
        ff_format_kernel,
        in_specs=[pl.BlockSpec(memory_space=pltpu.VMEM)],
        out_specs=[pl.BlockSpec(memory_space=pltpu.VMEM)] * 3,
        out_shape=[jax.ShapeDtypeStruct(shape, F32) for shape in ((lines, cols), (lines, cols), (cols, lines))],
        compiler_params=pltpu.CompilerParams(vmem_limit_bytes=VMEM_LIMIT),
        name="feed_forward_grads",
    )(blocks)


GROUPS = ((0, 4), (4, 4), (8, 2))
K_AT = (0, 64, 128)
V_AT = (256, 320, 192)


def stack_heads(wide, tok):
    turned, tall = [], []
    for pair in range(wide.shape[1] // LANES):
        chunk = wide[:, pair * LANES : (pair + 1) * LANES]
        flat = chunk.astype(F32).T.astype(BF16)
        turned += [flat[:HALF], flat[HALF:]]
        tall += [chunk[:, :HALF], chunk[:, HALF:]]
    return jnp.concatenate(turned, axis=1), jnp.concatenate(tall, axis=0)


def key_block(i, bounds_ref, limits_ref, same_ref, other_ref):
    tok = same_ref.shape[2]
    pair, near = i // 2, i % 2
    row = (bounds_ref[1] ^ (2 * near)) - 4 * pair
    kv = jnp.concatenate([same_ref[near, pair], other_ref[near, pair]], axis=0)
    key = lax.broadcasted_iota(jnp.int32, (2 * tok, tok), 0)
    key = key + jnp.where(key < tok, row * tok, (row ^ 1) * tok - tok)
    return near, pair, kv, (key >= limits_ref[0:1, :]) & (key <= limits_ref[1:2, :])


def forward_kernel(bounds_ref, limits_ref, q_ref, same_ref, other_ref, att_ref, turned_ref, inv_ref, q_turned):
    tok = q_ref.shape[0]
    turned, tall = stack_heads(q_ref[:, : att_ref.shape[1]], tok)
    q_turned[...] = turned
    turned_ref[...] = jnp.zeros_like(turned_ref)
    inv_ref[...] = jnp.zeros_like(inv_ref)

    @pl.loop(0, bounds_ref[0])
    def step(i):
        near, pair, kv, ok = key_block(i, bounds_ref, limits_ref, same_ref, other_ref)
        for g, (first, count) in enumerate(GROUPS):
            at = slice(first * tok, (first + count) * tok)
            keys = kv[:, K_AT[g] : K_AT[g] + HALF]
            vals = kv[:, V_AT[g] : V_AT[g] + HALF]
            logit = dot(keys, q_turned[:, at])
            allowed = jnp.concatenate([ok] * count, axis=1)
            expo = jnp.where(allowed, jnp.exp(logit), 0.0)
            inv_ref[:, at] += jnp.sum(expo, axis=0, keepdims=True)
            turned_ref[:, at] += dot(vals, expo.astype(BF16), ((0,), (0,)))

    inverse = 1.0 / inv_ref[...]
    inv_ref[...] = inverse
    turned_ref[...] = turned_ref[...] * inverse
    for pair in range(att_ref.shape[1] // LANES):
        at = 2 * pair * tok
        both = jnp.concatenate([turned_ref[:, at : at + tok], turned_ref[:, at + tok : at + 2 * tok]], axis=0)
        att_ref[:, pair * LANES : (pair + 1) * LANES] = both.T.astype(BF16)


def vmem(n):
    return [pl.BlockSpec(memory_space=pltpu.VMEM)] * n


SMEM = pl.BlockSpec(memory_space=pltpu.SMEM)


def forward_call(bounds, limits, q, same, other, width):
    tok = q.shape[0]
    wide = width // HALF * tok
    work = same.size // same.shape[3] * 2 * wide
    return pl.pallas_call(
        forward_kernel,
        in_specs=[SMEM] + vmem(4),
        out_specs=vmem(3),
        out_shape=[
            jax.ShapeDtypeStruct((tok, width), BF16),
            jax.ShapeDtypeStruct((HALF, wide), F32),
            jax.ShapeDtypeStruct((1, wide), F32),
        ],
        scratch_shapes=[pltpu.VMEM((HALF, wide), BF16)],
        compiler_params=pltpu.CompilerParams(vmem_limit_bytes=VMEM_LIMIT),
        cost_estimate=pl.CostEstimate(flops=4 * HALF * work, bytes_accessed=4 * same.size, transcendentals=work),
        name="attention_forward",
    )(bounds, limits, q, same, other)


def backward_kernel(
    bounds_ref,
    limits_ref,
    q_ref,
    grad_ref,
    turned_ref,
    inv_ref,
    same_ref,
    other_ref,
    raw_ref,
    gain_ref,
    cos_ref,
    sin_ref,
    dq_ref,
    gain_grad_ref,
    same_out,
    other_out,
    q_turned,
    q_tall,
    g_turned,
    g_tall,
    dq_acc,
):
    tok = q_ref.shape[0]
    q_turned[...], q_tall[...] = stack_heads(q_ref[:, : dq_ref.shape[1]], tok)
    g_turned[...], g_tall[...] = stack_heads(grad_ref[...], tok)
    dq_acc[...] = jnp.zeros_like(dq_acc)
    same_out[...] = jnp.zeros_like(same_out)
    other_out[...] = jnp.zeros_like(other_out)
    delta = jnp.sum(g_turned[...].astype(F32) * turned_ref[...], axis=0, keepdims=True)

    @pl.loop(0, bounds_ref[0])
    def step(i):
        near, pair, kv, ok = key_block(i, bounds_ref, limits_ref, same_ref, other_ref)
        for g, (first, count) in enumerate(GROUPS):
            at = slice(first * tok, (first + count) * tok)
            keys = kv[:, K_AT[g] : K_AT[g] + HALF]
            vals = kv[:, V_AT[g] : V_AT[g] + HALF]
            allowed = jnp.concatenate([ok] * count, axis=1)
            prob = jnp.where(allowed, jnp.exp(dot(keys, q_turned[:, at])) * inv_ref[:, at], 0.0)
            d_score = (prob * (dot(vals, g_turned[:, at]) - delta[:, at])).astype(BF16)
            d_keys = dot(d_score, q_tall[at, :]).astype(BF16)
            d_vals = dot(prob.astype(BF16), g_tall[at, :]).astype(BF16)
            dq_acc[:, at] += dot(keys, d_score, ((0,), (0,)))
            same_out[near, pair, :, K_AT[g] : K_AT[g] + HALF] = d_keys[:tok]
            other_out[near, pair, :, K_AT[g] : K_AT[g] + HALF] = d_keys[tok:]
            same_out[near, pair, :, V_AT[g] : V_AT[g] + HALF] = d_vals[:tok]
            other_out[near, pair, :, V_AT[g] : V_AT[g] + HALF] = d_vals[tok:]

    total = jnp.zeros((1, LANES), F32)
    for pair in range(dq_ref.shape[1] // LANES):
        at = 2 * pair * tok
        both = jnp.concatenate([dq_acc[:, at : at + tok], dq_acc[:, at + tok : at + 2 * tok]], axis=0)
        cols = slice(pair * LANES, (pair + 1) * LANES)
        d_raw, term = head_backward(
            both.T * SCALE, raw_ref[:, cols], gain_ref[...], jnp.ones((1, LANES), F32), cos_ref[...], sin_ref[...]
        )
        dq_ref[:, cols] = d_raw.astype(BF16)
        total += term
    gain_grad_ref[...] = total


def backward_call(bounds, limits, q, grad, turned, inv, same, other, raw, gain, cosine, sine):
    tok, width = grad.shape
    wide = width // HALF * tok
    work = same.size // same.shape[3] * 2 * wide
    return pl.pallas_call(
        backward_kernel,
        in_specs=[SMEM] + vmem(11),
        out_specs=vmem(4),
        out_shape=[
            jax.ShapeDtypeStruct((tok, width), BF16),
            jax.ShapeDtypeStruct((1, LANES), F32),
            jax.ShapeDtypeStruct(same.shape, BF16),
            jax.ShapeDtypeStruct(other.shape, BF16),
        ],
        scratch_shapes=[
            pltpu.VMEM((HALF, wide), BF16),
            pltpu.VMEM((wide, HALF), BF16),
            pltpu.VMEM((HALF, wide), BF16),
            pltpu.VMEM((wide, HALF), BF16),
            pltpu.VMEM((HALF, wide), F32),
        ],
        compiler_params=pltpu.CompilerParams(vmem_limit_bytes=VMEM_LIMIT),
        cost_estimate=BESIDE,
        name="attention_backward",
    )(bounds, limits, q, grad, turned, inv, same, other, raw, gain, cosine, sine)


def kv_back_kernel(raw_ref, gain_ref, flag_ref, cos_ref, sin_ref, *refs):
    *part_refs, out_ref, gain_grad_ref = refs
    skip = raw_ref.shape[1] - out_ref.shape[1]
    total = jnp.zeros((1, LANES), F32)
    for part in range(out_ref.shape[1] // LANES):
        at = slice(part * LANES, (part + 1) * LANES)
        grad = sum(ref[:, at].astype(F32) for ref in part_refs)
        done, term = head_backward(
            grad, raw_ref[:, skip + at.start : skip + at.stop], gain_ref[:, at], flag_ref[:, at], cos_ref[...], sin_ref[...]
        )
        out_ref[:, at] = done.astype(BF16)
        total += term
    gain_grad_ref[...] = total


def kv_back_call(parts, raw, gain, flag, cosine, sine):
    tok, width = parts[0].shape
    return pl.pallas_call(
        kv_back_kernel,
        in_specs=vmem(5 + len(parts)),
        out_specs=vmem(2),
        out_shape=[jax.ShapeDtypeStruct((tok, width), BF16), jax.ShapeDtypeStruct((1, LANES), F32)],
        compiler_params=pltpu.CompilerParams(vmem_limit_bytes=VMEM_LIMIT),
        cost_estimate=BESIDE,
        name="key_value_heads_back",
    )(raw, gain, flag, cosine, sine, *parts)


def rope_tables(positions, head_dim):
    half = head_dim // 2
    inverse = jnp.exp(jnp.arange(half, dtype=F32) * (-2.0 * math.log(10000.0) / head_dim))
    angles = positions.astype(F32)[:, None] * inverse[None, :]
    cosine, sine = jnp.cos(angles), jnp.sin(angles)
    return jnp.concatenate([cosine] * 4, axis=1), jnp.concatenate([-sine, sine, -sine, sine], axis=1)


def norm_scale(vectors):
    return lax.rsqrt(jnp.mean(vectors * vectors, axis=-1, keepdims=True) + EPSILON)


def norm_back(vectors, scaler, gains, grads_in):
    scaled = grads_in * gains
    inner_mean = jnp.mean(scaled * vectors, axis=-1, keepdims=True)
    return scaler * scaled - vectors * (scaler * scaler * scaler) * inner_mean


def backwards(array, axis, width):
    count = array.shape[axis] // width
    pieces = [lax.slice_in_dim(array, i * width, (i + 1) * width, axis=axis) for i in range(count)]
    return jnp.concatenate(pieces[::-1], axis=axis)


def body(
    tokens,
    w_query,
    key_value_weight,
    w_out,
    w_gate,
    w_up,
    w_down,
    attn_gain,
    ffn_gain,
    query_gain,
    key_gain,
    segments,
    positions,
    out_grad,
):
    tok, width = tokens.shape
    rows = lax.axis_size("row")
    row = lax.axis_index("row")
    col = lax.axis_index("col")
    cols = lax.axis_size("col")
    w_rows = w_query.shape[0]
    q_width = w_query.shape[1]
    kv_half = key_value_weight.shape[1] // 2
    ff_cols = w_gate.shape[1]
    ff = ff_cols // MEMBERS
    seq_len = min(SEQ_MAX, tok * rows)
    span = seq_len // tok
    half = tok // 2

    w_packed = pack_call(col, w_query, key_value_weight, w_out)
    head_cols = w_packed.shape[1] - q_width
    w_all = lax.all_gather(w_packed, "row", axis=0, tiled=True)
    w_o_all = w_all[:, head_cols:]
    og_low = lax.dynamic_slice_in_dim(out_grad, col * half, half, 0)
    og_all = gather_cube_slowly(og_low)
    order, near_order = distances(True), distances(False)
    group = og_all.shape[0]

    w_ff = jnp.concatenate(
        [
            w_gate.reshape(w_rows, MEMBERS, ff),
            w_up.reshape(w_rows, MEMBERS, ff),
            w_down.T.reshape(w_rows, MEMBERS, ff),
        ],
        axis=2,
    ).transpose(1, 0, 2)
    w_ff = jnp.concatenate([w_ff] * (rows // MEMBERS), axis=0)

    input_f = tokens.astype(F32)
    act_scale = norm_scale(input_f)
    act_low = (input_f * act_scale * attn_gain).astype(BF16)
    cosine, sine = rope_tables(positions, HALF)
    q_lanes = jnp.tile(query_gain, 2)[None, :]
    k_lanes = jnp.tile(key_gain, 2)[None, :]
    kv_flag = jnp.concatenate([jnp.ones((1, 3 * HALF), F32), jnp.zeros((1, 3 * HALF), F32)], axis=1)
    kv_gain = jnp.where(kv_flag > 0, jnp.tile(k_lanes, (1, 3)), 1.0)
    q_flag = jnp.ones((1, q_width), F32)
    q_gain = jnp.tile(q_lanes * SCALE, (1, q_width // LANES))
    gain = jnp.concatenate([q_gain, kv_gain], axis=1)
    flag = jnp.concatenate([q_flag, kv_flag], axis=1)
    act_low, og_all = lax.optimization_barrier((act_low, og_all))
    raw, heads, kv_low = heads_call(act_low, w_all, gain, flag, cosine, sine, head_cols - q_width)
    same_kv, other_kv, w_ff = gather_earlier(kv_low, span, w_ff)
    w_ff_all = lax.all_to_all(w_ff, "row", split_axis=0, concat_axis=0, tiled=True).reshape(width, 3 * ff)

    in_span = row % span
    seq_segments = lax.dynamic_slice_in_dim(segments, (row - in_span) * tok, seq_len, 0)
    own_segments = lax.dynamic_slice_in_dim(segments, row * tok, tok, 0)
    own_index = in_span * tok + jnp.arange(tok, dtype=jnp.int32)
    index = jnp.arange(seq_len, dtype=jnp.int32)
    start = jnp.min(jnp.where(seq_segments[None, :] == own_segments[:, None], index[None, :], seq_len), axis=1)
    start = jnp.where(own_segments < 0, own_index, start)
    limits = jnp.stack([start, own_index])
    bounds = jnp.stack([2 * (in_span // 4 + 1 - jnp.min(start) // (4 * tok)), in_span])
    attn_low, turned, inv = forward_call(bounds, limits, heads, same_kv, other_kv, q_width)
    attn_part = dot(attn_low, w_o_all, ((1,), (1,))).astype(BF16)

    def mine(array, which):
        return lax.dynamic_slice_in_dim(array, which * half, half, 0)

    arrived = swap_col(mine(attn_part, 1 - col))
    hidden = mine(input_f, col) + (mine(attn_part, col).astype(F32) + arrived.astype(F32))

    ffn_scale = norm_scale(hidden)
    ffn_low = (hidden * ffn_scale * ffn_gain).astype(BF16)
    ffn_same, ffn_other, w_ff_all = gather_cube(ffn_low, w_ff_all)
    ffn_all = jnp.concatenate([ffn_same, ffn_other], axis=0)
    gate_up = dot(ffn_all, w_ff_all[:, : 2 * ff])
    gate_pre, up_pre = gate_up[:, :ff], gate_up[:, ff:]
    d_inner = dot(og_all, w_ff_all[:, 2 * ff :])
    sigma = jax.nn.sigmoid(gate_pre)
    silu_gate = gate_pre * sigma
    inner_low = (silu_gate * up_pre).astype(BF16)
    d_gate = d_inner * up_pre * (sigma * (1.0 + gate_pre * (1.0 - sigma)))
    d_up = d_inner * silu_gate
    d_gate_up = jnp.concatenate([d_gate, d_up], axis=1).astype(BF16)

    w_gate_up = w_ff_all[:, : 2 * ff]
    away = dot(d_gate_up[group // 2 :], w_gate_up, ((1,), (1,))).astype(BF16)
    here = dot(d_gate_up[: group // 2], w_gate_up, ((1,), (1,)))
    total = (here + swap_core(away).astype(F32)).astype(BF16).reshape(2, 2, 2, half, width)

    left, right = total[..., : width // 2], total[..., width // 2 :]
    (left_away, right_away), grads_ff = beside(
        (left[1], right[:, 1]),
        lambda one, two: (swap_cube(one, 1), swap_cube(two, cols)),
        (ffn_all, og_all, d_gate_up, inner_low),
        lambda *arrays: ff_grads_call(*arrays, rows),
    )
    left, right = add_low(left[0], left_away), add_low(right[:, 0], right_away)
    grads_ff = lax.psum_scatter(
        grads_ff, "row", scatter_dimension=0, tiled=True, axis_index_groups=across_groups()
    )

    def down(inner_low):
        w_down_all = w_ff_all[:, 2 * ff :]
        away = dot(inner_low[group // 2 :], w_down_all, ((1,), (1,))).astype(BF16)
        return away, dot(inner_low[: group // 2], w_down_all, ((1,), (1,))).astype(BF16)

    (left_away, right_away), (out_away, out_here) = beside(
        (left[1], right[:, 1]),
        lambda one, two: (swap_cube(one, cols), swap_cube(two, 2 * cols)),
        (inner_low,),
        down,
    )
    left, right = add_low(left[0], left_away), add_low(right[:, 0], right_away)
    ffn_out = over_core(out_here, out_away).reshape(2, 2, 2, half, width)
    left = halve(left, 0, 2 * cols)
    right = halve(right, 0, 1)
    ffn_back = jnp.concatenate([left, right], axis=1)
    ffn_gain_part = jnp.sum(ffn_back * hidden * ffn_scale, axis=0)
    d_hidden = og_low.astype(F32) + norm_back(hidden, ffn_scale, ffn_gain, ffn_back)
    d_hidden_half = d_hidden.astype(BF16)
    d_hidden_low = halves(d_hidden_half, swap_col(d_hidden_half), col)

    d_attn = dot(d_hidden_low, w_o_all).astype(BF16)
    d_q, q_gain_part, same_d, other_d = backward_call(
        bounds, limits, heads, d_attn, turned, inv, same_kv, other_kv, raw, q_lanes, cosine, sine
    )
    d_kv_total = over_core(same_d, other_d).reshape(-1, tok, same_d.shape[3])

    ffn_out = halve(after(ffn_out, d_hidden_low), 0, 1)

    count = d_kv_total.shape[0] // 2
    (kv_away,), (grad_o, grad_q) = beside(
        (d_kv_total[count:],),
        lambda block: (swap_near(block),),
        (d_hidden_low, act_low, d_q),
        lambda hid, act, grad: (
            over_core(*rows_call(near_order, hid, attn_low)),
            over_core(*rows_call(near_order, act, grad)),
        ),
    )
    d_kv_total = add_low(d_kv_total[:count], kv_away)
    grad_o = over_near(grad_o)
    grad_q = over_near(after(grad_q, d_kv_total))
    kv_parts = over_far(d_kv_total, span, False, False)
    *kv_parts, ffn_out = lax.optimization_barrier((*kv_parts, ffn_out))
    grad_oq = jnp.concatenate([grad_o, grad_q], axis=2)
    grad_oq = lax.psum_scatter(
        grad_oq, "row", scatter_dimension=0, tiled=True, axis_index_groups=far_groups()
    )
    d_kv, k_gain_part = kv_back_call(kv_parts, raw, kv_gain, kv_flag, cosine, sine)
    d_one = jnp.concatenate([d_q, d_kv], axis=1)

    per_row = HALF // rows
    fold = lambda part: (part[0, :HALF] + part[0, HALF:]).reshape(rows, 1, per_row)
    line = lambda values: jnp.pad(values, ((0, 0), (0, 0), (0, d_kv.shape[1] - values.shape[2])))
    small = [
        line(jnp.concatenate([fold(q_gain_part), fold(k_gain_part)], axis=2)),
        line(ffn_gain_part.reshape(rows, 1, w_rows)),
        jnp.zeros((rows, 14, d_kv.shape[1]), F32),
    ]
    small = jnp.concatenate(small, axis=1).astype(BF16)
    kv_partial = over_core(*rows_call(order, act_low, d_kv, small))
    d_one = after(d_one, kv_partial)
    kv_partial = over_near(kv_partial)
    grads_ff = exchange_group(after(grads_ff, kv_partial))
    ffn_out = halve(after(ffn_out, kv_partial), 0, cols)
    grad_kv, grads_ff, ffn_out = lax.optimization_barrier(
        (over_far(kv_partial, rows, True, True), grads_ff, halve(ffn_out, 0, 2 * cols))
    )
    grad_oq = after(grad_oq, grads_ff)[0].astype(F32)
    grad_o, grad_q = grad_oq[:, :q_width].T, grad_oq[:, q_width:]
    out_half = (hidden + ffn_out).astype(BF16)
    output = halves(out_half, swap_col(out_half), col)
    grad_kv = add_up(grad_kv)
    act_back = dot(d_one, w_all[:, :head_cols], ((1,), (1,))).astype(BF16)
    act_back = act_back.astype(F32) + swap_col(act_back).astype(F32)
    input_grad = d_hidden_low.astype(F32) + norm_back(input_f, act_scale, attn_gain, act_back)
    grad_kv, small = grad_kv[:w_rows], grad_kv[w_rows : w_rows + 2]
    grad_query = jnp.where(col == 0, grad_q, backwards(grad_q, 1, LANES))
    grad_out = jnp.where(col == 0, grad_o, backwards(grad_o, 0, LANES))

    kv_own = grad_kv.astype(BF16)
    kv_away = swap_col(kv_own)
    kv_first = jnp.where(col == 0, kv_own, kv_away).astype(F32)
    kv_last = jnp.where(col == 0, kv_away, kv_own).astype(F32)

    def one_head(array, at):
        return array[:, at : at + HALF]

    pieces = []
    for at in (K_AT, V_AT):
        pieces += [one_head(kv_first, at[0]), one_head(kv_first, at[1])]
        pieces += [one_head(kv_first, at[2]) + one_head(kv_last, at[2])]
        pieces += [one_head(kv_last, at[1]), one_head(kv_last, at[0])]
    grad_keyval = jnp.concatenate(pieces, axis=1)

    grad_gate, grad_up, grad_down = ff_format_call(grads_ff)

    attn_part_gain = jnp.sum(
        jnp.concatenate([grad_q, grad_kv], axis=1) * w_packed[:, :head_cols].astype(F32), axis=1
    )
    gains = jnp.concatenate([attn_part_gain, small[1, :w_rows], small[0, : 2 * per_row]])
    gains = gains + swap_col(gains)
    own_gains = lambda whole: lax.dynamic_slice_in_dim(whole, row * w_rows, w_rows, 0)
    grad_attn_gain = gains[:w_rows] / own_gains(attn_gain)
    grad_ffn_gain = gains[w_rows : 2 * w_rows]
    grad_query_gain = gains[2 * w_rows : 2 * w_rows + per_row]
    grad_key_gain = gains[2 * w_rows + per_row :]
    return (
        output,
        input_grad,
        grad_query,
        grad_keyval,
        grad_out,
        grad_gate,
        grad_up,
        grad_down,
        grad_attn_gain,
        grad_ffn_gain,
        grad_query_gain,
        grad_key_gain,
    )


def solution(mesh):
    placed = (
        P("row", None),
        P("row", "col"),
        P("row", None),
        P("col", "row"),
        P("row", "col"),
        P("row", "col"),
        P("col", "row"),
        P(),
        P(),
        P(),
        P(),
        P(),
        P("row"),
        P("row", None),
    )
    return jax.shard_map(
        body,
        mesh=mesh,
        in_specs=placed,
        out_specs=(
            P("row", None),
            P("row", None),
            P("row", "col"),
            P("row", None),
            P("col", "row"),
            P("row", "col"),
            P("row", "col"),
            P("col", "row"),
            P("row"),
            P("row"),
            P("row"),
            P("row"),
        ),
        check_vma=False,
    )
```
